32 devices in a mesh: dp: 8 (over z, x), row: 2 (over core), col: 2 (over y).
Axes of the slice: x: 2, y: 2, z: 4, core: 2. Of those that a mesh axis runs over, the one named last changes fastest.
Arguments:
- tokens: bfloat16 [4096, 1280], P(('dp', 'row', 'col')), may hold values from -6 to 6
- cotangent: bfloat16 [4096, 1280], P(('dp', 'row', 'col')), may hold values from -6 to 6
- seg_ids: int32 [32, 128], P('dp'), may hold values from 0 to 12, as said below
- parents: int32 [32, 13], P('dp'), may hold values from 0 to 4, as said below
- norm1_gain: float32 [1280], P('col'), may hold values from 0.5 to 1.5
- w_query: bfloat16 [1280, 20, 64], P('col', 'row', 'dp'), may hold values from -0.15625 to 0.15625
- key_value_weight: bfloat16 [1280, 2, 320], P('col', 'row', 'dp'), may hold values from -0.15625 to 0.15625
- w_out: bfloat16 [20, 64, 1280], P('row', 'dp', 'col'), may hold values from -0.625 to 0.625
- norm2_gain: float32 [1280], P('col'), may hold values from 0.5 to 1.5
- w_gate: bfloat16 [1280, 3584], P('col', ('dp', 'row')), may hold values from -0.15625 to 0.15625
- w_up: bfloat16 [1280, 3584], P('col', ('dp', 'row')), may hold values from -0.15625 to 0.15625
- w_down: bfloat16 [3584, 1280], P(('dp', 'row'), 'col'), may hold values from -0.09375 to 0.09375
Outputs:
- layer_out: bfloat16 [4096, 1280], P(('dp', 'row', 'col'))
- in_grad: bfloat16 [4096, 1280], P(('dp', 'row', 'col'))
- norm1_grad: float32 [1280], P('col')
- query_grad: float32 [1280, 20, 64], P('col', 'row', 'dp')
- keyval_grad: float32 [1280, 2, 320], P('col', 'row', 'dp')
- out_grad: float32 [20, 64, 1280], P('row', 'dp', 'col')
- norm2_grad: float32 [1280], P('col')
- gate_grad: float32 [1280, 3584], P('col', ('dp', 'row'))
- up_grad: float32 [1280, 3584], P('col', ('dp', 'row'))
- down_grad: float32 [3584, 1280], P(('dp', 'row'), 'col')
The draws below stay inside these ranges and needn't reach their ends.
Inputs may be any that keep to these rules, and one draw needn't show every extreme that they name: `seg_ids`: along each tree the segment number never falls, the first 42 tokens are segment 0, and each of the 13 segments holds at least one token. `parents`: entry s of a tree is the parent of segment s: 0 for segments 0 to 4; segments 5 to 12 each have one of segments 1 to 4 as parent, and each of segments 1 to 4 is the parent of exactly two of them.
All inputs are finite; a program needn't handle non-finite values.
Results may differ from the reference program's by a relative error of at most 0.018.
Values may be sent and summed in bfloat16 or wider, within the bound.
A program may use at most 128 MiB of HBM per device.

```python
import math
import jax
import jax.numpy as jnp
from jax import lax

MODEL_WIDTH = 1280
QUERY_HEADS = 20
KEY_VALUE_HEADS = 5
HEAD_SIZE = 64
FF = 3584
TREE_TOKENS = 128
SEGS = 13
TRUNK = 42
TREES = 32
TOKENS = 4096


def draw_seg_ids(key, part):
    key = jax.random.fold_in(key, 11)
    key_rows = jax.random.split(key, TREES)

    def one_tree(tree_key):
        spots = jax.random.permutation(tree_key, TREE_TOKENS - TRUNK - 1)[:SEGS - 2] + TRUNK + 1
        places = jnp.arange(TREE_TOKENS, dtype=jnp.int32)
        cuts = jnp.sum((places[:, None] >= spots[None, :]).astype(jnp.int32), axis=1)
        return (places >= TRUNK).astype(jnp.int32) + cuts
    return jax.vmap(one_tree)(key_rows).astype(jnp.int32)


def draw_parents(key, part):
    key = jax.random.fold_in(key, 23)
    key_rows = jax.random.split(key, TREES)
    branch_list = jnp.array([1, 1, 2, 2, 3, 3, 4, 4], dtype=jnp.int32)

    def one_tree(tree_key):
        leaves = jax.random.permutation(tree_key, branch_list)
        return jnp.concatenate([jnp.zeros((5,), jnp.int32), leaves])
    return jax.vmap(one_tree)(key_rows).astype(jnp.int32)


def block_scale(own_key, extent, shards, least, top_value):
    def one(dim, blocks):
        heights = jax.random.uniform(jax.random.fold_in(jax.random.fold_in(own_key, 6), dim), (blocks,), jnp.float32, least / len(shards), top_value / len(shards))
        return jnp.repeat(jnp.exp(heights), extent[dim] // blocks).reshape((-1,) + (1,) * (len(extent) - dim - 1))

    level = one(*shards[0])
    for cut in shards[1:]:
        level = level * one(*cut)
    return level


def bell_draw(own_key, dims, scale, limit, shards=(), kind=jnp.bfloat16):
    drawn = jax.random.normal(own_key, dims, jnp.float32) * scale
    if len(shards) > 0:
        drawn = block_scale(own_key, dims, shards, -0.22, 0.18) * drawn
    return jnp.clip(drawn, min=-limit, max=limit).astype(kind)


def setup_inputs(seed: int = 0) -> dict:
    seeds = jax.random.split(jax.random.key(seed), 13)
    return {
        "tokens": bell_draw(seeds[0], (TOKENS, MODEL_WIDTH), 1.0, 6.0, ((0, 32),)),
        "cotangent": bell_draw(seeds[1], (TOKENS, MODEL_WIDTH), 1.0, 6.0, ((0, 32),)),
        "seg_ids": draw_seg_ids(jax.random.fold_in(seeds[12], 71), 0),
        "parents": draw_parents(jax.random.fold_in(seeds[12], 71), 0),
        "norm1_gain": jnp.clip(1.0 + 0.1 * jax.random.normal(seeds[4], (MODEL_WIDTH,), jnp.float32), 0.5, 1.5),
        "w_query": bell_draw(seeds[5], (MODEL_WIDTH, QUERY_HEADS, HEAD_SIZE), MODEL_WIDTH ** -0.5, 0.15625, ((0, 2), (1, 2), (2, 8))),
        "key_value_weight": bell_draw(seeds[6], (MODEL_WIDTH, 2, KEY_VALUE_HEADS * HEAD_SIZE), MODEL_WIDTH ** -0.5, 0.15625, ((0, 2), (1, 2), (2, 8))),
        "w_out": bell_draw(seeds[7], (QUERY_HEADS, HEAD_SIZE, MODEL_WIDTH), (QUERY_HEADS * HEAD_SIZE * 8 // TREE_TOKENS) ** -0.5, 0.625, ((0, 2), (1, 8), (2, 2))),
        "norm2_gain": jnp.clip(1.0 + 0.1 * jax.random.normal(seeds[8], (MODEL_WIDTH,), jnp.float32), 0.5, 1.5),
        "w_gate": bell_draw(seeds[9], (MODEL_WIDTH, FF), MODEL_WIDTH ** -0.5, 0.15625, ((0, 2), (1, 16))),
        "w_up": bell_draw(seeds[10], (MODEL_WIDTH, FF), MODEL_WIDTH ** -0.5, 0.15625, ((0, 2), (1, 16))),
        "w_down": bell_draw(seeds[11], (FF, MODEL_WIDTH), FF ** -0.5, 0.09375, ((0, 16), (1, 2))),
    }


EPS = 1e-05
THETA = 10000.0
HIGH = lax.Precision.HIGHEST

@jax.custom_vjp
def lower_part(v):
    return lax.optimization_barrier(v.astype(jnp.bfloat16)).astype(jnp.float32)

@jax.custom_vjp
def low_back(v):
    return v

def low_keep(v):
    return (lower_part(v), None)

def low_pass(kept, grad):
    return (grad,)

def back_keep(v):
    return (v, None)

def back_low(kept, grad):
    return (lower_part(grad),)
lower_part.defvjp(low_keep, low_pass)
low_back.defvjp(back_keep, back_low)

def tree_layout(segment, parent):
    labels = jnp.arange(SEGS, dtype=jnp.int32)
    member = (segment[:, None] == labels[None, :]).astype(jnp.float32)
    link = ((parent[:, None] == labels[None, :]) & (labels[:, None] > 0)).astype(jnp.float32)
    ident = jnp.eye(SEGS, dtype=jnp.float32)

    def climb(level, reach):
        return ident + jnp.dot(link, reach, precision=HIGH)
    reach = lax.fori_loop(0, SEGS, climb, ident)
    visible = jnp.dot(jnp.dot(member, reach, precision=HIGH), member.T, precision=HIGH) > 0.5
    places = jnp.arange(segment.shape[0], dtype=jnp.int32)
    allowed = visible & (places[:, None] >= places[None, :])
    sizes = lax.optimization_barrier(jnp.sum(member, axis=0))
    earlier = (labels[None, :] < labels[:, None]).astype(jnp.float32)
    starts = jnp.dot(earlier, sizes, precision=HIGH)
    above = jnp.dot(reach, sizes, precision=HIGH) - sizes
    tree_depth = places.astype(jnp.float32) + jnp.dot(member, above - starts, precision=HIGH)
    return (allowed, tree_depth)

def rotate(value_rows, tree_depth, sign):
    half = value_rows.shape[-1] // 2
    freqs = jnp.arange(half, dtype=jnp.float32) * (2.0 / value_rows.shape[-1])
    inverse = jnp.exp(freqs * -math.log(THETA))
    angle = tree_depth[:, None] * inverse[None, :]
    cosine = jnp.cos(angle)[:, None, :]
    sine = sign * jnp.sin(angle)[:, None, :]
    first = value_rows[..., :half]
    second = value_rows[..., half:]
    return jnp.concatenate([first * cosine - second * sine, second * cosine + first * sine], axis=-1)

def attend_tree(pieces):
    query, key_rows, value_rows, allowed = pieces
    group = query.shape[1] // key_rows.shape[1]
    keys_all = jnp.repeat(key_rows, group, axis=1)
    values_all = jnp.repeat(value_rows, group, axis=1)
    scale = query.shape[2] ** (-0.5)
    scores = low_back(jnp.einsum('qhd,khd->hqk', query, keys_all, precision=HIGH) * scale)
    masked = jnp.where(allowed[None], scores, -1e+30)
    row_max = lax.optimization_barrier(jnp.max(masked, axis=-1, keepdims=True))
    total = jnp.log(lax.optimization_barrier(jnp.sum(jnp.exp(masked - row_max), axis=-1, keepdims=True))) + row_max
    probs = lower_part(jnp.exp(masked - total))
    return jnp.einsum('hqk,khd->qhd', probs, values_all, precision=HIGH)

def rms_scale(value_rows):
    return lax.rsqrt(lax.optimization_barrier(jnp.mean(value_rows * value_rows, axis=-1, keepdims=True)) + EPS)

def layer(stream, gain1, w_query, key_value_weight, w_out, gain2, w_gate, w_up, w_down, allowed, tree_depth):
    tree_batch = allowed.shape[0]
    count = stream.shape[0]
    normed = lower_part(stream * rms_scale(stream) * gain1)
    query_pre = low_back(jnp.dot(normed, w_query.reshape(MODEL_WIDTH, QUERY_HEADS * HEAD_SIZE), precision=HIGH))
    key_unrotated = low_back(jnp.dot(normed, key_value_weight[:, 0, :], precision=HIGH))
    value_unrotated = low_back(jnp.dot(normed, key_value_weight[:, 1, :], precision=HIGH))
    turn_angle = jax.vmap(rotate, (0, 0, None))
    query = lower_part(turn_angle(query_pre.reshape(tree_batch, TREE_TOKENS, QUERY_HEADS, HEAD_SIZE), tree_depth, 1.0))
    key_rows = lower_part(turn_angle(key_unrotated.reshape(tree_batch, TREE_TOKENS, KEY_VALUE_HEADS, HEAD_SIZE), tree_depth, 1.0))
    value_rows = lower_part(value_unrotated.reshape(tree_batch, TREE_TOKENS, KEY_VALUE_HEADS, HEAD_SIZE))
    mixed = lax.map(jax.checkpoint(attend_tree), (query, key_rows, value_rows, allowed))
    mixed = lower_part(low_back(mixed.reshape(count, QUERY_HEADS * HEAD_SIZE)))
    attn = low_back(jnp.dot(mixed, w_out.reshape(QUERY_HEADS * HEAD_SIZE, MODEL_WIDTH), precision=HIGH))
    resid = stream + attn
    normed2 = lower_part(resid * rms_scale(resid) * gain2)
    gate = low_back(jnp.dot(normed2, w_gate, precision=HIGH))
    up_part = low_back(jnp.dot(normed2, w_up, precision=HIGH))
    hidden = lower_part(jax.nn.silu(gate) * up_part)
    return resid + low_back(jnp.dot(hidden, w_down, precision=HIGH))

def reference(tokens, cotangent, seg_ids, parents, norm1_gain, w_query, key_value_weight, w_out, norm2_gain, w_gate, w_up, w_down):
    allowed, tree_depth = jax.vmap(tree_layout)(seg_ids, parents)
    params = tuple((p.astype(jnp.float32) for p in (norm1_gain, w_query, key_value_weight, w_out, norm2_gain, w_gate, w_up, w_down)))
    group_trees = 4
    groups = TREES // group_trees
    stream_all = tokens.astype(jnp.float32).reshape(groups, group_trees * TREE_TOKENS, MODEL_WIDTH)
    cot_all = cotangent.astype(jnp.float32).reshape(groups, group_trees * TREE_TOKENS, MODEL_WIDTH)
    allowed_all = allowed.reshape(groups, group_trees, TREE_TOKENS, TREE_TOKENS)
    depth_all = tree_depth.reshape(groups, group_trees, TREE_TOKENS)
    zero_block = tuple((jnp.zeros_like(p) for p in params))

    def one_group(sums, pieces):
        stream, cot, allow, places = pieces

        def forward(stream_in, *weights):
            return layer(stream_in, *weights, allow, places)
        result, pullback = jax.vjp(forward, stream, *params)
        grads = pullback(cot)
        sums = tuple((a + b for a, b in zip(sums, grads[1:])))
        return (sums, (result.astype(jnp.bfloat16), grads[0].astype(jnp.bfloat16)))
    sums, (results, input_grads) = lax.scan(one_group, zero_block, (stream_all, cot_all, allowed_all, depth_all))
    return (results.reshape(TOKENS, MODEL_WIDTH), input_grads.reshape(TOKENS, MODEL_WIDTH), sums[0], sums[1], sums[2], sums[3], sums[4], sums[5], sums[6], sums[7])
```

```python
import functools
import math

import jax
import jax.numpy as jnp
from jax import lax
from jax.experimental import pallas as pl
from jax.experimental.pallas import tpu as pltpu
from jax.sharding import PartitionSpec as P

MODEL_WIDTH = 1280
QUERY_HEADS = 20
KEY_VALUE_HEADS = 5
HEAD_SIZE = 64
TREE_TOKENS = 128
SEGS = 13
PLANES = 4

EPS = 1e-05
THETA = 10000.0
MESH = pl.DeviceIdType.MESH
F32 = jnp.float32
BF16 = jnp.bfloat16


class Layout:
    def __init__(self, shape):
        self.planes = PLANES
        self.lines = shape["dp"] // PLANES
        self.cores = shape["row"]
        self.cols = shape["col"]
        self.dp = shape["dp"]
        self.width = MODEL_WIDTH // self.cols
        self.qrows = QUERY_HEADS // self.cores * (HEAD_SIZE // self.dp)
        self.kvrows = KEY_VALUE_HEADS * HEAD_SIZE // self.dp
        self.kv_at = self.qrows
        self.out_at = -(-(self.kv_at + self.kvrows) // 16) * 16
        self.arows = -(-(self.out_at + self.qrows) // 16) * 16

    def fits(self):
        return self.width % 128 == 0 and self.qrows % 16 == 0 and self.cores == 2 and self.dp % PLANES == 0

    def here(self):
        dp = lax.axis_index("dp")
        return dp // self.lines, lax.rem(dp, self.lines), lax.axis_index("row"), lax.axis_index("col")

    def device(self, z, x, r, c):
        return (z * self.lines + x, r, c)

    def plane_offsets(self):
        return [(dx, dc) for dx in range(self.lines) for dc in range(self.cols) if dx or dc]


def greet(lay, peers):
    barrier = pltpu.get_barrier_semaphore()
    for peer in peers:
        pl.semaphore_signal(barrier, inc=1, device_id=peer, device_id_type=MESH)
    pl.semaphore_wait(barrier, len(peers))


def neighbours(lay):
    z, x, r, c = lay.here()
    peers = [lay.device(lax.rem(z + k, lay.planes), x, r, c) for k in range(1, lay.planes)]
    for dx, dc in lay.plane_offsets():
        peers.append(lay.device(z, lax.rem(x + dx, lay.lines), r, lax.rem(c + dc, lay.cols)))
    peers.append(lay.device(z, x, 1 - r, c))
    return peers


def send(src, dst, sems, slot, peer):
    copy = pltpu.make_async_remote_copy(
        src_ref=src,
        dst_ref=dst,
        send_sem=sems[0].at[slot],
        recv_sem=sems[1].at[slot],
        device_id=peer,
        device_id_type=MESH,
    )
    copy.start()
    return copy


def gather_kernel(lay, a_ref, f_ref, dy_ref, ga, gf, gdy, own, az_s, az_r, ap_s, ap_r, ac_s, ac_r, fp_s, fp_r, fc_s, fc_r, dz_s, dz_r):
    z, x, r, c = lay.here()
    W = lay.width
    n_off = len(lay.plane_offsets())
    greet(lay, neighbours(lay))
    span = pl.ds(pl.multiple_of(c * W, 128), W)
    frows = f_ref.shape[1]

    def a_at(zz):
        return ga.at[zz * lay.lines + x, r, :, span]

    def f_at(xx):
        return gf.at[:, pl.ds(pl.multiple_of((xx * lay.cores + r) * frows, 16), frows), :]

    f_own = gf.at[:, pl.ds(pl.multiple_of((x * lay.cores + r) * frows, 16), frows), span]
    locals_ = [
        pltpu.make_async_copy(a_ref, a_at(z), own.at[0]),
        pltpu.make_async_copy(f_ref, f_own, own.at[1]),
        pltpu.make_async_copy(dy_ref, gdy.at[0], own.at[2]),
    ]
    for copy in locals_:
        copy.start()
    az = []
    for k in range(1, lay.planes):
        peer = lay.device(lax.rem(z + k, lay.planes), x, r, c)
        az.append(send(a_ref, a_at(z), (az_s, az_r), k - 1, peer))
    ap = {}
    for k in range(lay.planes):
        zz = lax.rem(z + lay.planes - k, lay.planes)
        if k:
            az[k - 1].wait_recv()
        for j, (dx, dc) in enumerate(lay.plane_offsets()):
            peer = lay.device(z, lax.rem(x + dx, lay.lines), r, lax.rem(c + dc, lay.cols))
            src = a_ref if k == 0 else a_at(zz)
            ap[k, j] = send(src, a_at(zz), (ap_s, ap_r), k * n_off + j, peer)
        if k == 0:
            fp = []
            for j, (dx, dc) in enumerate(lay.plane_offsets()):
                peer = lay.device(z, lax.rem(x + dx, lay.lines), r, lax.rem(c + dc, lay.cols))
                fp.append(send(f_ref, f_own, (fp_s, fp_r), j, peer))
            dz = []
            for q in range(1, lay.planes):
                peer = lay.device(lax.rem(z + q, lay.planes), x, r, c)
                dz.append(send(dy_ref, gdy.at[q], (dz_s, dz_r), q - 1, peer))
    for copy in locals_:
        copy.wait()
    sibling = lay.device(z, x, 1 - r, c)
    last = []
    for k in range(lay.planes):
        zz = lax.rem(z + lay.planes - k, lay.planes)
        for j in range(n_off):
            ap[k, j].wait_recv()
        for dx in range(lay.lines):
            block = ga.at[zz * lay.lines + lax.rem(x + dx, lay.lines), r]
            last.append(send(block, block, (ac_s, ac_r), k * lay.lines + dx, sibling))
    for j in range(n_off):
        fp[j].wait_recv()
    for dx in range(lay.lines):
        block = f_at(lax.rem(x + dx, lay.lines))
        last.append(send(block, block, (fc_s, fc_r), dx, sibling))
    for copy in last:
        copy.wait()
    for copy in dz:
        copy.wait()
    for copy in az + fp + list(ap.values()):
        copy.wait_send()


def gather_weights(lay, a_shard, f_shard, dy):
    n_off = len(lay.plane_offsets())
    dma = lambda n: pltpu.SemaphoreType.DMA((n,))
    np_, nx = lay.planes, lay.lines
    counts = [np_ - 1, np_ * n_off, np_ * nx, n_off, nx, np_ - 1]
    scratch = [dma(3)]
    for n in counts:
        scratch += [dma(n), dma(n)]
    frows = f_shard.shape[1]
    hbm = pl.BlockSpec(memory_space=pl.ANY)
    return pl.pallas_call(
        functools.partial(gather_kernel, lay),
        out_shape=(
            jax.ShapeDtypeStruct((lay.dp, lay.cores, lay.arows, MODEL_WIDTH), BF16),
            jax.ShapeDtypeStruct((3, nx * lay.cores * frows, MODEL_WIDTH), BF16),
            jax.ShapeDtypeStruct((np_,) + dy.shape, BF16),
        ),
        in_specs=[hbm] * 3,
        out_specs=(hbm,) * 3,
        scratch_shapes=scratch,
        compiler_params=pltpu.CompilerParams(collective_id=0, has_side_effects=True),
        name="gather_weights",
    )(a_shard, f_shard, dy)


def tokens_kernel(lay, n_ref, gn, own, s_s, s_r):
    z, x, r, c = lay.here()
    greet(lay, [lay.device(lax.rem(z + k, lay.planes), x, r, c) for k in range(1, lay.planes)])
    copies = []
    for k in range(1, lay.planes):
        peer = lay.device(lax.rem(z + k, lay.planes), x, r, c)
        copies.append(send(n_ref, gn.at[k], (s_s, s_r), k - 1, peer))
    mine = pltpu.make_async_copy(n_ref, gn.at[0], own.at[0])
    mine.start()
    mine.wait()
    for copy in copies:
        copy.wait()


def gather_tokens(lay, rows):
    hbm = pl.BlockSpec(memory_space=pl.ANY)
    dma = lambda n: pltpu.SemaphoreType.DMA((n,))
    n = lay.planes - 1
    return pl.pallas_call(
        functools.partial(tokens_kernel, lay),
        out_shape=jax.ShapeDtypeStruct((lay.planes,) + rows.shape, BF16),
        in_specs=[hbm],
        out_specs=hbm,
        scratch_shapes=[dma(1), dma(n), dma(n)],
        compiler_params=pltpu.CompilerParams(collective_id=1, has_side_effects=True),
        name="gather_tokens",
    )(rows)


def add_rows(total, step, left, right, dest):
    def some(i, _):
        rows = pl.ds(pl.multiple_of(i * step, step), step)
        dest[rows, :] = (left[rows, :].astype(F32) + right[rows, :].astype(F32)).astype(dest.dtype)
        return 0

    lax.fori_loop(0, total // step, some, 0)


def sum_rows(total, step, parts, dest):
    def some(i, _):
        rows = pl.ds(pl.multiple_of(i * step, step), step)
        acc = parts[0][rows, :].astype(F32)
        for part in parts[1:]:
            acc = acc + part[rows, :].astype(F32)
        dest[rows, :] = acc.astype(dest.dtype)
        return 0

    lax.fori_loop(0, total // step, some, 0)


def feed_grads_kernel(lay, g_ref, d_ref, out_ref, do_ref, core_in, mixed, plane_in, d_in, cs, cr, ps, pr, zs, zr):
    z, x, r, c = lay.here()
    W = lay.width
    offs = lay.plane_offsets()
    frows = out_ref.shape[1]
    greet(lay, neighbours(lay))
    sibling = lay.device(z, x, 1 - r, c)

    def rows_of(xx, rr):
        return pl.ds(pl.multiple_of((xx * lay.cores + rr) * frows, 16), frows)

    def lanes(cc):
        return pl.ds(pl.multiple_of(cc * W, 128), W)

    core = []
    order = [(dx + 1) % lay.lines for dx in range(lay.lines)]
    for i, dx in enumerate(order):
        xx = lax.rem(x + dx, lay.lines)
        core.append(send(g_ref.at[:, rows_of(xx, 1 - r), :], core_in.at[i], (cs, cr), i, sibling))
    dz = []
    for k in range(1, lay.planes):
        peer = lay.device(lax.rem(z + lay.planes - k, lay.planes), x, r, c)
        dz.append(send(d_ref.at[k], d_in.at[k - 1], (zs, zr), k - 1, peer))
    plane = {}
    for i, dx in enumerate(order):
        xx = lax.rem(x + dx, lay.lines)
        core[i].wait_recv()
        for w in range(3):
            add_rows(frows, 32, g_ref.at[w, rows_of(xx, r), :], core_in.at[i, w], mixed.at[i, w])
        for dc in range(lay.cols):
            if dx or dc:
                cc = lax.rem(c + dc, lay.cols)
                j = offs.index((dx, dc))
                peer = lay.device(z, xx, r, cc)
                plane[j] = send(mixed.at[i, :, :, lanes(cc)], plane_in.at[j], (ps, pr), j, peer)
    for copy in dz:
        copy.wait_recv()
    sum_rows(d_ref.shape[1], 16, [d_ref.at[0]] + [d_in.at[k] for k in range(lay.planes - 1)], do_ref)
    for j in range(len(offs)):
        plane[j].wait_recv()
    mine = order.index(0)
    for w in range(3):
        sum_rows(frows, 32, [mixed.at[mine, w, :, lanes(c)]] + [plane_in.at[j, w] for j in range(len(offs))], out_ref.at[w])
    for copy in core + dz + list(plane.values()):
        copy.wait_send()


def reduce_feed(lay, grads, d_rows):
    frows = grads.shape[1] // (lay.lines * lay.cores)
    n_off = len(lay.plane_offsets())
    dma = lambda n: pltpu.SemaphoreType.DMA((n,))
    vmem = pl.BlockSpec(memory_space=pltpu.VMEM)
    sems = []
    for n in (lay.lines, n_off, lay.planes - 1):
        sems += [dma(n), dma(n)]
    return pl.pallas_call(
        functools.partial(feed_grads_kernel, lay),
        out_shape=(
            jax.ShapeDtypeStruct((3, frows, lay.width), F32),
            jax.ShapeDtypeStruct(d_rows.shape[1:], F32),
        ),
        in_specs=[vmem] * 2,
        out_specs=(vmem,) * 2,
        scratch_shapes=[
            pltpu.VMEM((lay.lines, 3, frows, MODEL_WIDTH), BF16),
            pltpu.VMEM((lay.lines, 3, frows, MODEL_WIDTH), BF16),
            pltpu.VMEM((n_off, 3, frows, lay.width), BF16),
            pltpu.VMEM((lay.planes - 1,) + d_rows.shape[1:], BF16),
        ]
        + sems,
        compiler_params=pltpu.CompilerParams(collective_id=2, has_side_effects=True, vmem_limit_bytes=56 * 2**20),
        name="reduce_feed",
    )(grads, d_rows)


def attn_grads_kernel(lay, g_ref, d_ref, n_ref, out_ref, do_ref, gain_ref, core_in, mixed, plane_in, line, z_in, d_in, nbuf, nin, cs, cr, ps, pr, zs, zr, ds_, dr, gs, gr):
    z, x, r, c = lay.here()
    W = lay.width
    offs = lay.plane_offsets()
    n_off = len(offs)
    greet(lay, neighbours(lay))
    sibling = lay.device(z, x, 1 - r, c)

    def lanes(cc):
        return pl.ds(pl.multiple_of(cc * W, 128), W)

    core = {}
    for k in list(range(1, lay.planes)) + [0]:
        zz = lax.rem(z + k, lay.planes)
        for dx in range(lay.lines):
            i = k * lay.lines + dx
            block = g_ref.at[zz * lay.lines + lax.rem(x + dx, lay.lines), 1 - r]
            core[i] = send(block, core_in.at[i], (cs, cr), i, sibling)
    gain_core = send(n_ref, nin.at[0], (gs, gr), 0, sibling)
    dz = []
    for k in range(1, lay.planes):
        peer = lay.device(lax.rem(z + lay.planes - k, lay.planes), x, r, c)
        dz.append(send(d_ref.at[k], d_in.at[k - 1], (ds_, dr), k - 1, peer))
    plane = {}
    for k in list(range(1, lay.planes)) + [0]:
        zz = lax.rem(z + k, lay.planes)
        for dx in range(lay.lines):
            i = k * lay.lines + dx
            xx = lax.rem(x + dx, lay.lines)
            core[i].wait_recv()
            add_rows(lay.arows, 16, g_ref.at[zz * lay.lines + xx, r], core_in.at[i], mixed.at[i])
            for dc in range(lay.cols):
                if dx or dc:
                    cc = lax.rem(c + dc, lay.cols)
                    j = offs.index((dx, dc))
                    plane[k, j] = send(mixed.at[i, :, lanes(cc)], plane_in.at[k * n_off + j], (ps, pr), k * n_off + j, lay.device(z, xx, r, cc))
    gain_core.wait_recv()
    nbuf[0] = n_ref[...] + nin[0]
    gains = []
    for j, (dx, dc) in enumerate(offs):
        peer = lay.device(z, lax.rem(x + dx, lay.lines), r, lax.rem(c + dc, lay.cols))
        gains.append(send(nbuf.at[0], nin.at[1 + j], (gs, gr), 1 + j, peer))
    zsend = []
    for k in list(range(1, lay.planes)) + [0]:
        for j in range(n_off):
            plane[k, j].wait_recv()
        parts = [mixed.at[k * lay.lines, :, lanes(c)]] + [plane_in.at[k * n_off + j] for j in range(n_off)]
        sum_rows(lay.arows, 16, parts, line.at[k])
        if k:
            peer = lay.device(lax.rem(z + k, lay.planes), x, r, c)
            zsend.append(send(line.at[k], z_in.at[k - 1], (zs, zr), k - 1, peer))
    for copy in gains:
        copy.wait_recv()
    total = nbuf[0]
    for j in range(n_off):
        total = total + nin[1 + j]
    nbuf[1] = total
    zgains = []
    for k in range(1, lay.planes):
        peer = lay.device(lax.rem(z + k, lay.planes), x, r, c)
        zgains.append(send(nbuf.at[1], nin.at[n_off + k], (gs, gr), n_off + k, peer))
    for copy in dz:
        copy.wait_recv()
    sum_rows(d_ref.shape[1], 16, [d_ref.at[0]] + [d_in.at[k] for k in range(lay.planes - 1)], do_ref)
    for copy in zgains:
        copy.wait_recv()
    total = nbuf[1]
    for k in range(1, lay.planes):
        total = total + nin[n_off + k]
    gain_ref[...] = total
    for copy in zsend:
        copy.wait_recv()
    sum_rows(lay.arows, 16, [line.at[0]] + [z_in.at[k] for k in range(lay.planes - 1)], out_ref)
    for copy in list(core.values()) + dz + list(plane.values()) + zsend + gains + zgains + [gain_core]:
        copy.wait_send()


def reduce_attn(lay, grads, d_rows, gains):
    n_off = len(lay.plane_offsets())
    dma = lambda n: pltpu.SemaphoreType.DMA((n,))
    vmem = pl.BlockSpec(memory_space=pltpu.VMEM)
    np_, nx = lay.planes, lay.lines
    sems = []
    for n in (np_ * nx, np_ * n_off, np_ - 1, np_ - 1, n_off + np_):
        sems += [dma(n), dma(n)]
    return pl.pallas_call(
        functools.partial(attn_grads_kernel, lay),
        out_shape=(
            jax.ShapeDtypeStruct((lay.arows, lay.width), F32),
            jax.ShapeDtypeStruct(d_rows.shape[1:], F32),
            jax.ShapeDtypeStruct(gains.shape, F32),
        ),
        in_specs=[vmem] * 3,
        out_specs=(vmem,) * 3,
        scratch_shapes=[
            pltpu.VMEM((np_ * nx, lay.arows, MODEL_WIDTH), BF16),
            pltpu.VMEM((np_ * nx, lay.arows, MODEL_WIDTH), BF16),
            pltpu.VMEM((np_ * n_off, lay.arows, lay.width), BF16),
            pltpu.VMEM((np_, lay.arows, lay.width), BF16),
            pltpu.VMEM((np_ - 1, lay.arows, lay.width), BF16),
            pltpu.VMEM((np_ - 1,) + d_rows.shape[1:], BF16),
            pltpu.VMEM((2,) + gains.shape, F32),
            pltpu.VMEM((n_off + np_,) + gains.shape, F32),
        ]
        + sems,
        compiler_params=pltpu.CompilerParams(collective_id=3, has_side_effects=True, vmem_limit_bytes=56 * 2**20),
        name="reduce_attn",
    )(grads, d_rows, gains)


def dot_nt(left, right):
    return lax.dot_general(left, right, (((1,), (1,)), ((), ())), preferred_element_type=F32)


def dot_tn(left, right):
    return lax.dot_general(left, right, (((0,), (0,)), ((), ())), preferred_element_type=F32)


def dot_nn(left, right):
    return jnp.dot(left, right, preferred_element_type=F32)


def tree_masks(segment, parent):
    labels = jnp.arange(parent.shape[0], dtype=jnp.int32)
    above = jnp.sum(jnp.where(segment[:, None] == labels[None, :], parent[None, :], 0), axis=1)
    places = jnp.arange(segment.shape[0], dtype=jnp.int32)
    seen = (segment[None, :] == segment[:, None]) | (segment[None, :] == above[:, None]) | (segment[None, :] == 0)
    allowed = seen & (places[:, None] >= places[None, :])
    return allowed, jnp.sum(allowed.astype(F32), axis=1) - 1.0


def rotate(rows, cosine, sine):
    half = rows.shape[-1] // 2
    first, second = rows[..., :half], rows[..., half:]
    return jnp.concatenate([first * cosine - second * sine, second * cosine + first * sine], axis=-1)


def body(lay, tokens, cotangent, seg_ids, parents, norm1_gain, w_query, key_value_weight, w_out, norm2_gain, w_gate, w_up, w_down):
    W = lay.width
    T = TREE_TOKENS
    D = HEAD_SIZE
    frows = w_down.shape[0]
    hidden = lay.lines * lay.cores * frows
    scale = D**-0.5
    row, col = lax.axis_index("row"), lax.axis_index("col")
    a_shard = jnp.concatenate(
        [
            jnp.transpose(w_query, (1, 2, 0)).reshape(lay.qrows, W),
            jnp.transpose(key_value_weight[:, 0, :]),
            jnp.zeros((lay.out_at - lay.kv_at - lay.kvrows, W), BF16),
            w_out.reshape(lay.qrows, W),
            jnp.zeros((lay.arows - lay.out_at - lay.qrows, W), BF16),
        ],
        axis=0,
    )
    f_shard = jnp.stack([w_gate.T, w_up.T, w_down], axis=0)
    gains = lax.all_gather(jnp.stack([norm1_gain, norm2_gain]), "col", axis=1, tiled=True)
    gain1, gain2 = gains[0], gains[1]
    ga, gf, gdy = gather_weights(lay, a_shard, f_shard, cotangent)

    def natural(part):
        p = part.reshape(lay.dp, lay.cores, QUERY_HEADS // lay.cores, D // lay.dp, MODEL_WIDTH)
        return jnp.transpose(p, (1, 2, 0, 3, 4)).reshape(QUERY_HEADS * D, MODEL_WIDTH)

    def placed(grad):
        p = grad.reshape(lay.cores, QUERY_HEADS // lay.cores, lay.dp, D // lay.dp, MODEL_WIDTH)
        return jnp.transpose(p, (2, 0, 1, 3, 4)).reshape(lay.dp, lay.cores, lay.qrows, MODEL_WIDTH)

    wq = natural(ga[:, :, : lay.qrows])
    wo = natural(ga[:, :, lay.out_at : lay.out_at + lay.qrows])
    wkv = jnp.transpose(ga[:, :, lay.kv_at : lay.kv_at + lay.kvrows], (1, 0, 2, 3)).reshape(2 * KEY_VALUE_HEADS * D, MODEL_WIDTH)

    tree = row * lay.cols + col
    segment = lax.dynamic_index_in_dim(seg_ids, tree, 0, keepdims=False)
    parent = lax.dynamic_index_in_dim(parents, tree, 0, keepdims=False)
    allowed, depth = tree_masks(segment, parent)
    inverse = jnp.exp(jnp.arange(D // 2, dtype=F32) * (2.0 / D) * -math.log(THETA))
    angle = depth[:, None] * inverse[None, :]
    cosine, sine = jnp.cos(angle)[:, None, :], jnp.sin(angle)[:, None, :]

    stream = tokens.astype(F32)
    rstd1 = lax.rsqrt(jnp.mean(stream * stream, axis=1, keepdims=True) + EPS)
    normed = (stream * rstd1 * gain1).astype(BF16)
    query = rotate(dot_nt(normed, wq).reshape(T, QUERY_HEADS, D), cosine, sine).astype(BF16)
    kv_pre = dot_nt(normed, wkv)
    kvw = KEY_VALUE_HEADS * D
    keys = rotate(kv_pre[:, :kvw].reshape(T, KEY_VALUE_HEADS, D), cosine, sine).astype(BF16)
    values = kv_pre[:, kvw:].reshape(T, KEY_VALUE_HEADS, D).astype(BF16)
    group = QUERY_HEADS // KEY_VALUE_HEADS
    qg = query.reshape(T, KEY_VALUE_HEADS, group, D)
    scores = jnp.einsum("qghd,kgd->ghqk", qg, keys, preferred_element_type=F32) * scale
    masked = jnp.where(allowed, scores, -1e30)
    top = jnp.max(masked, axis=-1, keepdims=True)
    weight = jnp.exp(masked - top)
    probs = weight / jnp.sum(weight, axis=-1, keepdims=True)
    probs_low = probs.astype(BF16)
    mixed = jnp.einsum("ghqk,kgd->qghd", probs_low, values, preferred_element_type=F32).astype(BF16)
    mixed2 = mixed.reshape(T, QUERY_HEADS * D)
    resid = stream + dot_nn(mixed2, wo)
    rstd2 = lax.rsqrt(jnp.mean(resid * resid, axis=1, keepdims=True) + EPS)
    normed2 = (resid * rstd2 * gain2).astype(BF16)

    gn = gather_tokens(lay, normed2).reshape(lay.planes * T, MODEL_WIDTH)
    dy = gdy.reshape(lay.planes * T, MODEL_WIDTH)
    gate, up = dot_nt(gn, gf[0]), dot_nt(gn, gf[1])
    sig = jax.nn.sigmoid(gate)
    act = (gate * sig * up).astype(BF16)
    down = dot_nn(act, gf[2]).astype(BF16)
    d_act = dot_nt(dy, gf[2])
    d_up = (d_act * gate * sig).astype(BF16)
    d_gate = (d_act * up * sig * (1.0 + gate * (1.0 - sig))).astype(BF16)
    f_grads = jnp.stack([dot_tn(d_gate, gn).astype(BF16), dot_tn(d_up, gn).astype(BF16), dot_tn(act, dy).astype(BF16)])
    d_n2 = (dot_nn(d_gate, gf[0]) + dot_nn(d_up, gf[1])).astype(BF16)
    f_out, d_normed2 = reduce_feed(lay, f_grads, d_n2.reshape(lay.planes, T, MODEL_WIDTH))

    scaled2 = d_normed2 * gain2
    gain2_grad = jnp.sum(d_normed2 * resid * rstd2, axis=0)
    inner2 = jnp.sum(scaled2 * resid, axis=1, keepdims=True)
    d_resid = cotangent.astype(F32) + rstd2 * scaled2 - resid * (rstd2 * rstd2 * rstd2 * inner2 / MODEL_WIDTH)
    d_attn = d_resid.astype(BF16)
    out_grad = dot_tn(mixed2, d_attn)
    d_mixed = dot_nt(d_attn, wo).astype(BF16).reshape(T, KEY_VALUE_HEADS, group, D)
    d_probs = jnp.einsum("qghd,kgd->ghqk", d_mixed, values, preferred_element_type=F32)
    delta = jnp.sum(probs * d_probs, axis=-1, keepdims=True)
    d_scores = (probs * (d_probs - delta)).astype(BF16)
    d_query = jnp.einsum("ghqk,kgd->qghd", d_scores, keys, preferred_element_type=F32).reshape(T, QUERY_HEADS, D) * scale
    d_keys = jnp.einsum("ghqk,qghd->kgd", d_scores, qg, preferred_element_type=F32) * scale
    d_values = jnp.einsum("ghqk,qghd->kgd", probs_low, d_mixed, preferred_element_type=F32)
    dq = rotate(d_query, cosine, -sine).reshape(T, QUERY_HEADS * D).astype(BF16)
    dk = rotate(d_keys, cosine, -sine).reshape(T, kvw).astype(BF16)
    dkv = jnp.concatenate([dk, d_values.reshape(T, kvw).astype(BF16)], axis=1)
    q_grad = dot_tn(dq, normed).astype(BF16)
    kv_grad = dot_tn(dkv, normed).astype(BF16)
    kv_placed = jnp.transpose(kv_grad.reshape(lay.cores, lay.dp, lay.kvrows, MODEL_WIDTH), (1, 0, 2, 3))
    a_grads = jnp.concatenate(
        [
            placed(q_grad),
            kv_placed,
            jnp.zeros((lay.dp, lay.cores, lay.out_at - lay.kv_at - lay.kvrows, MODEL_WIDTH), BF16),
            placed(out_grad.astype(BF16)),
            jnp.zeros((lay.dp, lay.cores, lay.arows - lay.out_at - lay.qrows, MODEL_WIDTH), BF16),
        ],
        axis=2,
    )
    d_normed = dot_nn(dq, wq) + dot_nn(dkv, wkv)
    scaled1 = d_normed * gain1
    gain1_grad = jnp.sum(d_normed * stream * rstd1, axis=0)
    inner1 = jnp.sum(scaled1 * stream, axis=1, keepdims=True)
    in_grad = d_resid + rstd1 * scaled1 - stream * (rstd1 * rstd1 * rstd1 * inner1 / MODEL_WIDTH)

    gain_rows = jnp.concatenate([gain1_grad[None], gain2_grad[None], jnp.zeros((6, MODEL_WIDTH), F32)], axis=0)
    a_out, down_sum, gain_sum = reduce_attn(lay, a_grads, down.reshape(lay.planes, T, MODEL_WIDTH), gain_rows)
    layer_out = (resid + down_sum).astype(BF16)
    own_gains = lax.dynamic_slice_in_dim(gain_sum, col * W, W, 1)
    heads = QUERY_HEADS // lay.cores
    query_grad = jnp.transpose(a_out[: lay.qrows].reshape(heads, D // lay.dp, W), (2, 0, 1))
    keyval_grad = jnp.transpose(a_out[lay.kv_at : lay.kv_at + lay.kvrows])[:, None, :]
    out_block = a_out[lay.out_at : lay.out_at + lay.qrows].reshape(heads, D // lay.dp, W)
    return (
        layer_out,
        in_grad.astype(BF16),
        own_gains[0],
        query_grad,
        keyval_grad,
        out_block,
        own_gains[1],
        f_out[0].T,
        f_out[1].T,
        f_out[2],
    )


def general_layout(segment, parent):
    labels = jnp.arange(SEGS, dtype=jnp.int32)
    member = (segment[:, None] == labels[None, :]).astype(jnp.float32)
    link = ((parent[:, None] == labels[None, :]) & (labels[:, None] > 0)).astype(jnp.float32)
    ident = jnp.eye(SEGS, dtype=jnp.float32)

    def climb(level, reach):
        return ident + jnp.dot(link, reach, precision=lax.Precision.HIGHEST)

    reach = lax.fori_loop(0, SEGS, climb, ident)
    visible = jnp.dot(jnp.dot(member, reach, precision=lax.Precision.HIGHEST), member.T, precision=lax.Precision.HIGHEST) > 0.5
    places = jnp.arange(segment.shape[0], dtype=jnp.int32)
    allowed = visible & (places[:, None] >= places[None, :])
    sizes = jnp.sum(member, axis=0)
    earlier = (labels[None, :] < labels[:, None]).astype(jnp.float32)
    starts = jnp.dot(earlier, sizes, precision=lax.Precision.HIGHEST)
    above = jnp.dot(reach, sizes, precision=lax.Precision.HIGHEST) - sizes
    tree_depth = places.astype(jnp.float32) + jnp.dot(member, above - starts, precision=lax.Precision.HIGHEST)
    return (allowed, tree_depth)


def general_rotate(value_rows, tree_depth, sign):
    half = value_rows.shape[-1] // 2
    freqs = jnp.arange(half, dtype=jnp.float32) * (2.0 / value_rows.shape[-1])
    inverse = jnp.exp(freqs * -math.log(THETA))
    angle = tree_depth[:, None] * inverse[None, :]
    cosine = jnp.cos(angle)[:, None, :]
    sine = sign * jnp.sin(angle)[:, None, :]
    first = value_rows[..., :half]
    second = value_rows[..., half:]
    return jnp.concatenate(
        [first * cosine - second * sine, second * cosine + first * sine], axis=-1
    )


def product(left, right):
    return jnp.dot(left, right, preferred_element_type=jnp.float32)


def general_body(
    tokens,
    cotangent,
    seg_ids,
    parents,
    norm1_gain,
    w_query,
    key_value_weight,
    w_out,
    norm2_gain,
    w_gate,
    w_up,
    w_down,
):
    columns = lax.axis_size("col")
    row_index = lax.axis_index("row")
    col_index = lax.axis_index("col")
    feature_width = MODEL_WIDTH // columns
    half_rows = columns * TREE_TOKENS // 2
    heads_here = QUERY_HEADS // 2
    query_total_width = heads_here * HEAD_SIZE
    heads_per_group = QUERY_HEADS // KEY_VALUE_HEADS
    scale = HEAD_SIZE ** (-0.5)
    stream_rows, cot_rows = (
        lax.all_to_all(tokens, "col", split_axis=1, concat_axis=0, tiled=True),
        lax.all_to_all(cotangent, "col", split_axis=1, concat_axis=0, tiled=True),
    )

    def col_total(value_rows):
        return lax.psum(value_rows, "col")

    def gather_rows(value_rows):
        return lax.all_gather(value_rows, "row", axis=0, tiled=True)

    def gather_cols(value_rows):
        return lax.all_gather(value_rows, "col", axis=0, tiled=True)

    def col_reduce(term, rows):
        return lax.psum_scatter(
            term(jnp.int32(0), rows * lax.axis_size("col")), "col", scatter_dimension=0, tiled=True
        )

    def row_reduce(term, rows):
        return lax.psum_scatter(
            term(jnp.int32(0), rows * lax.axis_size("row")), "row", scatter_dimension=0, tiled=True
        )

    def fetch():
        blocks = (
            lax.all_gather(w_query, "dp", axis=2, tiled=True),
            lax.all_gather(key_value_weight, "dp", axis=2, tiled=True),
            lax.all_gather(w_out, "dp", axis=1, tiled=True),
            lax.all_gather(w_gate, "dp", axis=1, tiled=True),
            lax.all_gather(w_up, "dp", axis=1, tiled=True),
            lax.all_gather(w_down, "dp", axis=0, tiled=True),
        )
        wide = None
        return (blocks, wide)

    def local_heads(pair_part):
        spread_heads = jnp.repeat(pair_part, heads_per_group, axis=1)
        return lax.dynamic_slice_in_dim(spread_heads, row_index * heads_here, heads_here, 1)

    def fold_heads(grad_here):
        spread_heads = jnp.zeros((TREE_TOKENS, QUERY_HEADS, HEAD_SIZE), jnp.float32)
        spread_heads = lax.dynamic_update_slice_in_dim(
            spread_heads, grad_here, row_index * heads_here, 1
        )
        return jnp.sum(
            spread_heads.reshape(TREE_TOKENS, KEY_VALUE_HEADS, heads_per_group, HEAD_SIZE), axis=2
        )

    gradients = (
        jnp.zeros((feature_width,), jnp.float32),
        jnp.zeros((feature_width, heads_here, HEAD_SIZE), jnp.float32),
        jnp.zeros((feature_width, 1, KEY_VALUE_HEADS * HEAD_SIZE), jnp.float32),
        jnp.zeros((heads_here, HEAD_SIZE, feature_width), jnp.float32),
        jnp.zeros((feature_width,), jnp.float32),
        jnp.zeros((feature_width, w_gate.shape[1] * lax.axis_size("dp")), jnp.float32),
        jnp.zeros((feature_width, w_up.shape[1] * lax.axis_size("dp")), jnp.float32),
        jnp.zeros((w_down.shape[0] * lax.axis_size("dp"), feature_width), jnp.float32),
    )
    results = []
    input_grads = []
    for batch_index in range(2):
        blocks, wide = fetch()
        (
            forward_query_block,
            forward_key_value_block,
            forward_out_block,
            forward_gate_block,
            forward_up_block,
            forward_down_block,
        ) = blocks
        forward_query_matrix = forward_query_block.reshape(feature_width, query_total_width)
        forward_key_value_matrix = forward_key_value_block.reshape(
            feature_width, KEY_VALUE_HEADS * HEAD_SIZE
        )
        forward_out_matrix = forward_out_block.reshape(query_total_width, feature_width)
        forward_stream = lax.dynamic_slice_in_dim(
            stream_rows, batch_index * half_rows, half_rows, 0
        ).astype(jnp.float32)
        forward_rstd1 = lax.rsqrt(
            col_total(jnp.sum(forward_stream * forward_stream, axis=1)) / MODEL_WIDTH + EPS
        )
        normed = (forward_stream * forward_rstd1[:, None] * norm1_gain).astype(jnp.bfloat16)
        forward_normed_all = gather_rows(normed)

        def qkv_term(start, count):
            return jnp.concatenate(
                [
                    product(forward_normed_all, forward_query_matrix),
                    product(forward_normed_all, forward_key_value_matrix),
                ],
                axis=1,
            )

        projected_rows = col_reduce(qkv_term, TREE_TOKENS)
        half_cols = columns // 2
        tree_slot = (
            col_index // half_cols * (2 * half_cols)
            + batch_index * half_cols
            + col_index % half_cols
        )
        segment = lax.dynamic_index_in_dim(seg_ids, tree_slot, 0, keepdims=False)
        parent = lax.dynamic_index_in_dim(parents, tree_slot, 0, keepdims=False)
        forward_allowed, forward_tree_depth = general_layout(segment, parent)
        query_pre = projected_rows[:, :query_total_width].reshape(
            TREE_TOKENS, heads_here, HEAD_SIZE
        )
        forward_query = general_rotate(query_pre, forward_tree_depth, 1.0).astype(jnp.bfloat16)
        own_unrotated = projected_rows[:, query_total_width:].reshape(
            TREE_TOKENS, KEY_VALUE_HEADS, HEAD_SIZE
        )
        own_part = jnp.where(
            row_index == 0, general_rotate(own_unrotated, forward_tree_depth, 1.0), own_unrotated
        ).astype(jnp.bfloat16)
        forward_pair = lax.all_gather(own_part[:, None], "row", axis=1, tiled=True)
        forward_keys_here = local_heads(forward_pair[:, 0])
        forward_values_here = local_heads(forward_pair[:, 1])
        forward_scores = (
            jnp.einsum(
                "qhd,khd->hqk", forward_query, forward_keys_here, preferred_element_type=jnp.float32
            )
            * scale
        )
        forward_masked = jnp.where(forward_allowed[None], forward_scores, -1e30)
        row_max = jnp.max(forward_masked, axis=-1, keepdims=True)
        forward_total = (
            jnp.log(jnp.sum(jnp.exp(forward_masked - row_max), axis=-1, keepdims=True)) + row_max
        )
        probs = jnp.exp(forward_masked - forward_total).astype(jnp.bfloat16)
        mixed = jnp.einsum(
            "hqk,khd->qhd", probs, forward_values_here, preferred_element_type=jnp.float32
        )
        mixed = mixed.astype(jnp.bfloat16).reshape(TREE_TOKENS, query_total_width)
        forward_mixed_all = gather_cols(mixed)

        def out_term(start, count):
            return product(forward_mixed_all, forward_out_matrix)

        forward_resid = forward_stream + row_reduce(out_term, half_rows)
        forward_rstd2 = lax.rsqrt(
            col_total(jnp.sum(forward_resid * forward_resid, axis=1)) / MODEL_WIDTH + EPS
        )
        normed2 = (forward_resid * forward_rstd2[:, None] * norm2_gain).astype(jnp.bfloat16)
        normed2_all = gather_rows(normed2)
        forward_hidden_here = forward_gate_block.shape[1]

        def gate_term(start, count):
            return jnp.concatenate(
                [product(normed2_all, forward_gate_block), product(normed2_all, forward_up_block)],
                axis=1,
            )

        gate_up = col_reduce(gate_term, TREE_TOKENS)
        forward_gate = gate_up[:, :forward_hidden_here]
        forward_up_part = gate_up[:, forward_hidden_here:]
        hidden = (jax.nn.silu(forward_gate) * forward_up_part).astype(jnp.bfloat16)
        forward_hidden_all = gather_cols(hidden)

        def down_term(start, count):
            return product(forward_hidden_all, forward_down_block)

        result = (forward_resid + row_reduce(down_term, half_rows)).astype(jnp.bfloat16)
        forward_saved = (
            forward_stream,
            forward_rstd1,
            forward_normed_all,
            forward_query,
            forward_pair,
            forward_total,
            forward_allowed,
            forward_tree_depth,
            forward_mixed_all,
            forward_resid,
            forward_rstd2,
            normed2_all,
            forward_gate,
            forward_up_part,
            forward_hidden_all,
        )
        result, saved = (result, forward_saved)
        blocks, wide = fetch()
        backward_gradients = gradients
        query_block, key_value_block, out_block, gate_block, up_block, down_block = blocks
        (
            stream,
            rstd1,
            normed_all,
            query,
            pair,
            total,
            allowed,
            tree_depth,
            mixed_all,
            resid,
            rstd2,
            kept_features,
            gate,
            up_part,
            hidden_all,
        ) = saved
        query_matrix = query_block.reshape(feature_width, query_total_width)
        key_value_matrix = key_value_block.reshape(feature_width, KEY_VALUE_HEADS * HEAD_SIZE)
        out_matrix = out_block.reshape(query_total_width, feature_width)
        hidden_here = gate_block.shape[1]
        cot_low = lax.dynamic_slice_in_dim(cot_rows, batch_index * half_rows, half_rows, 0)
        cot_full = cot_low.astype(jnp.float32)
        cot_all = gather_rows(cot_low)
        down_grad = jnp.einsum("tf,td->fd", hidden_all, cot_all, preferred_element_type=jnp.float32)

        def hidden_term(start, count):
            return jnp.einsum("td,fd->tf", cot_all, down_block, preferred_element_type=jnp.float32)

        d_hidden = col_reduce(hidden_term, TREE_TOKENS)
        sigmoid_gate = jax.nn.sigmoid(gate)
        d_up = (d_hidden * gate * sigmoid_gate).astype(jnp.bfloat16)
        d_gate = (d_hidden * up_part * sigmoid_gate * (1.0 + gate * (1.0 - sigmoid_gate))).astype(
            jnp.bfloat16
        )
        d_both = gather_cols(jnp.concatenate([d_gate, d_up], axis=1))
        gate_grad = jnp.einsum(
            "td,tf->df", kept_features, d_both[:, :hidden_here], preferred_element_type=jnp.float32
        )
        up_grad = jnp.einsum(
            "td,tf->df", kept_features, d_both[:, hidden_here:], preferred_element_type=jnp.float32
        )

        def back2_term(start, count):
            first = jnp.einsum(
                "tf,df->td", d_both[:, :hidden_here], gate_block, preferred_element_type=jnp.float32
            )
            return first + jnp.einsum(
                "tf,df->td", d_both[:, hidden_here:], up_block, preferred_element_type=jnp.float32
            )

        d_normed2 = row_reduce(back2_term, half_rows)
        scaled2 = d_normed2 * norm2_gain
        gain2_grad = jnp.sum(d_normed2 * resid * rstd2[:, None], axis=0)
        inner2 = col_total(jnp.sum(scaled2 * resid, axis=1))
        d_resid = (
            cot_full
            + rstd2[:, None] * scaled2
            - resid * (rstd2 * rstd2 * rstd2 * inner2 / MODEL_WIDTH)[:, None]
        )
        d_attn_all = gather_rows(d_resid.astype(jnp.bfloat16))
        out_grad = jnp.einsum(
            "tq,td->qd", mixed_all, d_attn_all, preferred_element_type=jnp.float32
        )

        def mixed_term(start, count):
            return jnp.einsum(
                "td,qd->tq", d_attn_all, out_matrix, preferred_element_type=jnp.float32
            )

        d_mixed = (
            col_reduce(mixed_term, TREE_TOKENS)
            .astype(jnp.bfloat16)
            .reshape(TREE_TOKENS, heads_here, HEAD_SIZE)
        )
        keys_here = local_heads(pair[:, 0])
        values_here = local_heads(pair[:, 1])
        scores = (
            jnp.einsum("qhd,khd->hqk", query, keys_here, preferred_element_type=jnp.float32) * scale
        )
        masked = jnp.where(allowed[None], scores, -1e30)
        probs_full = jnp.exp(masked - total)
        probs_low = probs_full.astype(jnp.bfloat16)
        d_probs = jnp.einsum(
            "qhd,khd->hqk", d_mixed, values_here, preferred_element_type=jnp.float32
        )
        delta = jnp.sum(probs_full * d_probs, axis=-1, keepdims=True)
        d_scores = (probs_full * (d_probs - delta)).astype(jnp.bfloat16)
        d_query = (
            jnp.einsum("hqk,khd->qhd", d_scores, keys_here, preferred_element_type=jnp.float32)
            * scale
        )
        d_keys = (
            jnp.einsum("hqk,qhd->khd", d_scores, query, preferred_element_type=jnp.float32) * scale
        )
        d_values = jnp.einsum(
            "hqk,qhd->khd", probs_low, d_mixed, preferred_element_type=jnp.float32
        )
        d_pair = jnp.stack([fold_heads(d_keys), fold_heads(d_values)], axis=1)
        own_gradient = lax.psum_scatter(
            d_pair.astype(jnp.bfloat16), "row", scatter_dimension=1, tiled=True
        ).astype(jnp.float32)[:, 0]
        own_gradient = jnp.where(
            row_index == 0, general_rotate(own_gradient, tree_depth, -1.0), own_gradient
        )
        query_pre_gradient = general_rotate(d_query, tree_depth, -1.0)
        d_proj = jnp.concatenate(
            [
                query_pre_gradient.reshape(TREE_TOKENS, query_total_width),
                own_gradient.reshape(TREE_TOKENS, KEY_VALUE_HEADS * HEAD_SIZE),
            ],
            axis=1,
        ).astype(jnp.bfloat16)
        d_proj_all = gather_cols(d_proj)
        query_grad = jnp.einsum(
            "td,tq->dq",
            normed_all,
            d_proj_all[:, :query_total_width],
            preferred_element_type=jnp.float32,
        )
        keyval_grad = jnp.einsum(
            "td,tq->dq",
            normed_all,
            d_proj_all[:, query_total_width:],
            preferred_element_type=jnp.float32,
        )
        in_matrix = jnp.concatenate([query_matrix, key_value_matrix], axis=1)

        def back1_term(start, count):
            return jnp.einsum(
                "tq,dq->td", d_proj_all, in_matrix, preferred_element_type=jnp.float32
            )

        d_normed = row_reduce(back1_term, half_rows)
        scaled1 = d_normed * norm1_gain
        gain1_grad = jnp.sum(d_normed * stream * rstd1[:, None], axis=0)
        inner1 = col_total(jnp.sum(scaled1 * stream, axis=1))
        d_stream = (
            d_resid
            + rstd1[:, None] * scaled1
            - stream * (rstd1 * rstd1 * rstd1 * inner1 / MODEL_WIDTH)[:, None]
        )
        updates = (
            gain1_grad,
            query_grad.reshape(query_block.shape),
            keyval_grad.reshape(key_value_block.shape),
            out_grad.reshape(out_block.shape),
            gain2_grad,
            gate_grad,
            up_grad,
            down_grad,
        )
        backward_gradients = tuple((a + b for a, b in zip(backward_gradients, updates)))
        d_stream, gradients = (d_stream.astype(jnp.bfloat16), backward_gradients)
        results.append(result)
        input_grads.append(d_stream)
    shards = (
        lax.psum_scatter(
            gradients[1].astype(jnp.bfloat16), "dp", scatter_dimension=2, tiled=True
        ).astype(jnp.float32),
        lax.psum_scatter(
            gradients[2].astype(jnp.bfloat16), "dp", scatter_dimension=2, tiled=True
        ).astype(jnp.float32),
        lax.psum_scatter(
            gradients[3].astype(jnp.bfloat16), "dp", scatter_dimension=1, tiled=True
        ).astype(jnp.float32),
        lax.psum_scatter(
            gradients[5].astype(jnp.bfloat16), "dp", scatter_dimension=1, tiled=True
        ).astype(jnp.float32),
        lax.psum_scatter(
            gradients[6].astype(jnp.bfloat16), "dp", scatter_dimension=1, tiled=True
        ).astype(jnp.float32),
        lax.psum_scatter(
            gradients[7].astype(jnp.bfloat16), "dp", scatter_dimension=0, tiled=True
        ).astype(jnp.float32),
    )
    gains = lax.psum((gradients[0], gradients[4]), ("dp", "row"))
    final_out, final_grad = (
        lax.all_to_all(
            jnp.concatenate(results, axis=0), "col", split_axis=0, concat_axis=1, tiled=True
        ),
        lax.all_to_all(
            jnp.concatenate(input_grads, axis=0), "col", split_axis=0, concat_axis=1, tiled=True
        ),
    )
    return (
        final_out,
        final_grad,
        gains[0],
        shards[0],
        shards[1],
        shards[2],
        gains[1],
        shards[3],
        shards[4],
        shards[5],
    )


def solution(mesh):
    placed = (
        P(("dp", "row", "col"), None),
        P(("dp", "row", "col"), None),
        P("dp", None),
        P("dp", None),
        P("col"),
        P("col", "row", "dp"),
        P("col", "row", "dp"),
        P("row", "dp", "col"),
        P("col"),
        P("col", ("dp", "row")),
        P("col", ("dp", "row")),
        P(("dp", "row"), "col"),
    )
    lay = Layout(mesh.shape)
    work = functools.partial(body, lay) if lay.fits() else general_body
    return jax.shard_map(
        work,
        mesh=mesh,
        in_specs=placed,
        out_specs=(
            P(("dp", "row", "col"), None),
            P(("dp", "row", "col"), None),
            P("col"),
            P("col", "row", "dp"),
            P("col", "row", "dp"),
            P("row", "dp", "col"),
            P("col"),
            P("col", ("dp", "row")),
            P("col", ("dp", "row")),
            P(("dp", "row"), "col"),
        ),
        check_vma=False,
    )
```

```python
import functools
import math

import jax
import jax.numpy as jnp
from jax import lax
from jax.experimental import pallas as pl
from jax.experimental.pallas import tpu as pltpu
from jax.sharding import PartitionSpec as P

MODEL_WIDTH = 1280
QUERY_HEADS = 20
KEY_VALUE_HEADS = 5
HEAD_SIZE = 64
TREE_TOKENS = 128
SEGS = 13
PLANES = 4

EPS = 1e-05
THETA = 10000.0
MESH = pl.DeviceIdType.MESH
F32 = jnp.float32
BF16 = jnp.bfloat16


class Layout:
    def __init__(self, shape):
        self.planes = PLANES
        self.lines = shape["dp"] // PLANES
        self.cores = shape["row"]
        self.cols = shape["col"]
        self.dp = shape["dp"]
        self.width = MODEL_WIDTH // self.cols
        self.qrows = QUERY_HEADS // self.cores * (HEAD_SIZE // self.dp)
        self.kvrows = KEY_VALUE_HEADS * HEAD_SIZE // self.dp
        self.kv_at = self.qrows
        self.out_at = -(-(self.kv_at + self.kvrows) // 16) * 16
        self.arows = -(-(self.out_at + self.qrows) // 16) * 16
        self.acut = -(-(self.arows // 2) // 16) * 16

    def fits(self):
        return self.lines == 2 and self.cores == 2 and self.cols == 2 and self.dp == 2 * PLANES

    def here(self):
        dp = lax.axis_index("dp")
        return dp // self.lines, lax.rem(dp, self.lines), lax.axis_index("row"), lax.axis_index("col")

    def device(self, z, x, r, c):
        return (z * self.lines + x, r, c)


def greet(lay, peers):
    barrier = pltpu.get_barrier_semaphore()
    for peer in peers:
        pl.semaphore_signal(barrier, inc=1, device_id=peer, device_id_type=MESH)
    pl.semaphore_wait(barrier, len(peers))


def dot_nt(left, right):
    return lax.dot_general(left, right, (((1,), (1,)), ((), ())), preferred_element_type=F32)


def dot_tn(left, right):
    return lax.dot_general(left, right, (((0,), (0,)), ((), ())), preferred_element_type=F32)


def dot_nn(left, right):
    return jnp.dot(left, right, preferred_element_type=F32)


class Links:
    def __init__(self, send_sems, recv_sems):
        self.send_sems, self.recv_sems, self.used = send_sems, recv_sems, 0
        self.open = []

    def send(self, src, dst, peer, source=None):
        copy = pltpu.make_async_remote_copy(
            src_ref=src,
            dst_ref=dst,
            send_sem=self.send_sems.at[self.used],
            recv_sem=self.recv_sems.at[self.used],
            device_id=peer,
            device_id_type=MESH,
        )
        self.used += 1
        copy.start()
        self.open.append((source, copy))
        return copy

    def flush(self, *sources):
        for source, copy in self.open:
            if not sources or source in sources:
                copy.wait_send()
        self.open = [o for o in self.open if sources and o[0] not in sources]


def turn(rows, cosine, sine):
    lanes = rows.shape[1]
    many = lanes // 128
    half = HEAD_SIZE // 2
    lane = lax.broadcasted_iota(jnp.int32, rows.shape, 1)
    swapped = jnp.where(
        lax.rem(lane, HEAD_SIZE) < half, pltpu.roll(rows, lanes - half, 1), pltpu.roll(rows, half, 1)
    )
    wide = lambda t: t if many == 1 else jnp.concatenate([t] * many, axis=1)
    return rows * wide(cosine) + swapped * wide(sine)


def stack_heads(rows, count):
    return jnp.concatenate([rows[:, i * HEAD_SIZE : (i + 1) * HEAD_SIZE] for i in range(count)], axis=0)


def spread_heads(rows, count):
    return jnp.concatenate([rows[i * TREE_TOKENS : (i + 1) * TREE_TOKENS] for i in range(count)], axis=1)


def add_into(dest, other, step):
    def some(i, _):
        rows = pl.ds(pl.multiple_of(i * step, step), step)
        dest[rows, :] = (dest[rows, :].astype(F32) + other[rows, :].astype(F32)).astype(dest.dtype)
        return 0

    lax.fori_loop(0, dest.shape[0] // step, some, 0)


def sum_into(dest, parts, step):
    def some(i, _):
        rows = pl.ds(pl.multiple_of(i * step, step), step)
        acc = parts[0][rows, :].astype(F32)
        for part in parts[1:]:
            acc = acc + part[rows, :].astype(F32)
        dest[rows, :] = acc.astype(dest.dtype)
        return 0

    lax.fori_loop(0, dest.shape[0] // step, some, 0)


ORDER = (0, 1, 3, 2)


def layer_kernel(
    lay,
    a_ref, f_ref, tok_ref, cot_ref, gain_ref, seg_ref, par_ref,
    out_ref, in_grad_ref, gain_out, a_out, f_out,
    ga, gf, wq, wkv, wo, gn, gdy, act, dgate, dup, d_act, gfull, normed, qs, ks, vs, probs, mix, resid,
    rot_cos, rot_sin, dq, dk5, dv5, d_part, d_in, y_part, y_in,
    fc_in, f1a, f1b, f2a, f2b, ac_in, a1a, a1b, a2a, a2b, az_in, nsum, nin,
    send_sems, recv_sems, own_sems,
):
    z, x, r, c = lay.here()
    W, T, D = lay.width, TREE_TOKENS, HEAD_SIZE
    frows = f_ref.shape[1]
    hid = lay.lines * lay.cores * frows
    groups = KEY_VALUE_HEADS
    per = QUERY_HEADS // KEY_VALUE_HEADS
    kvw = KEY_VALUE_HEADS * D
    scale = D**-0.5
    x_other, c_other, r_other = 1 - x, 1 - c, 1 - r
    x_peer = lay.device(z, x_other, r, c)
    y_peer = lay.device(z, x, r, c_other)
    sibling = lay.device(z, x, r_other, c)
    plus = lambda k: lax.rem(z + k, lay.planes)
    minus = lambda k: lax.rem(z + lay.planes - k, lay.planes)
    z_peer = lambda k: lay.device(plus(k), x, r, c)
    lanes = lambda cc: pl.ds(pl.multiple_of(cc * W, 128), W)
    links = Links(send_sems, recv_sems)
    send = links.send

    greet(lay, [z_peer(k) for k in ORDER[1:]] + [x_peer, y_peer, sibling])

    gain_y = send(gain_ref, gfull.at[:, lanes(c)], y_peer)

    def block(zz, xx, rr):
        return ga.at[zz * lay.lines + xx, rr]

    own = [
        pltpu.make_async_copy(a_ref, block(z, x, r).at[:, lanes(c)], own_sems.at[0]),
        pltpu.make_async_copy(cot_ref, gdy.at[0], own_sems.at[1]),
        pltpu.make_async_copy(gain_ref, gfull.at[:, lanes(c)], own_sems.at[2]),
    ]
    for copy in own:
        copy.start()
    az, dz, ax, ay, arx, ary, acore = {}, {}, {}, {}, {}, {}, {}
    ax[0] = send(a_ref, block(z, x, r).at[:, lanes(c)], x_peer)
    ay[0] = send(a_ref, block(z, x, r).at[:, lanes(c)], y_peer)
    for k in ORDER[1:]:
        az[k] = send(a_ref, block(z, x, r).at[:, lanes(c)], z_peer(k))
    for s, k in enumerate(ORDER):
        if k:
            dz[s] = send(cot_ref, gdy.at[s], z_peer(k))

    cut = lay.acut

    def a_own(k):
        az[k].wait_recv()
        here = block(minus(k), x, r).at[:, lanes(c)]
        ax[k] = send(here, here, x_peer, "ga")
        ay[k] = send(here, here, y_peer, "ga")

    def a_relay(k):
        ax[k].wait_recv()
        top = block(minus(k), x_other, r).at[pl.ds(0, cut), lanes(c)]
        ary[k] = send(top, top, y_peer, "ga")
        ay[k].wait_recv()
        low = block(minus(k), x, r).at[pl.ds(cut, lay.arows - cut), lanes(c_other)]
        arx[k] = send(low, low, x_peer, "ga")
        acore[k, 0] = send(block(minus(k), x, r), block(minus(k), x, r), sibling, "ga")

    def a_finish(k):
        ary[k].wait_recv()
        arx[k].wait_recv()
        acore[k, 1] = send(block(minus(k), x_other, r), block(minus(k), x_other, r), sibling, "ga")

    def a_unpack(k):
        acore[k, 0].wait_recv()
        acore[k, 1].wait_recv()
        zz = minus(k)
        heads = QUERY_HEADS // lay.cores
        for rr in range(lay.cores):

            def pair(m, _):
                for base, dest in ((0, wq), (lay.out_at, wo)):
                    rows = pl.ds(pl.multiple_of(base + m * 16, 16), 16)
                    left = ga[zz * lay.lines, rr, rows, :].astype(F32)
                    right = ga[zz * lay.lines + 1, rr, rows, :].astype(F32)
                    at = (rr * heads + 2 * m) * D + zz * 16
                    dest[pl.ds(pl.multiple_of(at, 16), 16), :] = jnp.concatenate([left[:8], right[:8]], axis=0).astype(BF16)
                    dest[pl.ds(pl.multiple_of(at + D, 16), 16), :] = jnp.concatenate([left[8:], right[8:]], axis=0).astype(BF16)
                return 0

            lax.fori_loop(0, heads // 2, pair, 0)
            n = lay.kvrows
            left = ga[zz * lay.lines, rr, lay.kv_at : lay.out_at, :].astype(F32)
            right = ga[zz * lay.lines + 1, rr, lay.kv_at : lay.out_at, :].astype(F32)
            at = rr * kvw + zz * (2 * n)
            wkv[pl.ds(pl.multiple_of(at, 16), 2 * n), :] = jnp.concatenate([left[:n], right[:n]], axis=0).astype(BF16)

    stream = tok_ref[...].astype(F32)
    rstd1 = lax.rsqrt(jnp.sum(stream * stream, axis=1, keepdims=True) / MODEL_WIDTH + EPS)
    tree = r * lay.cols + c
    seg_row = jnp.broadcast_to(seg_ref[pl.ds(tree, 1), :].astype(F32), (T, T))
    par_row = par_ref[pl.ds(tree, 1), :].astype(F32)
    seg_col = jnp.transpose(seg_row)
    above = jnp.zeros((T, T), F32)
    for s in range(par_ref.shape[1]):
        above = jnp.where(seg_col == s, par_row[:, s : s + 1], above)
    row_at = lax.broadcasted_iota(jnp.int32, (T, T), 0)
    lane_at = lax.broadcasted_iota(jnp.int32, (T, T), 1)
    seen = (seg_row == seg_col) | (seg_row == above) | (seg_row == 0.0)
    allowed = jnp.where(seen & (row_at >= lane_at), 1.0, 0.0)
    depth = jnp.sum(allowed, axis=1, keepdims=True) - 1.0
    freq = lax.rem(lane_at, D // 2).astype(F32) * (2.0 / D)
    angle = depth * jnp.exp(freq * -math.log(THETA))
    rot_cos[...] = jnp.cos(angle)
    sine = jnp.sin(angle)
    rot_sin[...] = jnp.where(lax.rem(lane_at, D) < D // 2, -sine, sine)
    for copy in own:
        copy.wait()
    gain_y.wait_recv()
    normed[...] = (stream * rstd1 * gfull[0:1, :]).astype(BF16)

    a_own(1)
    a_relay(0)
    a_own(3)
    a_finish(0)
    a_relay(1)
    a_finish(1)
    a_unpack(0)
    a_own(2)
    a_relay(3)
    a_unpack(1)
    a_finish(3)
    a_relay(2)

    def f_rows(xx, rr):
        return pl.ds(pl.multiple_of((xx * lay.cores + rr) * frows, 16), frows)

    def f_part(xx, low):
        half = frows // 2
        return pl.ds(pl.multiple_of((xx * lay.cores + r) * frows + low * half, 16), half)

    fx, fy, frx, fry, fcore = {}, {}, {}, {}, {}
    f_own = []
    for i, w in enumerate((2, 0, 1)):
        here = gf.at[w, f_rows(x, r), lanes(c)]
        copy = pltpu.make_async_copy(f_ref.at[w], here, own_sems.at[3 + i])
        copy.start()
        f_own.append(copy)
        fx[w] = send(f_ref.at[w], here, x_peer)
        fy[w] = send(f_ref.at[w], here, y_peer)

    def f_relay(w):
        fx[w].wait_recv()
        top = gf.at[w, f_part(x_other, 0), lanes(c)]
        fry[w] = send(top, top, y_peer, "gf")
        fy[w].wait_recv()
        low = gf.at[w, f_part(x, 1), lanes(c_other)]
        frx[w] = send(low, low, x_peer, "gf")
        mine = gf.at[w, f_rows(x, r), :]
        fcore[w, 0] = send(mine, mine, sibling, "gf")

    def f_finish(w):
        fry[w].wait_recv()
        frx[w].wait_recv()
        there = gf.at[w, f_rows(x_other, r), :]
        fcore[w, 1] = send(there, there, sibling, "gf")

    def f_ready(w):
        fcore[w, 0].wait_recv()
        fcore[w, 1].wait_recv()

    a_unpack(3)
    for copy in f_own:
        copy.wait()
    a_finish(2)
    a_unpack(2)

    kv = dot_nt(normed[...], wkv[...])
    turned = turn(kv, rot_cos[...], rot_sin[...])
    for g in range(groups):
        ks[g] = turned[:, g * D : (g + 1) * D].astype(BF16)
        vs[g] = kv[:, kvw + g * D : kvw + (g + 1) * D].astype(BF16)
    allowed4 = jnp.concatenate([allowed] * per, axis=0) > 0.5
    for g in range(groups):
        cols = slice(g * per * D, (g + 1) * per * D)
        pre = turn(dot_nt(normed[...], wq[cols, :]), rot_cos[...], rot_sin[...])
        qs[g] = stack_heads(pre, per).astype(BF16)
        scores = jnp.where(allowed4, dot_nt(qs[g], ks[g]) * scale, -1e30)
        weight = jnp.exp(scores - jnp.max(scores, axis=1, keepdims=True))
        share = weight / jnp.sum(weight, axis=1, keepdims=True)
        probs[g] = share
        mixed = dot_nn(share.astype(BF16), vs[g])
        mix[:, cols] = spread_heads(mixed, per).astype(BF16)
    f_relay(2)
    res = stream + dot_nn(mix[...], wo[...])
    resid[...] = res
    rstd2 = lax.rsqrt(jnp.sum(res * res, axis=1, keepdims=True) / MODEL_WIDTH + EPS)
    gn[0] = (res * rstd2 * gfull[1:2, :]).astype(BF16)
    nz = {}
    for s, k in enumerate(ORDER):
        if k:
            nz[s] = send(gn.at[0], gn.at[s], z_peer(k))
    f_finish(2)
    f_relay(0)
    for s in dz:
        dz[s].wait_recv()
    f_ready(2)
    n_rows = lay.planes * T
    dy_all = lambda: gdy[...].reshape(n_rows, MODEL_WIDTH)
    d_act[...] = dot_nt(dy_all(), gf[2])
    f_finish(0)
    f_relay(1)
    f_ready(0)
    f_finish(1)
    f_ready(1)

    def feed(first, last):
        count = (last - first) * T
        rows = slice(first * T, last * T)
        n2 = gn[first:last].reshape(count, MODEL_WIDTH)
        gate = dot_nt(n2, gf[0])
        up = dot_nt(n2, gf[1])
        sig = 1.0 / (1.0 + jnp.exp(-gate))
        silu = gate * sig
        act[rows, :] = (silu * up).astype(BF16)
        da = d_act[rows, :]
        dup[rows, :] = (da * silu).astype(BF16)
        dgate[rows, :] = (da * up * sig * (1.0 + gate * (1.0 - sig))).astype(BF16)

    def back(first, last):
        count = (last - first) * T
        rows = slice(first * T, last * T)
        part = dot_nn(dgate[rows, :], gf[0]) + dot_nn(dup[rows, :], gf[1])
        d_part[first:last] = part.astype(BF16).reshape(last - first, T, MODEL_WIDTH)

    dnz = {}

    def back_send(s):
        dnz[s] = send(d_part.at[s], d_in.at[s - 1], lay.device(minus(ORDER[s]), x, r, c))

    nz[1].wait_recv()
    nz[2].wait_recv()
    feed(1, 3)
    back(1, 3)
    back_send(1)
    back_send(2)
    nz[3].wait_recv()
    feed(3, 4)
    back(3, 4)
    back_send(3)
    feed(0, 1)
    back(0, 1)

    links.flush("ga", "gf")
    fc, fs1a, fs1b, fs2a, fs2b = {}, {}, {}, {}, {}

    def f_grad(w):
        n2 = gn[...].reshape(n_rows, MODEL_WIDTH)
        if w == 0:
            grad = dot_tn(dgate[...], n2)
        elif w == 1:
            grad = dot_tn(dup[...], n2)
        else:
            grad = dot_tn(act[...], dy_all())
        gf[w] = grad.astype(BF16)
        for xx in range(lay.lines):
            fc[w, xx] = send(gf.at[w, f_rows(xx, r_other), :], fc_in.at[w, xx], sibling)

    def f_stage1(w):
        for xx in range(lay.lines):
            fc[w, xx].wait_recv()
            add_into(gf.at[w, f_rows(xx, r), :], fc_in.at[w, xx], 32)
        fs1a[w] = send(gf.at[w, f_part(x_other, 0), :], f1a.at[w], x_peer)
        for xx in range(lay.lines):
            fs1b[w, xx] = send(gf.at[w, f_part(xx, 1), lanes(c_other)], f1b.at[w, xx], y_peer)

    def f_stage2(w):
        fs1a[w].wait_recv()
        add_into(gf.at[w, f_part(x, 0), :], f1a.at[w], 16)
        fs2a[w] = send(gf.at[w, f_part(x, 0), lanes(c_other)], f2a.at[w], y_peer)
        for xx in range(lay.lines):
            fs1b[w, xx].wait_recv()
            add_into(gf.at[w, f_part(xx, 1), lanes(c)], f1b.at[w, xx], 16)
        fs2b[w] = send(gf.at[w, f_part(x_other, 1), lanes(c)], f2b.at[w], x_peer)

    def f_total(w):
        half = frows // 2
        fs2a[w].wait_recv()
        sum_into(f_out.at[w, pl.ds(0, half), :], [gf.at[w, f_part(x, 0), lanes(c)], f2a.at[w]], 16)
        fs2b[w].wait_recv()
        sum_into(f_out.at[w, pl.ds(half, half), :], [gf.at[w, f_part(x, 1), lanes(c)], f2b.at[w]], 16)

    f_grad(0)
    f_grad(1)
    f_stage1(0)
    y_all = dot_nn(act[...], gf[2])
    y_part[...] = y_all.astype(BF16).reshape(lay.planes, T, MODEL_WIDTH)
    yz = {}
    for s, k in enumerate(ORDER):
        if k:
            yz[s] = send(y_part.at[s], y_in.at[s - 1], lay.device(minus(k), x, r, c))
    f_grad(2)
    f_stage1(1)
    f_stage1(2)
    f_stage2(0)

    for s in dnz:
        dnz[s].wait_recv()
    d_n2 = d_part[0].astype(F32)
    for s in range(lay.planes - 1):
        d_n2 = d_n2 + d_in[s].astype(F32)
    res = resid[...]
    rstd2 = lax.rsqrt(jnp.sum(res * res, axis=1, keepdims=True) / MODEL_WIDTH + EPS)
    gain2_grad = jnp.sum(d_n2 * res * rstd2, axis=0, keepdims=True)
    scaled2 = d_n2 * gfull[1:2, :]
    inner2 = jnp.sum(scaled2 * res, axis=1, keepdims=True)
    d_res = cot_ref[...].astype(F32) + rstd2 * scaled2 - res * (rstd2 * rstd2 * rstd2 * inner2 / MODEL_WIDTH)
    d_attn = d_res.astype(BF16)

    def place_heads(source, other, base):
        heads = QUERY_HEADS // lay.cores
        for rr in range(lay.cores):
            for m in range(heads // 2):
                at = (rr * heads + 2 * m) * D
                grad = dot_tn(source[:, at : at + 2 * D], other)
                for dp in range(lay.dp):
                    tile = jnp.concatenate([grad[dp * 8 : dp * 8 + 8], grad[D + dp * 8 : D + dp * 8 + 8]], axis=0)
                    ga[dp, rr, base + m * 16 : base + m * 16 + 16, :] = tile.astype(BF16)

    place_heads(mix, d_attn, lay.out_at)
    for g in range(groups):
        cols = slice(g * per * D, (g + 1) * per * D)
        dms = stack_heads(dot_nt(d_attn, wo[cols, :]), per).astype(BF16)
        share = probs[g]
        dp_ = dot_nt(dms, vs[g])
        delta = jnp.sum(share * dp_, axis=1, keepdims=True)
        ds_ = (share * (dp_ - delta)).astype(BF16)
        d_query = spread_heads(dot_nn(ds_, ks[g]) * scale, per)
        dq[:, cols] = turn(d_query, rot_cos[...], -rot_sin[...]).astype(BF16)
        dk5[g] = dot_tn(ds_, qs[g]) * scale
        dv5[g] = dot_tn(share.astype(BF16), dms)
    f_stage2(1)
    zeros = jnp.zeros((T, D), F32)
    dk_all = jnp.concatenate([dk5[g] for g in range(groups)] + [zeros], axis=1)
    dk = turn(dk_all, rot_cos[...], -rot_sin[...])[:, :kvw].astype(BF16)
    dv = jnp.concatenate([dv5[g] for g in range(groups)], axis=1).astype(BF16)
    place_heads(dq, normed[...], 0)
    for rr, rows in enumerate((dk, dv)):
        grad = dot_tn(rows, normed[...])
        pad = jnp.zeros((lay.out_at - lay.kv_at - lay.kvrows, MODEL_WIDTH), F32)
        for dp in range(lay.dp):
            tile = jnp.concatenate([grad[dp * lay.kvrows : (dp + 1) * lay.kvrows], pad], axis=0)
            ga[dp, rr, lay.kv_at : lay.out_at, :] = tile.astype(BF16)

    last_order = (2, 1, 3, 0)
    ac, as1a, as1b, as2a, as2b, asz = {}, {}, {}, {}, {}, {}
    for k in last_order:
        for xx in range(lay.lines):
            ac[k, xx] = send(block(plus(k), xx, r_other), ac_in.at[k, xx], sibling)

    top = pl.ds(0, cut)
    low = pl.ds(cut, lay.arows - cut)

    def a_stage1(k):
        for xx in range(lay.lines):
            ac[k, xx].wait_recv()
            add_into(block(plus(k), xx, r), ac_in.at[k, xx], 16)
        as1a[k] = send(block(plus(k), x_other, r).at[top, :], a1a.at[k], x_peer)
        for xx in range(lay.lines):
            as1b[k, xx] = send(block(plus(k), xx, r).at[low, lanes(c_other)], a1b.at[k, xx], y_peer)

    def a_stage2(k):
        as1a[k].wait_recv()
        add_into(block(plus(k), x, r).at[top, :], a1a.at[k], 16)
        as2a[k] = send(block(plus(k), x, r).at[top, lanes(c_other)], a2a.at[k], y_peer)
        for xx in range(lay.lines):
            as1b[k, xx].wait_recv()
            add_into(block(plus(k), xx, r).at[low, lanes(c)], a1b.at[k, xx], 16)
        as2b[k] = send(block(plus(k), x_other, r).at[low, lanes(c)], a2b.at[k], x_peer)

    def a_line(k):
        as2a[k].wait_recv()
        add_into(block(plus(k), x, r).at[top, lanes(c)], a2a.at[k], 16)
        as2b[k].wait_recv()
        add_into(block(plus(k), x, r).at[low, lanes(c)], a2b.at[k], 16)
        if k:
            asz[k] = send(block(plus(k), x, r).at[:, lanes(c)], az_in.at[k - 1], z_peer(k))

    a_stage1(2)
    d_normed = dot_nn(dq[...], wq[...]) + dot_nn(dk, wkv[:kvw, :]) + dot_nn(dv, wkv[kvw:, :])
    a_stage1(1)
    f_stage2(2)
    stream = tok_ref[...].astype(F32)
    rstd1 = lax.rsqrt(jnp.sum(stream * stream, axis=1, keepdims=True) / MODEL_WIDTH + EPS)
    gain1_grad = jnp.sum(d_normed * stream * rstd1, axis=0, keepdims=True)
    nsum[0] = jnp.concatenate([gain1_grad, gain2_grad, jnp.zeros((6, MODEL_WIDTH), F32)], axis=0)
    g_core = send(nsum.at[0], nin.at[0], sibling)
    scaled1 = d_normed * gfull[0:1, :]
    inner1 = jnp.sum(scaled1 * stream, axis=1, keepdims=True)
    in_grad = d_res + rstd1 * scaled1 - stream * (rstd1 * rstd1 * rstd1 * inner1 / MODEL_WIDTH)
    in_grad_ref[...] = in_grad.astype(BF16)
    a_stage1(3)
    a_stage1(0)
    a_stage2(2)
    g_core.wait_recv()
    nsum[1] = nsum[0] + nin[0]
    g_x = send(nsum.at[1], nin.at[1], x_peer)
    for s in yz:
        yz[s].wait_recv()
    y = resid[...] + y_part[0].astype(F32)
    for s in range(lay.planes - 1):
        y = y + y_in[s].astype(F32)
    out_ref[...] = y.astype(BF16)
    f_total(0)
    f_total(1)
    a_stage2(1)
    a_line(2)
    g_x.wait_recv()
    nsum[2] = nsum[1] + nin[1]
    g_y = send(nsum.at[2], nin.at[2], y_peer)
    f_total(2)
    a_stage2(3)
    a_line(1)
    g_y.wait_recv()
    nsum[3] = nsum[2] + nin[2]
    g_z = {k: send(nsum.at[3], nin.at[2 + k], z_peer(k)) for k in ORDER[1:]}
    a_stage2(0)
    a_line(3)
    total = nsum[3]
    for k in g_z:
        g_z[k].wait_recv()
        total = total + nin[2 + k]
    nsum[4] = total
    gain_out[...] = nsum[4, :, lanes(c)]
    a_line(0)
    for k in asz:
        asz[k].wait_recv()
    sum_into(a_out, [block(z, x, r).at[:, lanes(c)]] + [az_in.at[k] for k in range(lay.planes - 1)], 16)
    links.flush()


def whole_layer(lay, a_shard, f_shard, tokens, cotangent, gains, seg_ids, parents):
    vm = lambda *shape: pltpu.VMEM(shape, BF16)
    vf = lambda *shape: pltpu.VMEM(shape, F32)
    M, T, D, W = MODEL_WIDTH, TREE_TOKENS, HEAD_SIZE, lay.width
    frows = f_shard.shape[1]
    hid = lay.lines * lay.cores * frows
    G, per = KEY_VALUE_HEADS, QUERY_HEADS // KEY_VALUE_HEADS
    n, nl, half = lay.planes, lay.lines, frows // 2
    vmem = pl.BlockSpec(memory_space=pltpu.VMEM)
    cut, rest = lay.acut, lay.arows - lay.acut
    scratch = [
        vm(lay.dp, lay.cores, lay.arows, M),
        vm(3, hid, M),
        vm(QUERY_HEADS * D, M),
        vm(2 * G * D, M),
        vm(QUERY_HEADS * D, M),
        vm(n, T, M),
        vm(n, T, M),
        vm(n * T, hid),
        vm(n * T, hid),
        vm(n * T, hid),
        vf(n * T, hid),
        vf(8, M),
        vm(T, M),
        vm(G, per * T, D),
        vm(G, T, D),
        vm(G, T, D),
        vf(G, per * T, T),
        vm(T, M),
        vf(T, M),
        vf(T, T),
        vf(T, T),
        vm(T, M),
        vf(G, T, D),
        vf(G, T, D),
        vm(n, T, M),
        vm(n - 1, T, M),
        vm(n, T, M),
        vm(n - 1, T, M),
        vm(3, nl, frows, M),
        vm(3, half, M),
        vm(3, nl, half, W),
        vm(3, half, W),
        vm(3, half, W),
        vm(n, nl, lay.arows, M),
        vm(n, cut, M),
        vm(n, nl, rest, W),
        vm(n, cut, W),
        vm(n, rest, W),
        vm(n - 1, lay.arows, W),
        vf(5, 8, M),
        vf(2 + n, 8, M),
        pltpu.SemaphoreType.DMA((144,)),
        pltpu.SemaphoreType.DMA((144,)),
        pltpu.SemaphoreType.DMA((6,)),
    ]
    return pl.pallas_call(
        functools.partial(layer_kernel, lay),
        out_shape=(
            jax.ShapeDtypeStruct((T, M), BF16),
            jax.ShapeDtypeStruct((T, M), BF16),
            jax.ShapeDtypeStruct((8, W), F32),
            jax.ShapeDtypeStruct((lay.arows, W), F32),
            jax.ShapeDtypeStruct((3, frows, W), F32),
        ),
        in_specs=[vmem] * 7,
        out_specs=(vmem,) * 5,
        scratch_shapes=scratch,
        compiler_params=pltpu.CompilerParams(collective_id=0, has_side_effects=True, vmem_limit_bytes=62 * 2**20),
        name="whole_layer",
    )(a_shard, f_shard, tokens, cotangent, gains, seg_ids, parents)


def body(lay, tokens, cotangent, seg_ids, parents, norm1_gain, w_query, key_value_weight, w_out, norm2_gain, w_gate, w_up, w_down):
    W = lay.width
    a_shard = jnp.concatenate(
        [
            jnp.transpose(w_query, (1, 2, 0)).reshape(lay.qrows, W),
            jnp.transpose(key_value_weight[:, 0, :]),
            jnp.zeros((lay.out_at - lay.kv_at - lay.kvrows, W), BF16),
            w_out.reshape(lay.qrows, W),
            jnp.zeros((lay.arows - lay.out_at - lay.qrows, W), BF16),
        ],
        axis=0,
    )
    f_shard = jnp.stack([w_gate.T, w_up.T, w_down], axis=0)
    gains = jnp.concatenate([norm1_gain[None], norm2_gain[None], jnp.zeros((6, W), F32)], axis=0)
    layer_out, in_grad, gain_sum, a_out, f_out = whole_layer(
        lay, a_shard, f_shard, tokens, cotangent, gains, seg_ids, parents
    )
    heads = QUERY_HEADS // lay.cores
    shape = (heads, HEAD_SIZE // lay.dp, W)
    query_grad = jnp.transpose(a_out[: lay.qrows].reshape(shape), (2, 0, 1))
    keyval_grad = jnp.transpose(a_out[lay.kv_at : lay.kv_at + lay.kvrows])[:, None, :]
    out_grad = a_out[lay.out_at : lay.out_at + lay.qrows].reshape(shape)
    return (
        layer_out,
        in_grad,
        gain_sum[0],
        query_grad,
        keyval_grad,
        out_grad,
        gain_sum[1],
        f_out[0].T,
        f_out[1].T,
        f_out[2],
    )


def general_layout(segment, parent):
    labels = jnp.arange(SEGS, dtype=jnp.int32)
    member = (segment[:, None] == labels[None, :]).astype(jnp.float32)
    link = ((parent[:, None] == labels[None, :]) & (labels[:, None] > 0)).astype(jnp.float32)
    ident = jnp.eye(SEGS, dtype=jnp.float32)

    def climb(level, reach):
        return ident + jnp.dot(link, reach, precision=lax.Precision.HIGHEST)

    reach = lax.fori_loop(0, SEGS, climb, ident)
    visible = jnp.dot(jnp.dot(member, reach, precision=lax.Precision.HIGHEST), member.T, precision=lax.Precision.HIGHEST) > 0.5
    places = jnp.arange(segment.shape[0], dtype=jnp.int32)
    allowed = visible & (places[:, None] >= places[None, :])
    sizes = jnp.sum(member, axis=0)
    earlier = (labels[None, :] < labels[:, None]).astype(jnp.float32)
    starts = jnp.dot(earlier, sizes, precision=lax.Precision.HIGHEST)
    above = jnp.dot(reach, sizes, precision=lax.Precision.HIGHEST) - sizes
    tree_depth = places.astype(jnp.float32) + jnp.dot(member, above - starts, precision=lax.Precision.HIGHEST)
    return (allowed, tree_depth)


def general_rotate(value_rows, tree_depth, sign):
    half = value_rows.shape[-1] // 2
    freqs = jnp.arange(half, dtype=jnp.float32) * (2.0 / value_rows.shape[-1])
    inverse = jnp.exp(freqs * -math.log(THETA))
    angle = tree_depth[:, None] * inverse[None, :]
    cosine = jnp.cos(angle)[:, None, :]
    sine = sign * jnp.sin(angle)[:, None, :]
    first = value_rows[..., :half]
    second = value_rows[..., half:]
    return jnp.concatenate(
        [first * cosine - second * sine, second * cosine + first * sine], axis=-1
    )


def product(left, right):
    return jnp.dot(left, right, preferred_element_type=jnp.float32)


def general_body(
    tokens,
    cotangent,
    seg_ids,
    parents,
    norm1_gain,
    w_query,
    key_value_weight,
    w_out,
    norm2_gain,
    w_gate,
    w_up,
    w_down,
):
    columns = lax.axis_size("col")
    row_index = lax.axis_index("row")
    col_index = lax.axis_index("col")
    feature_width = MODEL_WIDTH // columns
    half_rows = columns * TREE_TOKENS // 2
    heads_here = QUERY_HEADS // 2
    query_total_width = heads_here * HEAD_SIZE
    heads_per_group = QUERY_HEADS // KEY_VALUE_HEADS
    scale = HEAD_SIZE ** (-0.5)
    stream_rows, cot_rows = (
        lax.all_to_all(tokens, "col", split_axis=1, concat_axis=0, tiled=True),
        lax.all_to_all(cotangent, "col", split_axis=1, concat_axis=0, tiled=True),
    )

    def col_total(value_rows):
        return lax.psum(value_rows, "col")

    def gather_rows(value_rows):
        return lax.all_gather(value_rows, "row", axis=0, tiled=True)

    def gather_cols(value_rows):
        return lax.all_gather(value_rows, "col", axis=0, tiled=True)

    def col_reduce(term, rows):
        return lax.psum_scatter(
            term(jnp.int32(0), rows * lax.axis_size("col")), "col", scatter_dimension=0, tiled=True
        )

    def row_reduce(term, rows):
        return lax.psum_scatter(
            term(jnp.int32(0), rows * lax.axis_size("row")), "row", scatter_dimension=0, tiled=True
        )

    def fetch():
        blocks = (
            lax.all_gather(w_query, "dp", axis=2, tiled=True),
            lax.all_gather(key_value_weight, "dp", axis=2, tiled=True),
            lax.all_gather(w_out, "dp", axis=1, tiled=True),
            lax.all_gather(w_gate, "dp", axis=1, tiled=True),
            lax.all_gather(w_up, "dp", axis=1, tiled=True),
            lax.all_gather(w_down, "dp", axis=0, tiled=True),
        )
        wide = None
        return (blocks, wide)

    def local_heads(pair_part):
        spread_heads = jnp.repeat(pair_part, heads_per_group, axis=1)
        return lax.dynamic_slice_in_dim(spread_heads, row_index * heads_here, heads_here, 1)

    def fold_heads(grad_here):
        spread_heads = jnp.zeros((TREE_TOKENS, QUERY_HEADS, HEAD_SIZE), jnp.float32)
        spread_heads = lax.dynamic_update_slice_in_dim(
            spread_heads, grad_here, row_index * heads_here, 1
        )
        return jnp.sum(
            spread_heads.reshape(TREE_TOKENS, KEY_VALUE_HEADS, heads_per_group, HEAD_SIZE), axis=2
        )

    gradients = (
        jnp.zeros((feature_width,), jnp.float32),
        jnp.zeros((feature_width, heads_here, HEAD_SIZE), jnp.float32),
        jnp.zeros((feature_width, 1, KEY_VALUE_HEADS * HEAD_SIZE), jnp.float32),
        jnp.zeros((heads_here, HEAD_SIZE, feature_width), jnp.float32),
        jnp.zeros((feature_width,), jnp.float32),
        jnp.zeros((feature_width, w_gate.shape[1] * lax.axis_size("dp")), jnp.float32),
        jnp.zeros((feature_width, w_up.shape[1] * lax.axis_size("dp")), jnp.float32),
        jnp.zeros((w_down.shape[0] * lax.axis_size("dp"), feature_width), jnp.float32),
    )
    results = []
    input_grads = []
    for batch_index in range(2):
        blocks, wide = fetch()
        (
            forward_query_block,
            forward_key_value_block,
            forward_out_block,
            forward_gate_block,
            forward_up_block,
            forward_down_block,
        ) = blocks
        forward_query_matrix = forward_query_block.reshape(feature_width, query_total_width)
        forward_key_value_matrix = forward_key_value_block.reshape(
            feature_width, KEY_VALUE_HEADS * HEAD_SIZE
        )
        forward_out_matrix = forward_out_block.reshape(query_total_width, feature_width)
        forward_stream = lax.dynamic_slice_in_dim(
            stream_rows, batch_index * half_rows, half_rows, 0
        ).astype(jnp.float32)
        forward_rstd1 = lax.rsqrt(
            col_total(jnp.sum(forward_stream * forward_stream, axis=1)) / MODEL_WIDTH + EPS
        )
        normed = (forward_stream * forward_rstd1[:, None] * norm1_gain).astype(jnp.bfloat16)
        forward_normed_all = gather_rows(normed)

        def qkv_term(start, count):
            return jnp.concatenate(
                [
                    product(forward_normed_all, forward_query_matrix),
                    product(forward_normed_all, forward_key_value_matrix),
                ],
                axis=1,
            )

        projected_rows = col_reduce(qkv_term, TREE_TOKENS)
        half_cols = columns // 2
        tree_slot = (
            col_index // half_cols * (2 * half_cols)
            + batch_index * half_cols
            + col_index % half_cols
        )
        segment = lax.dynamic_index_in_dim(seg_ids, tree_slot, 0, keepdims=False)
        parent = lax.dynamic_index_in_dim(parents, tree_slot, 0, keepdims=False)
        forward_allowed, forward_tree_depth = general_layout(segment, parent)
        query_pre = projected_rows[:, :query_total_width].reshape(
            TREE_TOKENS, heads_here, HEAD_SIZE
        )
        forward_query = general_rotate(query_pre, forward_tree_depth, 1.0).astype(jnp.bfloat16)
        own_unrotated = projected_rows[:, query_total_width:].reshape(
            TREE_TOKENS, KEY_VALUE_HEADS, HEAD_SIZE
        )
        own_part = jnp.where(
            row_index == 0, general_rotate(own_unrotated, forward_tree_depth, 1.0), own_unrotated
        ).astype(jnp.bfloat16)
        forward_pair = lax.all_gather(own_part[:, None], "row", axis=1, tiled=True)
        forward_keys_here = local_heads(forward_pair[:, 0])
        forward_values_here = local_heads(forward_pair[:, 1])
        forward_scores = (
            jnp.einsum(
                "qhd,khd->hqk", forward_query, forward_keys_here, preferred_element_type=jnp.float32
            )
            * scale
        )
        forward_masked = jnp.where(forward_allowed[None], forward_scores, -1e30)
        row_max = jnp.max(forward_masked, axis=-1, keepdims=True)
        forward_total = (
            jnp.log(jnp.sum(jnp.exp(forward_masked - row_max), axis=-1, keepdims=True)) + row_max
        )
        probs = jnp.exp(forward_masked - forward_total).astype(jnp.bfloat16)
        mixed = jnp.einsum(
            "hqk,khd->qhd", probs, forward_values_here, preferred_element_type=jnp.float32
        )
        mixed = mixed.astype(jnp.bfloat16).reshape(TREE_TOKENS, query_total_width)
        forward_mixed_all = gather_cols(mixed)

        def out_term(start, count):
            return product(forward_mixed_all, forward_out_matrix)

        forward_resid = forward_stream + row_reduce(out_term, half_rows)
        forward_rstd2 = lax.rsqrt(
            col_total(jnp.sum(forward_resid * forward_resid, axis=1)) / MODEL_WIDTH + EPS
        )
        normed2 = (forward_resid * forward_rstd2[:, None] * norm2_gain).astype(jnp.bfloat16)
        normed2_all = gather_rows(normed2)
        forward_hidden_here = forward_gate_block.shape[1]

        def gate_term(start, count):
            return jnp.concatenate(
                [product(normed2_all, forward_gate_block), product(normed2_all, forward_up_block)],
                axis=1,
            )

        gate_up = col_reduce(gate_term, TREE_TOKENS)
        forward_gate = gate_up[:, :forward_hidden_here]
        forward_up_part = gate_up[:, forward_hidden_here:]
        hidden = (jax.nn.silu(forward_gate) * forward_up_part).astype(jnp.bfloat16)
        forward_hidden_all = gather_cols(hidden)

        def down_term(start, count):
            return product(forward_hidden_all, forward_down_block)

        result = (forward_resid + row_reduce(down_term, half_rows)).astype(jnp.bfloat16)
        forward_saved = (
            forward_stream,
            forward_rstd1,
            forward_normed_all,
            forward_query,
            forward_pair,
            forward_total,
            forward_allowed,
            forward_tree_depth,
            forward_mixed_all,
            forward_resid,
            forward_rstd2,
            normed2_all,
            forward_gate,
            forward_up_part,
            forward_hidden_all,
        )
        result, saved = (result, forward_saved)
        blocks, wide = fetch()
        backward_gradients = gradients
        query_block, key_value_block, out_block, gate_block, up_block, down_block = blocks
        (
            stream,
            rstd1,
            normed_all,
            query,
            pair,
            total,
            allowed,
            tree_depth,
            mixed_all,
            resid,
            rstd2,
            kept_features,
            gate,
            up_part,
            hidden_all,
        ) = saved
        query_matrix = query_block.reshape(feature_width, query_total_width)
        key_value_matrix = key_value_block.reshape(feature_width, KEY_VALUE_HEADS * HEAD_SIZE)
        out_matrix = out_block.reshape(query_total_width, feature_width)
        hidden_here = gate_block.shape[1]
        cot_low = lax.dynamic_slice_in_dim(cot_rows, batch_index * half_rows, half_rows, 0)
        cot_full = cot_low.astype(jnp.float32)
        cot_all = gather_rows(cot_low)
        down_grad = jnp.einsum("tf,td->fd", hidden_all, cot_all, preferred_element_type=jnp.float32)

        def hidden_term(start, count):
            return jnp.einsum("td,fd->tf", cot_all, down_block, preferred_element_type=jnp.float32)

        d_hidden = col_reduce(hidden_term, TREE_TOKENS)
        sigmoid_gate = jax.nn.sigmoid(gate)
        d_up = (d_hidden * gate * sigmoid_gate).astype(jnp.bfloat16)
        d_gate = (d_hidden * up_part * sigmoid_gate * (1.0 + gate * (1.0 - sigmoid_gate))).astype(
            jnp.bfloat16
        )
        d_both = gather_cols(jnp.concatenate([d_gate, d_up], axis=1))
        gate_grad = jnp.einsum(
            "td,tf->df", kept_features, d_both[:, :hidden_here], preferred_element_type=jnp.float32
        )
        up_grad = jnp.einsum(
            "td,tf->df", kept_features, d_both[:, hidden_here:], preferred_element_type=jnp.float32
        )

        def back2_term(start, count):
            first = jnp.einsum(
                "tf,df->td", d_both[:, :hidden_here], gate_block, preferred_element_type=jnp.float32
            )
            return first + jnp.einsum(
                "tf,df->td", d_both[:, hidden_here:], up_block, preferred_element_type=jnp.float32
            )

        d_normed2 = row_reduce(back2_term, half_rows)
        scaled2 = d_normed2 * norm2_gain
        gain2_grad = jnp.sum(d_normed2 * resid * rstd2[:, None], axis=0)
        inner2 = col_total(jnp.sum(scaled2 * resid, axis=1))
        d_resid = (
            cot_full
            + rstd2[:, None] * scaled2
            - resid * (rstd2 * rstd2 * rstd2 * inner2 / MODEL_WIDTH)[:, None]
        )
        d_attn_all = gather_rows(d_resid.astype(jnp.bfloat16))
        out_grad = jnp.einsum(
            "tq,td->qd", mixed_all, d_attn_all, preferred_element_type=jnp.float32
        )

        def mixed_term(start, count):
            return jnp.einsum(
                "td,qd->tq", d_attn_all, out_matrix, preferred_element_type=jnp.float32
            )

        d_mixed = (
            col_reduce(mixed_term, TREE_TOKENS)
            .astype(jnp.bfloat16)
            .reshape(TREE_TOKENS, heads_here, HEAD_SIZE)
        )
        keys_here = local_heads(pair[:, 0])
        values_here = local_heads(pair[:, 1])
        scores = (
            jnp.einsum("qhd,khd->hqk", query, keys_here, preferred_element_type=jnp.float32) * scale
        )
        masked = jnp.where(allowed[None], scores, -1e30)
        probs_full = jnp.exp(masked - total)
        probs_low = probs_full.astype(jnp.bfloat16)
        d_probs = jnp.einsum(
            "qhd,khd->hqk", d_mixed, values_here, preferred_element_type=jnp.float32
        )
        delta = jnp.sum(probs_full * d_probs, axis=-1, keepdims=True)
        d_scores = (probs_full * (d_probs - delta)).astype(jnp.bfloat16)
        d_query = (
            jnp.einsum("hqk,khd->qhd", d_scores, keys_here, preferred_element_type=jnp.float32)
            * scale
        )
        d_keys = (
            jnp.einsum("hqk,qhd->khd", d_scores, query, preferred_element_type=jnp.float32) * scale
        )
        d_values = jnp.einsum(
            "hqk,qhd->khd", probs_low, d_mixed, preferred_element_type=jnp.float32
        )
        d_pair = jnp.stack([fold_heads(d_keys), fold_heads(d_values)], axis=1)
        own_gradient = lax.psum_scatter(
            d_pair.astype(jnp.bfloat16), "row", scatter_dimension=1, tiled=True
        ).astype(jnp.float32)[:, 0]
        own_gradient = jnp.where(
            row_index == 0, general_rotate(own_gradient, tree_depth, -1.0), own_gradient
        )
        query_pre_gradient = general_rotate(d_query, tree_depth, -1.0)
        d_proj = jnp.concatenate(
            [
                query_pre_gradient.reshape(TREE_TOKENS, query_total_width),
                own_gradient.reshape(TREE_TOKENS, KEY_VALUE_HEADS * HEAD_SIZE),
            ],
            axis=1,
        ).astype(jnp.bfloat16)
        d_proj_all = gather_cols(d_proj)
        query_grad = jnp.einsum(
            "td,tq->dq",
            normed_all,
            d_proj_all[:, :query_total_width],
            preferred_element_type=jnp.float32,
        )
        keyval_grad = jnp.einsum(
            "td,tq->dq",
            normed_all,
            d_proj_all[:, query_total_width:],
            preferred_element_type=jnp.float32,
        )
        in_matrix = jnp.concatenate([query_matrix, key_value_matrix], axis=1)

        def back1_term(start, count):
            return jnp.einsum(
                "tq,dq->td", d_proj_all, in_matrix, preferred_element_type=jnp.float32
            )

        d_normed = row_reduce(back1_term, half_rows)
        scaled1 = d_normed * norm1_gain
        gain1_grad = jnp.sum(d_normed * stream * rstd1[:, None], axis=0)
        inner1 = col_total(jnp.sum(scaled1 * stream, axis=1))
        d_stream = (
            d_resid
            + rstd1[:, None] * scaled1
            - stream * (rstd1 * rstd1 * rstd1 * inner1 / MODEL_WIDTH)[:, None]
        )
        updates = (
            gain1_grad,
            query_grad.reshape(query_block.shape),
            keyval_grad.reshape(key_value_block.shape),
            out_grad.reshape(out_block.shape),
            gain2_grad,
            gate_grad,
            up_grad,
            down_grad,
        )
        backward_gradients = tuple((a + b for a, b in zip(backward_gradients, updates)))
        d_stream, gradients = (d_stream.astype(jnp.bfloat16), backward_gradients)
        results.append(result)
        input_grads.append(d_stream)
    shards = (
        lax.psum_scatter(
            gradients[1].astype(jnp.bfloat16), "dp", scatter_dimension=2, tiled=True
        ).astype(jnp.float32),
        lax.psum_scatter(
            gradients[2].astype(jnp.bfloat16), "dp", scatter_dimension=2, tiled=True
        ).astype(jnp.float32),
        lax.psum_scatter(
            gradients[3].astype(jnp.bfloat16), "dp", scatter_dimension=1, tiled=True
        ).astype(jnp.float32),
        lax.psum_scatter(
            gradients[5].astype(jnp.bfloat16), "dp", scatter_dimension=1, tiled=True
        ).astype(jnp.float32),
        lax.psum_scatter(
            gradients[6].astype(jnp.bfloat16), "dp", scatter_dimension=1, tiled=True
        ).astype(jnp.float32),
        lax.psum_scatter(
            gradients[7].astype(jnp.bfloat16), "dp", scatter_dimension=0, tiled=True
        ).astype(jnp.float32),
    )
    gains = lax.psum((gradients[0], gradients[4]), ("dp", "row"))
    final_out, final_grad = (
        lax.all_to_all(
            jnp.concatenate(results, axis=0), "col", split_axis=0, concat_axis=1, tiled=True
        ),
        lax.all_to_all(
            jnp.concatenate(input_grads, axis=0), "col", split_axis=0, concat_axis=1, tiled=True
        ),
    )
    return (
        final_out,
        final_grad,
        gains[0],
        shards[0],
        shards[1],
        shards[2],
        gains[1],
        shards[3],
        shards[4],
        shards[5],
    )


def solution(mesh):
    placed = (
        P(("dp", "row", "col"), None),
        P(("dp", "row", "col"), None),
        P("dp", None),
        P("dp", None),
        P("col"),
        P("col", "row", "dp"),
        P("col", "row", "dp"),
        P("row", "dp", "col"),
        P("col"),
        P("col", ("dp", "row")),
        P("col", ("dp", "row")),
        P(("dp", "row"), "col"),
    )
    lay = Layout(mesh.shape)
    work = functools.partial(body, lay) if lay.fits() else general_body
    return jax.shard_map(
        work,
        mesh=mesh,
        in_specs=placed,
        out_specs=(
            P(("dp", "row", "col"), None),
            P(("dp", "row", "col"), None),
            P("col"),
            P("col", "row", "dp"),
            P("col", "row", "dp"),
            P("row", "dp", "col"),
            P("col"),
            P("col", ("dp", "row")),
            P("col", ("dp", "row")),
            P(("dp", "row"), "col"),
        ),
        check_vma=False,
    )
```

```python
import functools
import math

import jax
import jax.numpy as jnp
from jax import lax
from jax.experimental import pallas as pl
from jax.experimental.pallas import tpu as pltpu
from jax.sharding import PartitionSpec as P

MODEL_WIDTH = 1280
QUERY_HEADS = 20
KEY_VALUE_HEADS = 5
HEAD_SIZE = 64
TREE_TOKENS = 128
SEGS = 13
PLANES = 4

EPS = 1e-05
THETA = 10000.0
MESH = pl.DeviceIdType.MESH
F32 = jnp.float32
BF16 = jnp.bfloat16


class Layout:
    def __init__(self, shape):
        self.planes = PLANES
        self.lines = shape["dp"] // PLANES
        self.cores = shape["row"]
        self.cols = shape["col"]
        self.dp = shape["dp"]
        self.width = MODEL_WIDTH // self.cols
        self.qrows = QUERY_HEADS // self.cores * (HEAD_SIZE // self.dp)
        self.kvrows = KEY_VALUE_HEADS * HEAD_SIZE // self.dp
        self.kv_at = self.qrows
        self.out_at = -(-(self.kv_at + self.kvrows) // 16) * 16
        self.arows = -(-(self.out_at + self.qrows) // 16) * 16
        self.parts = ((0, self.out_at), (self.out_at, self.arows - self.out_at))
        self.cuts = tuple(-(-(rows // 2) // 16) * 16 for _, rows in self.parts)

    def fits(self):
        return self.lines == 2 and self.cores == 2 and self.cols == 2 and self.dp == 2 * PLANES

    def here(self):
        dp = lax.axis_index("dp")
        return dp // self.lines, lax.rem(dp, self.lines), lax.axis_index("row"), lax.axis_index("col")

    def inner(self, z):
        return lax.rem((z + 1) // 2, 2)

    def line(self, z):
        half = z // 2
        return z, z + 1 - 2 * lax.rem(z, 2), 2 - half, 3 - 3 * half

    def device(self, z, x, r, c):
        return (z * self.lines + x, r, c)


def greet(lay, peers):
    barrier = pltpu.get_barrier_semaphore()
    for peer in peers:
        pl.semaphore_signal(barrier, inc=1, device_id=peer, device_id_type=MESH)
    pl.semaphore_wait(barrier, len(peers))


def dot_nt(left, right):
    return lax.dot_general(left, right, (((1,), (1,)), ((), ())), preferred_element_type=F32)


def dot_tn(left, right):
    return lax.dot_general(left, right, (((0,), (0,)), ((), ())), preferred_element_type=F32)


def dot_nn(left, right):
    return jnp.dot(left, right, preferred_element_type=F32)


class Line:
    def __init__(self, lay, links, source, slots, pos_1, pos_x):
        z, x, r, c = lay.here()
        self.inner = lay.inner(z)
        base = links.take(4)
        self.slots = slots
        peers = lay.line(z)
        self.side, self.near = lay.device(peers[1], x, r, c), lay.device(peers[2], x, r, c)

        def copy(src, dst, s, t, peer):
            return pltpu.make_async_remote_copy(
                src_ref=src,
                dst_ref=dst,
                send_sem=links.send_sems.at[base + s],
                recv_sem=links.recv_sems.at[base + t],
                device_id=peer,
                device_id_type=MESH,
            )

        self.first = copy(source, pos_1, 0, 0, self.side)
        self.cross = copy(source, pos_x, 1, 2 - self.inner, self.near)
        self.passed = {p: copy(slots(p), slots(p), p, p - 1, self.side) for p in (2, 3)}

    def start(self):
        self.first.start()
        self.cross.start()

    def relay(self, p):
        @pl.when(self.inner == 1)
        def _():
            self.passed[p].wait_recv()
            self.passed[p].start()

    def arrive(self, p):
        if p == 1:
            self.first.wait_recv()
            return

        @pl.when(self.inner == 0)
        def _():
            self.passed[p].wait_recv()

    def flush(self):
        self.first.wait_send()
        self.cross.wait_send()

        @pl.when(self.inner == 1)
        def _():
            self.passed[2].wait_send()
            self.passed[3].wait_send()


class LineSum:
    def __init__(self, lay, links, landing):
        z, x, r, c = lay.here()
        base = links.take(3)
        side, mirror = lay.device(lay.line(z)[1], x, r, c), lay.device(lay.planes - 1 - z, x, r, c)
        self.copy = lambda source, s: pltpu.make_async_remote_copy(
            src_ref=source,
            dst_ref=landing.at[s],
            send_sem=links.send_sems.at[base + s],
            recv_sem=links.recv_sems.at[base + s],
            device_id=mirror if s == 2 else side,
            device_id_type=MESH,
        )
        self.landing, self.used = landing, set()

    def send(self, s, source):
        self.used.add(s)
        self.copy(source, s).start()

    def arrive(self, s):
        self.copy(self.landing.at[s], s).wait_recv()

    def flush(self):
        for s in sorted(self.used):
            self.copy(self.landing.at[s], s).wait_send()


class Links:
    def __init__(self, send_sems, recv_sems):
        self.send_sems, self.recv_sems, self.used = send_sems, recv_sems, 0
        self.open = []

    def take(self, count):
        first = self.used
        self.used += count
        return first

    def send(self, src, dst, peer, source=None):
        at = self.take(1)
        copy = pltpu.make_async_remote_copy(
            src_ref=src,
            dst_ref=dst,
            send_sem=self.send_sems.at[at],
            recv_sem=self.recv_sems.at[at],
            device_id=peer,
            device_id_type=MESH,
        )
        copy.start()
        self.open.append((source, copy))
        return copy

    def flush(self, *sources):
        for source, copy in self.open:
            if not sources or source in sources:
                copy.wait_send()
        self.open = [o for o in self.open if sources and o[0] not in sources]


def turn(rows, cosine, sine):
    lanes = rows.shape[1]
    many = lanes // 128
    half = HEAD_SIZE // 2
    lane = lax.broadcasted_iota(jnp.int32, rows.shape, 1)
    swapped = jnp.where(
        lax.rem(lane, HEAD_SIZE) < half, pltpu.roll(rows, lanes - half, 1), pltpu.roll(rows, half, 1)
    )
    wide = lambda t: t if many == 1 else jnp.concatenate([t] * many, axis=1)
    return rows * wide(cosine) + swapped * wide(sine)


def stack_heads(rows, count):
    return jnp.concatenate([rows[:, i * HEAD_SIZE : (i + 1) * HEAD_SIZE] for i in range(count)], axis=0)


def spread_heads(rows, count):
    return jnp.concatenate([rows[i * TREE_TOKENS : (i + 1) * TREE_TOKENS] for i in range(count)], axis=1)


def add_into(dest, other, step):
    def some(i, _):
        rows = pl.ds(pl.multiple_of(i * step, step), step)
        dest[rows, :] = (dest[rows, :].astype(F32) + other[rows, :].astype(F32)).astype(dest.dtype)
        return 0

    lax.fori_loop(0, dest.shape[0] // step, some, 0)


def sum_into(dest, parts, step):
    def some(i, _):
        rows = pl.ds(pl.multiple_of(i * step, step), step)
        acc = parts[0][rows, :].astype(F32)
        for part in parts[1:]:
            acc = acc + part[rows, :].astype(F32)
        dest[rows, :] = acc.astype(dest.dtype)
        return 0

    lax.fori_loop(0, dest.shape[0] // step, some, 0)


def layer_kernel(
    lay,
    q_ref, kv_ref, o_ref, gate_ref, up_ref, down_ref, tok_ref, cot_ref, gain_ref, seg_ref, par_ref,
    out_hbm, in_grad_hbm, gain_out, q_hbm, kv_hbm, o_hbm, gate_hbm, up_hbm, down_hbm,
    ga, gf, wq, wkv, wo, gn, gdy, act, dgate, dup, d_act, gfull, normed, qs, ks, vs, probs, mix, resid,
    rot_cos, rot_sin, dq, dk5, dv5, d_part, d_in, y_part, y_in,
    fc_in, f1a, f1b, f2a, f2b, ac_in, a1a, a1b, a2, az_in, nsum, nin,
    out_ref, in_grad_ref, a_out, f_out,
    send_sems, recv_sems, own_sems, out_sems,
):
    z, x, r, c = lay.here()
    W, T, D = lay.width, TREE_TOKENS, HEAD_SIZE
    frows = gate_ref.shape[0]
    hid = lay.lines * lay.cores * frows
    groups = KEY_VALUE_HEADS
    per = QUERY_HEADS // KEY_VALUE_HEADS
    kvw = KEY_VALUE_HEADS * D
    scale = D**-0.5
    x_other, c_other, r_other = 1 - x, 1 - c, 1 - r
    x_peer = lay.device(z, x_other, r, c)
    y_peer = lay.device(z, x, r, c_other)
    sibling = lay.device(z, x, r_other, c)
    planes = lay.line(z)
    inner = lay.inner(z)
    line = range(lay.planes)
    lanes = lambda cc: pl.ds(pl.multiple_of(cc * W, 128), W)
    links = Links(send_sems, recv_sems)
    send = links.send
    outgoing = []

    def put(source, dest):
        copy = pltpu.make_async_copy(source, dest, out_sems.at[len(outgoing)])
        copy.start()
        outgoing.append(copy)

    def block(zz, xx, rr):
        return ga.at[zz * lay.lines + xx, rr]

    half = frows // 2
    halves = (pl.ds(0, half), pl.ds(half, half))
    weights = lambda w: gf[w].reshape(hid, MODEL_WIDTH)

    mine = block(z, x, r).at[:, lanes(c)]
    f_refs = (gate_ref, up_ref, down_ref)
    own = [
        pltpu.make_async_copy(q_ref, mine.at[pl.ds(0, lay.qrows), :], own_sems.at[0]),
        pltpu.make_async_copy(o_ref, mine.at[pl.ds(lay.out_at, lay.qrows), :], own_sems.at[1]),
        pltpu.make_async_copy(cot_ref, gdy.at[0], own_sems.at[2]),
    ]
    for w in range(3):
        own.append(pltpu.make_async_copy(f_refs[w], gf.at[w, x, r, :, lanes(c)], own_sems.at[3 + w]))
    for copy in own:
        copy.start()
    pad = jnp.zeros((lay.out_at - lay.kv_at - lay.kvrows, W), BF16)
    mine[lay.kv_at : lay.out_at, :] = jnp.concatenate([kv_ref[...], pad], axis=0)
    if lay.arows > lay.out_at + lay.qrows:
        mine[lay.out_at + lay.qrows :, :] = jnp.zeros((lay.arows - lay.out_at - lay.qrows, W), BF16)

    greet(lay, [lay.device(planes[p], x, r, c) for p in line[1:]] + [x_peer, y_peer, sibling])
    for copy in own[:2]:
        copy.wait()

    gfull[:, lanes(c)] = gain_ref[...]
    gain_y = send(gain_ref, gfull.at[:, lanes(c)], y_peer)
    ax, ay, arx, ary, acore = {}, {}, {}, {}, {}

    def a_rows(part, first=0, rows=None):
        at, many = lay.parts[part]
        return pl.ds(at + first, many if rows is None else rows)

    def a_here(part, zz):
        return block(zz, x, r).at[a_rows(part), lanes(c)]

    a_line = [
        Line(lay, links, a_here(i, z), lambda p, i=i: a_here(i, planes[p]), a_here(i, z), a_here(i, z)) for i in range(2)
    ]
    dy_line = Line(lay, links, gdy.at[0], lambda p: gdy.at[p], gdy.at[1], gdy.at[3 - inner])
    n_line = Line(lay, links, gn.at[0], lambda p: gn.at[p], gn.at[1], gn.at[3 - inner])
    d_line, y_line, n_sum = (LineSum(lay, links, landing) for landing in (d_in, y_in, nin.at[pl.ds(3, 3)]))
    g_line = [LineSum(lay, links, az_in.at[:, a_rows(i), :]) for i in range(2)]

    def a_own(i, k):
        if k:
            a_line[i].arrive(k)
        here = a_here(i, planes[k])
        ax[i, k] = send(here, here, x_peer, "ga")
        ay[i, k] = send(here, here, y_peer, "ga")

    def a_core(i, k, xx, j):
        rows = block(planes[k], xx, r).at[a_rows(i), :]
        acore[i, k, j] = send(rows, rows, sibling, "ga")

    def a_relay(i, k):
        ax[i, k].wait_recv()
        top = block(planes[k], x_other, r).at[a_rows(i, 0, lay.cuts[i]), lanes(c)]
        ary[i, k] = send(top, top, y_peer, "ga")
        ay[i, k].wait_recv()
        low = block(planes[k], x, r).at[a_rows(i, lay.cuts[i], lay.parts[i][1] - lay.cuts[i]), lanes(c_other)]
        arx[i, k] = send(low, low, x_peer, "ga")
        a_core(i, k, x, 0)

    def a_finish(i, k):
        ary[i, k].wait_recv()
        arx[i, k].wait_recv()
        a_core(i, k, x_other, 1)

    def a_unpack(i, k):
        acore[i, k, 0].wait_recv()
        acore[i, k, 1].wait_recv()
        zz = planes[k]
        heads = QUERY_HEADS // lay.cores
        dest = (wq, wo)[i]
        for rr in range(lay.cores):

            def pair(m, _):
                rows = pl.ds(pl.multiple_of(lay.parts[i][0] + m * 16, 16), 16)
                left = ga[zz * lay.lines, rr, rows, :].astype(F32)
                right = ga[zz * lay.lines + 1, rr, rows, :].astype(F32)
                at = (rr * heads + 2 * m) * D + zz * 16
                dest[pl.ds(pl.multiple_of(at, 16), 16), :] = jnp.concatenate([left[:8], right[:8]], axis=0).astype(BF16)
                dest[pl.ds(pl.multiple_of(at + D, 16), 16), :] = jnp.concatenate([left[8:], right[8:]], axis=0).astype(BF16)
                return 0

            lax.fori_loop(0, heads // 2, pair, 0)
            if i == 0:
                n = lay.kvrows
                left = ga[zz * lay.lines, rr, lay.kv_at : lay.out_at, :].astype(F32)
                right = ga[zz * lay.lines + 1, rr, lay.kv_at : lay.out_at, :].astype(F32)
                at = rr * kvw + zz * (2 * n)
                wkv[pl.ds(pl.multiple_of(at, 16), 2 * n), :] = jnp.concatenate([left[:n], right[:n]], axis=0).astype(BF16)

    a_own(0, 0)
    a_line[0].start()

    stream = tok_ref[...].astype(F32)
    rstd1 = lax.rsqrt(jnp.sum(stream * stream, axis=1, keepdims=True) / MODEL_WIDTH + EPS)
    tree = r * lay.cols + c
    seg_row = jnp.broadcast_to(seg_ref[pl.ds(tree, 1), :].astype(F32), (T, T))
    par_row = par_ref[pl.ds(tree, 1), :].astype(F32)
    seg_col = jnp.transpose(seg_row)
    above = jnp.zeros((T, T), F32)
    for s in range(par_ref.shape[1]):
        above = jnp.where(seg_col == s, par_row[:, s : s + 1], above)
    row_at = lax.broadcasted_iota(jnp.int32, (T, T), 0)
    lane_at = lax.broadcasted_iota(jnp.int32, (T, T), 1)
    seen = (seg_row == seg_col) | (seg_row == above) | (seg_row == 0.0)
    allowed = jnp.where(seen & (row_at >= lane_at), 1.0, 0.0)
    depth = jnp.sum(allowed, axis=1, keepdims=True) - 1.0
    freq = lax.rem(lane_at, D // 2).astype(F32) * (2.0 / D)
    angle = depth * jnp.exp(freq * -math.log(THETA))
    rot_cos[...] = jnp.cos(angle)
    sine = jnp.sin(angle)
    rot_sin[...] = jnp.where(lax.rem(lane_at, D) < D // 2, -sine, sine)
    for copy in own[2:]:
        copy.wait()
    gain_y.wait_recv()
    normed[...] = (stream * rstd1 * gfull[0:1, :]).astype(BF16)

    a_line[0].relay(2)
    a_own(0, 1)
    a_relay(0, 0)
    a_line[0].relay(3)
    a_line[1].start()
    a_finish(0, 0)
    a_relay(0, 1)
    a_own(0, 2)
    a_finish(0, 1)
    a_unpack(0, 0)
    a_own(0, 3)
    a_line[1].relay(2)
    a_relay(0, 2)
    a_own(1, 0)
    a_finish(0, 2)
    a_line[1].relay(3)
    dy_line.start()
    a_unpack(0, 1)
    a_own(1, 1)
    a_relay(0, 3)
    a_own(1, 2)
    a_unpack(0, 2)
    a_relay(1, 0)
    a_own(1, 3)
    a_finish(0, 3)
    a_unpack(0, 3)

    fx, fy, frx, fry, fcore = {}, {}, {}, {}, {}

    def f_send(w):
        here = gf.at[w, x, r, :, lanes(c)]
        fx[w] = send(here, here, x_peer, "gf")
        fy[w] = send(here, here, y_peer, "gf")

    def f_relay(w):
        fx[w].wait_recv()
        top = gf.at[w, x_other, r, halves[0], lanes(c)]
        fry[w] = send(top, top, y_peer, "gf")
        fy[w].wait_recv()
        low = gf.at[w, x, r, halves[1], lanes(c_other)]
        frx[w] = send(low, low, x_peer, "gf")
        fcore[w, 0] = send(gf.at[w, x, r], gf.at[w, x, r], sibling, "gf")

    def f_finish(w):
        fry[w].wait_recv()
        frx[w].wait_recv()
        fcore[w, 1] = send(gf.at[w, x_other, r], gf.at[w, x_other, r], sibling, "gf")

    def f_ready(w):
        fcore[w, 0].wait_recv()
        fcore[w, 1].wait_recv()

    kv = dot_nt(normed[...], wkv[...])
    turned = turn(kv, rot_cos[...], rot_sin[...])
    for g in range(groups):
        ks[g] = turned[:, g * D : (g + 1) * D].astype(BF16)
        vs[g] = kv[:, kvw + g * D : kvw + (g + 1) * D].astype(BF16)
    allowed4 = jnp.concatenate([allowed] * per, axis=0) > 0.5
    between = {
        0: [lambda: a_relay(1, 1)],
        1: [lambda: a_finish(1, 0)],
        2: [lambda: a_relay(1, 2), lambda: a_unpack(1, 0)],
        3: [lambda: a_finish(1, 1), lambda: dy_line.relay(2)],
        4: [lambda: a_relay(1, 3), lambda: [f_send(w) for w in (2, 0, 1)]],
    }
    for g in range(groups):
        cols = slice(g * per * D, (g + 1) * per * D)
        pre = turn(dot_nt(normed[...], wq[cols, :]), rot_cos[...], rot_sin[...])
        qs[g] = stack_heads(pre, per).astype(BF16)
        scores = jnp.where(allowed4, dot_nt(qs[g], ks[g]) * scale, -1e30)
        weight = jnp.exp(scores - jnp.max(scores, axis=1, keepdims=True))
        share = weight / jnp.sum(weight, axis=1, keepdims=True)
        probs[g] = share
        mixed = dot_nn(share.astype(BF16), vs[g])
        mix[:, cols] = spread_heads(mixed, per).astype(BF16)
        for step in between[g]:
            step()
    a_unpack(1, 1)
    a_finish(1, 2)
    a_unpack(1, 2)
    a_finish(1, 3)
    a_unpack(1, 3)
    res = stream + dot_nn(mix[...], wo[...])
    resid[...] = res
    rstd2 = lax.rsqrt(jnp.sum(res * res, axis=1, keepdims=True) / MODEL_WIDTH + EPS)
    gn[0] = (res * rstd2 * gfull[1:2, :]).astype(BF16)
    n_line.start()
    dy_line.relay(3)
    f_relay(2)
    f_relay(0)
    f_finish(2)
    n_line.relay(2)
    for p in line[1:]:
        dy_line.arrive(p)
    f_ready(2)
    n_rows = lay.planes * T
    dy_all = lambda: gdy[...].reshape(n_rows, MODEL_WIDTH)
    d_act[...] = dot_nt(dy_all(), weights(2))
    f_relay(1)
    f_finish(0)
    n_line.relay(3)
    f_ready(0)
    f_finish(1)
    f_ready(1)

    def feed(first, last):
        count = (last - first) * T
        rows = slice(first * T, last * T)
        n2 = gn[first:last].reshape(count, MODEL_WIDTH)
        gate = dot_nt(n2, weights(0))
        up = dot_nt(n2, weights(1))
        sig = 1.0 / (1.0 + jnp.exp(-gate))
        silu = gate * sig
        act[rows, :] = (silu * up).astype(BF16)
        da = d_act[rows, :]
        dup[rows, :] = (da * silu).astype(BF16)
        dgate[rows, :] = (da * up * sig * (1.0 + gate * (1.0 - sig))).astype(BF16)

    def back(first, last):
        count = (last - first) * T
        rows = slice(first * T, last * T)
        part = dot_nn(dgate[rows, :], weights(0)) + dot_nn(dup[rows, :], weights(1))
        d_part[first:last] = part.astype(BF16).reshape(last - first, T, MODEL_WIDTH)

    n_line.arrive(1)
    n_line.arrive(2)
    feed(1, 3)
    back(1, 3)

    @pl.when(inner == 0)
    def _():
        d_line.send(0, d_part.at[2])
        d_line.send(1, d_part.at[1])

    n_line.arrive(3)
    feed(3, 4)
    back(3, 4)

    @pl.when(inner == 1)
    def _():
        d_line.send(0, d_part.at[3])
        d_line.send(1, d_part.at[1])

    feed(0, 1)
    back(0, 1)

    def mirror(line_sum, terms, landing):
        line_sum.arrive(0)
        p = 3 - inner
        terms[p] = (terms[p].astype(F32) + landing[0].astype(F32)).astype(BF16)
        line_sum.send(2, terms.at[p])

    links.flush("ga", "gf")
    for part in a_line:
        part.flush()
    fc, fs1a, fs1b, fs2a, fs2b = {}, {}, {}, {}, {}

    def f_grad(w):
        n2 = gn[...].reshape(n_rows, MODEL_WIDTH)
        if w == 0:
            grad = dot_tn(dgate[...], n2)
        elif w == 1:
            grad = dot_tn(dup[...], n2)
        else:
            grad = dot_tn(act[...], dy_all())
        gf[w] = grad.astype(BF16).reshape(lay.lines, lay.cores, frows, MODEL_WIDTH)
        fc[w] = send(gf.at[w, :, r_other], fc_in.at[w], sibling)

    def f_stage1(w):
        fc[w].wait_recv()
        for xx in range(lay.lines):
            add_into(gf.at[w, xx, r], fc_in.at[w, xx], 32)
        fs1a[w] = send(gf.at[w, x_other, r, halves[0], :], f1a.at[w], x_peer)
        fs1b[w] = send(gf.at[w, :, r, halves[1], lanes(c_other)], f1b.at[w], y_peer)

    def f_stage2(w):
        fs1a[w].wait_recv()
        add_into(gf.at[w, x, r, halves[0], :], f1a.at[w], 16)
        fs2a[w] = send(gf.at[w, x, r, halves[0], lanes(c_other)], f2a.at[w], y_peer)
        fs1b[w].wait_recv()
        for xx in range(lay.lines):
            add_into(gf.at[w, xx, r, halves[1], lanes(c)], f1b.at[w, xx], 16)
        fs2b[w] = send(gf.at[w, x_other, r, halves[1], lanes(c)], f2b.at[w], x_peer)

    def f_total(w, dest):
        fs2a[w].wait_recv()
        sum_into(f_out.at[w, halves[0], :], [gf.at[w, x, r, halves[0], lanes(c)], f2a.at[w]], 16)
        fs2b[w].wait_recv()
        sum_into(f_out.at[w, halves[1], :], [gf.at[w, x, r, halves[1], lanes(c)], f2b.at[w]], 16)
        put(f_out.at[w], dest)

    f_grad(0)
    f_grad(1)
    f_stage1(0)
    mirror(d_line, d_part, d_in)
    y_all = dot_nn(act[...], weights(2))
    y_part[...] = y_all.astype(BF16).reshape(lay.planes, T, MODEL_WIDTH)
    y_line.send(0, y_part.at[2 + inner])
    y_line.send(1, y_part.at[1])
    f_grad(2)
    f_stage1(1)
    f_stage1(2)
    f_stage2(0)
    f_stage2(1)

    d_line.arrive(1)
    d_line.arrive(2)
    d_n2 = d_part[0].astype(F32) + d_in[1].astype(F32) + d_in[2].astype(F32)
    res = resid[...]
    rstd2 = lax.rsqrt(jnp.sum(res * res, axis=1, keepdims=True) / MODEL_WIDTH + EPS)
    gain2_grad = jnp.sum(d_n2 * res * rstd2, axis=0, keepdims=True)
    scaled2 = d_n2 * gfull[1:2, :]
    inner2 = jnp.sum(scaled2 * res, axis=1, keepdims=True)
    d_res = cot_ref[...].astype(F32) + rstd2 * scaled2 - res * (rstd2 * rstd2 * rstd2 * inner2 / MODEL_WIDTH)
    d_attn = d_res.astype(BF16)

    def place_heads(source, other, base):
        heads = QUERY_HEADS // lay.cores
        for rr in range(lay.cores):
            for m in range(heads // 2):
                at = (rr * heads + 2 * m) * D
                grad = dot_tn(source[:, at : at + 2 * D], other)
                for dp in range(lay.dp):
                    tile = jnp.concatenate([grad[dp * 8 : dp * 8 + 8], grad[D + dp * 8 : D + dp * 8 + 8]], axis=0)
                    ga[dp, rr, base + m * 16 : base + m * 16 + 16, :] = tile.astype(BF16)

    to_plane = (planes[2] + inner * (planes[3] - planes[2]), planes[3] + inner * (planes[2] - planes[3]), planes[1], z)
    ac, as1a, as1b, as2a, as2b = {}, {}, {}, {}, {}

    def a_pair(zz, rr, rows):
        return ga.at[pl.ds(zz * lay.lines, lay.lines), rr, rows]

    def a_core_sums(i):
        for t in line:
            ac[i, t] = send(a_pair(to_plane[t], r_other, a_rows(i)), ac_in.at[t, :, a_rows(i), :], sibling)

    def ends(i):
        return a_rows(i, 0, lay.cuts[i]), a_rows(i, lay.cuts[i], lay.parts[i][1] - lay.cuts[i])

    def a_stage1(i, t):
        top, low = ends(i)
        zz = to_plane[t]
        ac[i, t].wait_recv()
        for xx in range(lay.lines):
            add_into(block(zz, xx, r).at[a_rows(i), :], ac_in.at[t, xx, a_rows(i), :], 16)
        as1a[i, t] = send(block(zz, x_other, r).at[top, :], a1a.at[t, top, :], x_peer)
        as1b[i, t] = send(a_pair(zz, r, low).at[:, :, lanes(c_other)], a1b.at[t, :, low, :], y_peer)

    def a_stage2(i, t):
        top, low = ends(i)
        zz = to_plane[t]
        as1a[i, t].wait_recv()
        add_into(block(zz, x, r).at[top, :], a1a.at[t, top, :], 16)
        as2a[i, t] = send(block(zz, x, r).at[top, lanes(c_other)], a2.at[t, top, :], y_peer)
        as1b[i, t].wait_recv()
        for xx in range(lay.lines):
            add_into(block(zz, xx, r).at[low, lanes(c)], a1b.at[t, xx, low, :], 16)
        as2b[i, t] = send(block(zz, x_other, r).at[low, lanes(c)], a2.at[t, low, :], x_peer)

    def a_line_sum(i, t):
        here = a_here(i, to_plane[t])
        as2a[i, t].wait_recv()
        as2b[i, t].wait_recv()
        add_into(here, a2.at[t, a_rows(i), :], 16)
        if t == 1:
            g_line[i].arrive(0)
            add_into(here, az_in.at[0, a_rows(i), :], 16)
        if t < 3:
            g_line[i].send((0, 2, 1)[t], here)

    def a_total(i):
        g_line[i].arrive(1)
        g_line[i].arrive(2)
        parts = [a_here(i, z), az_in.at[1, a_rows(i), :], az_in.at[2, a_rows(i), :]]
        sum_into(a_out.at[a_rows(i), :], parts, 16)
        if i == 0:
            put(a_out.at[pl.ds(0, lay.qrows), :], q_hbm)
            put(a_out.at[pl.ds(lay.kv_at, lay.kvrows), :], kv_hbm)
        else:
            put(a_out.at[pl.ds(lay.out_at, lay.qrows), :], o_hbm)

    place_heads(mix, d_attn, lay.out_at)
    a_core_sums(1)
    f_stage2(2)
    between = {
        0: [lambda: a_stage1(1, 0), lambda: a_stage1(1, 1)],
        1: [lambda: a_stage1(1, 2), lambda: a_stage1(1, 3)],
        2: [lambda: mirror(y_line, y_part, y_in)],
        3: [lambda: a_stage2(1, 0)],
        4: [lambda: a_stage2(1, 1)],
    }
    for g in range(groups):
        cols = slice(g * per * D, (g + 1) * per * D)
        dms = stack_heads(dot_nt(d_attn, wo[cols, :]), per).astype(BF16)
        share = probs[g]
        dp_ = dot_nt(dms, vs[g])
        delta = jnp.sum(share * dp_, axis=1, keepdims=True)
        ds_ = (share * (dp_ - delta)).astype(BF16)
        d_query = spread_heads(dot_nn(ds_, ks[g]) * scale, per)
        dq[:, cols] = turn(d_query, rot_cos[...], -rot_sin[...]).astype(BF16)
        dk5[g] = dot_tn(ds_, qs[g]) * scale
        dv5[g] = dot_tn(share.astype(BF16), dms)
        for step in between[g]:
            step()
    zeros = jnp.zeros((T, D), F32)
    dk_all = jnp.concatenate([dk5[g] for g in range(groups)] + [zeros], axis=1)
    dk = turn(dk_all, rot_cos[...], -rot_sin[...])[:, :kvw].astype(BF16)
    dv = jnp.concatenate([dv5[g] for g in range(groups)], axis=1).astype(BF16)
    place_heads(dq, normed[...], 0)
    for rr, rows in enumerate((dk, dv)):
        grad = dot_tn(rows, normed[...])
        pad = jnp.zeros((lay.out_at - lay.kv_at - lay.kvrows, MODEL_WIDTH), F32)
        for dp in range(lay.dp):
            tile = jnp.concatenate([grad[dp * lay.kvrows : (dp + 1) * lay.kvrows], pad], axis=0)
            ga[dp, rr, lay.kv_at : lay.out_at, :] = tile.astype(BF16)
    a_core_sums(0)
    a_stage2(1, 2)
    a_stage2(1, 3)
    a_stage1(0, 0)
    a_line_sum(1, 0)
    a_stage1(0, 1)
    a_line_sum(1, 1)
    d_normed = dot_nn(dq[...], wq[...]) + dot_nn(dk, wkv[:kvw, :]) + dot_nn(dv, wkv[kvw:, :])
    a_stage2(0, 0)
    a_stage1(0, 2)
    a_line_sum(1, 2)
    stream = tok_ref[...].astype(F32)
    rstd1 = lax.rsqrt(jnp.sum(stream * stream, axis=1, keepdims=True) / MODEL_WIDTH + EPS)
    gain1_grad = jnp.sum(d_normed * stream * rstd1, axis=0, keepdims=True)
    nsum[0] = jnp.concatenate([gain1_grad, gain2_grad, jnp.zeros((6, MODEL_WIDTH), F32)], axis=0)
    g_core = send(nsum.at[0], nin.at[0], sibling)
    a_stage2(0, 1)
    a_stage1(0, 3)
    scaled1 = d_normed * gfull[0:1, :]
    inner1 = jnp.sum(scaled1 * stream, axis=1, keepdims=True)
    in_grad = d_res + rstd1 * scaled1 - stream * (rstd1 * rstd1 * rstd1 * inner1 / MODEL_WIDTH)
    in_grad_ref[...] = in_grad.astype(BF16)
    put(in_grad_ref, in_grad_hbm)
    a_line_sum(0, 0)
    a_stage2(0, 2)
    g_core.wait_recv()
    nsum[1] = nsum[0] + nin[0]
    g_x = send(nsum.at[1], nin.at[1], x_peer)
    a_line_sum(1, 3)
    y_line.arrive(1)
    y_line.arrive(2)
    y = resid[...] + y_part[0].astype(F32) + y_in[1].astype(F32) + y_in[2].astype(F32)
    out_ref[...] = y.astype(BF16)
    put(out_ref, out_hbm)
    a_line_sum(0, 1)
    a_stage2(0, 3)
    g_x.wait_recv()
    nsum[2] = nsum[1] + nin[1]
    g_y = send(nsum.at[2], nin.at[2], y_peer)
    f_total(0, gate_hbm)
    f_total(1, up_hbm)
    f_total(2, down_hbm)
    a_total(1)
    a_line_sum(0, 2)
    g_y.wait_recv()
    nsum[3] = nsum[2] + nin[2]
    n_sum.send(0, nsum.at[3])
    n_sum.arrive(0)
    nsum[4] = nsum[3] + nin[3]
    n_sum.send(2, nsum.at[4])
    n_sum.arrive(2)
    nsum[5] = nsum[4] + nin[5]
    gain_out[...] = nsum[5, :, lanes(c)]
    a_line_sum(0, 3)
    a_total(0)
    links.flush()
    for part in [dy_line, n_line, d_line, y_line, n_sum] + g_line:
        part.flush()
    for copy in outgoing:
        copy.wait()


def whole_layer(lay, blocks, tokens, cotangent, gains, seg_ids, parents):
    vm = lambda *shape: pltpu.VMEM(shape, BF16)
    vf = lambda *shape: pltpu.VMEM(shape, F32)
    M, T, D, W = MODEL_WIDTH, TREE_TOKENS, HEAD_SIZE, lay.width
    frows = blocks[3].shape[0]
    hid = lay.lines * lay.cores * frows
    G, per = KEY_VALUE_HEADS, QUERY_HEADS // KEY_VALUE_HEADS
    n, nl, half = lay.planes, lay.lines, frows // 2
    vmem, hbm = pl.BlockSpec(memory_space=pltpu.VMEM), pl.BlockSpec(memory_space=pl.ANY)
    count = 184
    scratch = [
        vm(lay.dp, lay.cores, lay.arows, M),
        vm(3, nl, lay.cores, frows, M),
        vm(QUERY_HEADS * D, M),
        vm(2 * G * D, M),
        vm(QUERY_HEADS * D, M),
        vm(n, T, M),
        vm(n, T, M),
        vm(n * T, hid),
        vm(n * T, hid),
        vm(n * T, hid),
        vf(n * T, hid),
        vf(8, M),
        vm(T, M),
        vm(G, per * T, D),
        vm(G, T, D),
        vm(G, T, D),
        vf(G, per * T, T),
        vm(T, M),
        vf(T, M),
        vf(T, T),
        vf(T, T),
        vm(T, M),
        vf(G, T, D),
        vf(G, T, D),
        vm(n, T, M),
        vm(n - 1, T, M),
        vm(n, T, M),
        vm(n - 1, T, M),
        vm(3, nl, frows, M),
        vm(3, half, M),
        vm(3, nl, half, W),
        vm(3, half, W),
        vm(3, half, W),
        vm(n, nl, lay.arows, M),
        vm(n, lay.arows, M),
        vm(n, nl, lay.arows, W),
        vm(n, lay.arows, W),
        vm(n - 1, lay.arows, W),
        vf(6, 8, M),
        vf(2 + n, 8, M),
        vm(T, M),
        vm(T, M),
        vf(lay.arows, W),
        vf(3, frows, W),
        pltpu.SemaphoreType.DMA((count,)),
        pltpu.SemaphoreType.DMA((count,)),
        pltpu.SemaphoreType.DMA((6,)),
        pltpu.SemaphoreType.DMA((8,)),
    ]
    return pl.pallas_call(
        functools.partial(layer_kernel, lay),
        out_shape=(
            jax.ShapeDtypeStruct((T, M), BF16),
            jax.ShapeDtypeStruct((T, M), BF16),
            jax.ShapeDtypeStruct((8, W), F32),
        )
        + tuple(jax.ShapeDtypeStruct(b.shape, F32) for b in blocks),
        in_specs=[hbm, vmem, hbm, hbm, hbm, hbm, vmem, vmem, vmem, vmem, vmem],
        out_specs=(hbm, hbm, vmem) + (hbm,) * 6,
        scratch_shapes=scratch,
        compiler_params=pltpu.CompilerParams(collective_id=0, has_side_effects=True, vmem_limit_bytes=62 * 2**20),
        name="whole_layer",
    )(*blocks, tokens, cotangent, gains, seg_ids, parents)


def finish_kernel(count, *refs):
    held, (into, back) = refs[2 * count : 3 * count], refs[3 * count :]
    first = [pltpu.make_async_copy(refs[i], held[i], into.at[i]) for i in range(count)]
    last = [pltpu.make_async_copy(held[i], refs[count + i], back.at[i]) for i in range(count)]
    for copy in first:
        copy.start()
    for i in range(count):
        first[i].wait()
        last[i].start()
    for copy in last:
        copy.wait()


def finish(results):
    hbm = pl.BlockSpec(memory_space=pl.ANY)
    count = len(results)
    dma = pltpu.SemaphoreType.DMA((count,))
    return pl.pallas_call(
        functools.partial(finish_kernel, count),
        out_shape=tuple(jax.ShapeDtypeStruct(v.shape, v.dtype) for v in results),
        in_specs=[hbm] * count,
        out_specs=(hbm,) * count,
        scratch_shapes=[pltpu.VMEM(v.shape, v.dtype) for v in results] + [dma, dma],
        name="finish",
    )(*results)


def body(lay, tokens, cotangent, seg_ids, parents, norm1_gain, w_query, key_value_weight, w_out, norm2_gain, w_gate, w_up, w_down):
    W = lay.width
    blocks = (
        jnp.transpose(w_query, (1, 2, 0)).reshape(lay.qrows, W),
        jnp.transpose(key_value_weight[:, 0, :]),
        w_out.reshape(lay.qrows, W),
        w_gate.T,
        w_up.T,
        w_down,
    )
    gains = jnp.concatenate([norm1_gain[None], norm2_gain[None], jnp.zeros((6, W), F32)], axis=0)
    layer_out, in_grad, gain_sum, query, keyval, out, gate, up, down = whole_layer(
        lay, blocks, tokens, cotangent, gains, seg_ids, parents
    )
    layer_out, in_grad, query, keyval, out, gate, up, down = finish(
        (layer_out, in_grad, query, keyval, out, gate, up, down)
    )
    heads = QUERY_HEADS // lay.cores
    shape = (heads, HEAD_SIZE // lay.dp, W)
    return (
        layer_out,
        in_grad,
        gain_sum[0],
        jnp.transpose(query.reshape(shape), (2, 0, 1)),
        keyval.T[:, None, :],
        out.reshape(shape),
        gain_sum[1],
        gate.T,
        up.T,
        down,
    )


def general_layout(segment, parent):
    labels = jnp.arange(SEGS, dtype=jnp.int32)
    member = (segment[:, None] == labels[None, :]).astype(jnp.float32)
    link = ((parent[:, None] == labels[None, :]) & (labels[:, None] > 0)).astype(jnp.float32)
    ident = jnp.eye(SEGS, dtype=jnp.float32)

    def climb(level, reach):
        return ident + jnp.dot(link, reach, precision=lax.Precision.HIGHEST)

    reach = lax.fori_loop(0, SEGS, climb, ident)
    visible = jnp.dot(jnp.dot(member, reach, precision=lax.Precision.HIGHEST), member.T, precision=lax.Precision.HIGHEST) > 0.5
    places = jnp.arange(segment.shape[0], dtype=jnp.int32)
    allowed = visible & (places[:, None] >= places[None, :])
    sizes = jnp.sum(member, axis=0)
    earlier = (labels[None, :] < labels[:, None]).astype(jnp.float32)
    starts = jnp.dot(earlier, sizes, precision=lax.Precision.HIGHEST)
    above = jnp.dot(reach, sizes, precision=lax.Precision.HIGHEST) - sizes
    tree_depth = places.astype(jnp.float32) + jnp.dot(member, above - starts, precision=lax.Precision.HIGHEST)
    return (allowed, tree_depth)


def general_rotate(value_rows, tree_depth, sign):
    half = value_rows.shape[-1] // 2
    freqs = jnp.arange(half, dtype=jnp.float32) * (2.0 / value_rows.shape[-1])
    inverse = jnp.exp(freqs * -math.log(THETA))
    angle = tree_depth[:, None] * inverse[None, :]
    cosine = jnp.cos(angle)[:, None, :]
    sine = sign * jnp.sin(angle)[:, None, :]
    first = value_rows[..., :half]
    second = value_rows[..., half:]
    return jnp.concatenate(
        [first * cosine - second * sine, second * cosine + first * sine], axis=-1
    )


def product(left, right):
    return jnp.dot(left, right, preferred_element_type=jnp.float32)


def general_body(
    tokens,
    cotangent,
    seg_ids,
    parents,
    norm1_gain,
    w_query,
    key_value_weight,
    w_out,
    norm2_gain,
    w_gate,
    w_up,
    w_down,
):
    columns = lax.axis_size("col")
    row_index = lax.axis_index("row")
    col_index = lax.axis_index("col")
    feature_width = MODEL_WIDTH // columns
    half_rows = columns * TREE_TOKENS // 2
    heads_here = QUERY_HEADS // 2
    query_total_width = heads_here * HEAD_SIZE
    heads_per_group = QUERY_HEADS // KEY_VALUE_HEADS
    scale = HEAD_SIZE ** (-0.5)
    stream_rows, cot_rows = (
        lax.all_to_all(tokens, "col", split_axis=1, concat_axis=0, tiled=True),
        lax.all_to_all(cotangent, "col", split_axis=1, concat_axis=0, tiled=True),
    )

    def col_total(value_rows):
        return lax.psum(value_rows, "col")

    def gather_rows(value_rows):
        return lax.all_gather(value_rows, "row", axis=0, tiled=True)

    def gather_cols(value_rows):
        return lax.all_gather(value_rows, "col", axis=0, tiled=True)

    def col_reduce(term, rows):
        return lax.psum_scatter(
            term(jnp.int32(0), rows * lax.axis_size("col")), "col", scatter_dimension=0, tiled=True
        )

    def row_reduce(term, rows):
        return lax.psum_scatter(
            term(jnp.int32(0), rows * lax.axis_size("row")), "row", scatter_dimension=0, tiled=True
        )

    def fetch():
        blocks = (
            lax.all_gather(w_query, "dp", axis=2, tiled=True),
            lax.all_gather(key_value_weight, "dp", axis=2, tiled=True),
            lax.all_gather(w_out, "dp", axis=1, tiled=True),
            lax.all_gather(w_gate, "dp", axis=1, tiled=True),
            lax.all_gather(w_up, "dp", axis=1, tiled=True),
            lax.all_gather(w_down, "dp", axis=0, tiled=True),
        )
        wide = None
        return (blocks, wide)

    def local_heads(pair_part):
        spread_heads = jnp.repeat(pair_part, heads_per_group, axis=1)
        return lax.dynamic_slice_in_dim(spread_heads, row_index * heads_here, heads_here, 1)

    def fold_heads(grad_here):
        spread_heads = jnp.zeros((TREE_TOKENS, QUERY_HEADS, HEAD_SIZE), jnp.float32)
        spread_heads = lax.dynamic_update_slice_in_dim(
            spread_heads, grad_here, row_index * heads_here, 1
        )
        return jnp.sum(
            spread_heads.reshape(TREE_TOKENS, KEY_VALUE_HEADS, heads_per_group, HEAD_SIZE), axis=2
        )

    gradients = (
        jnp.zeros((feature_width,), jnp.float32),
        jnp.zeros((feature_width, heads_here, HEAD_SIZE), jnp.float32),
        jnp.zeros((feature_width, 1, KEY_VALUE_HEADS * HEAD_SIZE), jnp.float32),
        jnp.zeros((heads_here, HEAD_SIZE, feature_width), jnp.float32),
        jnp.zeros((feature_width,), jnp.float32),
        jnp.zeros((feature_width, w_gate.shape[1] * lax.axis_size("dp")), jnp.float32),
        jnp.zeros((feature_width, w_up.shape[1] * lax.axis_size("dp")), jnp.float32),
        jnp.zeros((w_down.shape[0] * lax.axis_size("dp"), feature_width), jnp.float32),
    )
    results = []
    input_grads = []
    for batch_index in range(2):
        blocks, wide = fetch()
        (
            forward_query_block,
            forward_key_value_block,
            forward_out_block,
            forward_gate_block,
            forward_up_block,
            forward_down_block,
        ) = blocks
        forward_query_matrix = forward_query_block.reshape(feature_width, query_total_width)
        forward_key_value_matrix = forward_key_value_block.reshape(
            feature_width, KEY_VALUE_HEADS * HEAD_SIZE
        )
        forward_out_matrix = forward_out_block.reshape(query_total_width, feature_width)
        forward_stream = lax.dynamic_slice_in_dim(
            stream_rows, batch_index * half_rows, half_rows, 0
        ).astype(jnp.float32)
        forward_rstd1 = lax.rsqrt(
            col_total(jnp.sum(forward_stream * forward_stream, axis=1)) / MODEL_WIDTH + EPS
        )
        normed = (forward_stream * forward_rstd1[:, None] * norm1_gain).astype(jnp.bfloat16)
        forward_normed_all = gather_rows(normed)

        def qkv_term(start, count):
            return jnp.concatenate(
                [
                    product(forward_normed_all, forward_query_matrix),
                    product(forward_normed_all, forward_key_value_matrix),
                ],
                axis=1,
            )

        projected_rows = col_reduce(qkv_term, TREE_TOKENS)
        half_cols = columns // 2
        tree_slot = (
            col_index // half_cols * (2 * half_cols)
            + batch_index * half_cols
            + col_index % half_cols
        )
        segment = lax.dynamic_index_in_dim(seg_ids, tree_slot, 0, keepdims=False)
        parent = lax.dynamic_index_in_dim(parents, tree_slot, 0, keepdims=False)
        forward_allowed, forward_tree_depth = general_layout(segment, parent)
        query_pre = projected_rows[:, :query_total_width].reshape(
            TREE_TOKENS, heads_here, HEAD_SIZE
        )
        forward_query = general_rotate(query_pre, forward_tree_depth, 1.0).astype(jnp.bfloat16)
        own_unrotated = projected_rows[:, query_total_width:].reshape(
            TREE_TOKENS, KEY_VALUE_HEADS, HEAD_SIZE
        )
        own_part = jnp.where(
            row_index == 0, general_rotate(own_unrotated, forward_tree_depth, 1.0), own_unrotated
        ).astype(jnp.bfloat16)
        forward_pair = lax.all_gather(own_part[:, None], "row", axis=1, tiled=True)
        forward_keys_here = local_heads(forward_pair[:, 0])
        forward_values_here = local_heads(forward_pair[:, 1])
        forward_scores = (
            jnp.einsum(
                "qhd,khd->hqk", forward_query, forward_keys_here, preferred_element_type=jnp.float32
            )
            * scale
        )
        forward_masked = jnp.where(forward_allowed[None], forward_scores, -1e30)
        row_max = jnp.max(forward_masked, axis=-1, keepdims=True)
        forward_total = (
            jnp.log(jnp.sum(jnp.exp(forward_masked - row_max), axis=-1, keepdims=True)) + row_max
        )
        probs = jnp.exp(forward_masked - forward_total).astype(jnp.bfloat16)
        mixed = jnp.einsum(
            "hqk,khd->qhd", probs, forward_values_here, preferred_element_type=jnp.float32
        )
        mixed = mixed.astype(jnp.bfloat16).reshape(TREE_TOKENS, query_total_width)
        forward_mixed_all = gather_cols(mixed)

        def out_term(start, count):
            return product(forward_mixed_all, forward_out_matrix)

        forward_resid = forward_stream + row_reduce(out_term, half_rows)
        forward_rstd2 = lax.rsqrt(
            col_total(jnp.sum(forward_resid * forward_resid, axis=1)) / MODEL_WIDTH + EPS
        )
        normed2 = (forward_resid * forward_rstd2[:, None] * norm2_gain).astype(jnp.bfloat16)
        normed2_all = gather_rows(normed2)
        forward_hidden_here = forward_gate_block.shape[1]

        def gate_term(start, count):
            return jnp.concatenate(
                [product(normed2_all, forward_gate_block), product(normed2_all, forward_up_block)],
                axis=1,
            )

        gate_up = col_reduce(gate_term, TREE_TOKENS)
        forward_gate = gate_up[:, :forward_hidden_here]
        forward_up_part = gate_up[:, forward_hidden_here:]
        hidden = (jax.nn.silu(forward_gate) * forward_up_part).astype(jnp.bfloat16)
        forward_hidden_all = gather_cols(hidden)

        def down_term(start, count):
            return product(forward_hidden_all, forward_down_block)

        result = (forward_resid + row_reduce(down_term, half_rows)).astype(jnp.bfloat16)
        forward_saved = (
            forward_stream,
            forward_rstd1,
            forward_normed_all,
            forward_query,
            forward_pair,
            forward_total,
            forward_allowed,
            forward_tree_depth,
            forward_mixed_all,
            forward_resid,
            forward_rstd2,
            normed2_all,
            forward_gate,
            forward_up_part,
            forward_hidden_all,
        )
        result, saved = (result, forward_saved)
        blocks, wide = fetch()
        backward_gradients = gradients
        query_block, key_value_block, out_block, gate_block, up_block, down_block = blocks
        (
            stream,
            rstd1,
            normed_all,
            query,
            pair,
            total,
            allowed,
            tree_depth,
            mixed_all,
            resid,
            rstd2,
            kept_features,
            gate,
            up_part,
            hidden_all,
        ) = saved
        query_matrix = query_block.reshape(feature_width, query_total_width)
        key_value_matrix = key_value_block.reshape(feature_width, KEY_VALUE_HEADS * HEAD_SIZE)
        out_matrix = out_block.reshape(query_total_width, feature_width)
        hidden_here = gate_block.shape[1]
        cot_low = lax.dynamic_slice_in_dim(cot_rows, batch_index * half_rows, half_rows, 0)
        cot_full = cot_low.astype(jnp.float32)
        cot_all = gather_rows(cot_low)
        down_grad = jnp.einsum("tf,td->fd", hidden_all, cot_all, preferred_element_type=jnp.float32)

        def hidden_term(start, count):
            return jnp.einsum("td,fd->tf", cot_all, down_block, preferred_element_type=jnp.float32)

        d_hidden = col_reduce(hidden_term, TREE_TOKENS)
        sigmoid_gate = jax.nn.sigmoid(gate)
        d_up = (d_hidden * gate * sigmoid_gate).astype(jnp.bfloat16)
        d_gate = (d_hidden * up_part * sigmoid_gate * (1.0 + gate * (1.0 - sigmoid_gate))).astype(
            jnp.bfloat16
        )
        d_both = gather_cols(jnp.concatenate([d_gate, d_up], axis=1))
        gate_grad = jnp.einsum(
            "td,tf->df", kept_features, d_both[:, :hidden_here], preferred_element_type=jnp.float32
        )
        up_grad = jnp.einsum(
            "td,tf->df", kept_features, d_both[:, hidden_here:], preferred_element_type=jnp.float32
        )

        def back2_term(start, count):
            first = jnp.einsum(
                "tf,df->td", d_both[:, :hidden_here], gate_block, preferred_element_type=jnp.float32
            )
            return first + jnp.einsum(
                "tf,df->td", d_both[:, hidden_here:], up_block, preferred_element_type=jnp.float32
            )

        d_normed2 = row_reduce(back2_term, half_rows)
        scaled2 = d_normed2 * norm2_gain
        gain2_grad = jnp.sum(d_normed2 * resid * rstd2[:, None], axis=0)
        inner2 = col_total(jnp.sum(scaled2 * resid, axis=1))
        d_resid = (
            cot_full
            + rstd2[:, None] * scaled2
            - resid * (rstd2 * rstd2 * rstd2 * inner2 / MODEL_WIDTH)[:, None]
        )
        d_attn_all = gather_rows(d_resid.astype(jnp.bfloat16))
        out_grad = jnp.einsum(
            "tq,td->qd", mixed_all, d_attn_all, preferred_element_type=jnp.float32
        )

        def mixed_term(start, count):
            return jnp.einsum(
                "td,qd->tq", d_attn_all, out_matrix, preferred_element_type=jnp.float32
            )

        d_mixed = (
            col_reduce(mixed_term, TREE_TOKENS)
            .astype(jnp.bfloat16)
            .reshape(TREE_TOKENS, heads_here, HEAD_SIZE)
        )
        keys_here = local_heads(pair[:, 0])
        values_here = local_heads(pair[:, 1])
        scores = (
            jnp.einsum("qhd,khd->hqk", query, keys_here, preferred_element_type=jnp.float32) * scale
        )
        masked = jnp.where(allowed[None], scores, -1e30)
        probs_full = jnp.exp(masked - total)
        probs_low = probs_full.astype(jnp.bfloat16)
        d_probs = jnp.einsum(
            "qhd,khd->hqk", d_mixed, values_here, preferred_element_type=jnp.float32
        )
        delta = jnp.sum(probs_full * d_probs, axis=-1, keepdims=True)
        d_scores = (probs_full * (d_probs - delta)).astype(jnp.bfloat16)
        d_query = (
            jnp.einsum("hqk,khd->qhd", d_scores, keys_here, preferred_element_type=jnp.float32)
            * scale
        )
        d_keys = (
            jnp.einsum("hqk,qhd->khd", d_scores, query, preferred_element_type=jnp.float32) * scale
        )
        d_values = jnp.einsum(
            "hqk,qhd->khd", probs_low, d_mixed, preferred_element_type=jnp.float32
        )
        d_pair = jnp.stack([fold_heads(d_keys), fold_heads(d_values)], axis=1)
        own_gradient = lax.psum_scatter(
            d_pair.astype(jnp.bfloat16), "row", scatter_dimension=1, tiled=True
        ).astype(jnp.float32)[:, 0]
        own_gradient = jnp.where(
            row_index == 0, general_rotate(own_gradient, tree_depth, -1.0), own_gradient
        )
        query_pre_gradient = general_rotate(d_query, tree_depth, -1.0)
        d_proj = jnp.concatenate(
            [
                query_pre_gradient.reshape(TREE_TOKENS, query_total_width),
                own_gradient.reshape(TREE_TOKENS, KEY_VALUE_HEADS * HEAD_SIZE),
            ],
            axis=1,
        ).astype(jnp.bfloat16)
        d_proj_all = gather_cols(d_proj)
        query_grad = jnp.einsum(
            "td,tq->dq",
            normed_all,
            d_proj_all[:, :query_total_width],
            preferred_element_type=jnp.float32,
        )
        keyval_grad = jnp.einsum(
            "td,tq->dq",
            normed_all,
            d_proj_all[:, query_total_width:],
            preferred_element_type=jnp.float32,
        )
        in_matrix = jnp.concatenate([query_matrix, key_value_matrix], axis=1)

        def back1_term(start, count):
            return jnp.einsum(
                "tq,dq->td", d_proj_all, in_matrix, preferred_element_type=jnp.float32
            )

        d_normed = row_reduce(back1_term, half_rows)
        scaled1 = d_normed * norm1_gain
        gain1_grad = jnp.sum(d_normed * stream * rstd1[:, None], axis=0)
        inner1 = col_total(jnp.sum(scaled1 * stream, axis=1))
        d_stream = (
            d_resid
            + rstd1[:, None] * scaled1
            - stream * (rstd1 * rstd1 * rstd1 * inner1 / MODEL_WIDTH)[:, None]
        )
        updates = (
            gain1_grad,
            query_grad.reshape(query_block.shape),
            keyval_grad.reshape(key_value_block.shape),
            out_grad.reshape(out_block.shape),
            gain2_grad,
            gate_grad,
            up_grad,
            down_grad,
        )
        backward_gradients = tuple((a + b for a, b in zip(backward_gradients, updates)))
        d_stream, gradients = (d_stream.astype(jnp.bfloat16), backward_gradients)
        results.append(result)
        input_grads.append(d_stream)
    shards = (
        lax.psum_scatter(
            gradients[1].astype(jnp.bfloat16), "dp", scatter_dimension=2, tiled=True
        ).astype(jnp.float32),
        lax.psum_scatter(
            gradients[2].astype(jnp.bfloat16), "dp", scatter_dimension=2, tiled=True
        ).astype(jnp.float32),
        lax.psum_scatter(
            gradients[3].astype(jnp.bfloat16), "dp", scatter_dimension=1, tiled=True
        ).astype(jnp.float32),
        lax.psum_scatter(
            gradients[5].astype(jnp.bfloat16), "dp", scatter_dimension=1, tiled=True
        ).astype(jnp.float32),
        lax.psum_scatter(
            gradients[6].astype(jnp.bfloat16), "dp", scatter_dimension=1, tiled=True
        ).astype(jnp.float32),
        lax.psum_scatter(
            gradients[7].astype(jnp.bfloat16), "dp", scatter_dimension=0, tiled=True
        ).astype(jnp.float32),
    )
    gains = lax.psum((gradients[0], gradients[4]), ("dp", "row"))
    final_out, final_grad = (
        lax.all_to_all(
            jnp.concatenate(results, axis=0), "col", split_axis=0, concat_axis=1, tiled=True
        ),
        lax.all_to_all(
            jnp.concatenate(input_grads, axis=0), "col", split_axis=0, concat_axis=1, tiled=True
        ),
    )
    return (
        final_out,
        final_grad,
        gains[0],
        shards[0],
        shards[1],
        shards[2],
        gains[1],
        shards[3],
        shards[4],
        shards[5],
    )


def solution(mesh):
    placed = (
        P(("dp", "row", "col"), None),
        P(("dp", "row", "col"), None),
        P("dp", None),
        P("dp", None),
        P("col"),
        P("col", "row", "dp"),
        P("col", "row", "dp"),
        P("row", "dp", "col"),
        P("col"),
        P("col", ("dp", "row")),
        P("col", ("dp", "row")),
        P(("dp", "row"), "col"),
    )
    lay = Layout(mesh.shape)
    work = functools.partial(body, lay) if lay.fits() else general_body
    return jax.shard_map(
        work,
        mesh=mesh,
        in_specs=placed,
        out_specs=(
            P(("dp", "row", "col"), None),
            P(("dp", "row", "col"), None),
            P("col"),
            P("col", "row", "dp"),
            P("col", "row", "dp"),
            P("row", "dp", "col"),
            P("col"),
            P("col", ("dp", "row")),
            P("col", ("dp", "row")),
            P(("dp", "row"), "col"),
        ),
        check_vma=False,
    )
```

```python
import functools
import math

import jax
import jax.numpy as jnp
from jax import lax
from jax.experimental import pallas as pl
from jax.experimental.pallas import tpu as pltpu
from jax.sharding import PartitionSpec as P

MODEL_WIDTH = 1280
QUERY_HEADS = 20
KEY_VALUE_HEADS = 5
HEAD_SIZE = 64
TREE_TOKENS = 128
SEGS = 13
PLANES = 4

EPS = 1e-05
THETA = 10000.0
MESH = pl.DeviceIdType.MESH
F32 = jnp.float32
BF16 = jnp.bfloat16


class Layout:
    def __init__(self, shape):
        self.planes = PLANES
        self.lines = shape["dp"] // PLANES
        self.cores = shape["row"]
        self.cols = shape["col"]
        self.dp = shape["dp"]
        self.width = MODEL_WIDTH // self.cols
        self.qrows = QUERY_HEADS // self.cores * (HEAD_SIZE // self.dp)
        self.kvrows = KEY_VALUE_HEADS * HEAD_SIZE // self.dp
        self.kv_at = self.qrows
        self.out_at = -(-(self.kv_at + self.kvrows) // 16) * 16
        self.arows = -(-(self.out_at + self.qrows) // 16) * 16
        self.parts = ((0, self.out_at), (self.out_at, self.arows - self.out_at))
        self.cuts = tuple(-(-(rows // 2) // 16) * 16 for _, rows in self.parts)

    def fits(self):
        return self.lines == 2 and self.cores == 2 and self.cols == 2 and self.dp == 2 * PLANES

    def here(self):
        dp = lax.axis_index("dp")
        return dp // self.lines, lax.rem(dp, self.lines), lax.axis_index("row"), lax.axis_index("col")

    def inner(self, z):
        return lax.rem((z + 1) // 2, 2)

    def line(self, z):
        half = z // 2
        return z, z + 1 - 2 * lax.rem(z, 2), 2 - half, 3 - 3 * half

    def device(self, z, x, r, c):
        return (z * self.lines + x, r, c)


def greet(lay, peers):
    barrier = pltpu.get_barrier_semaphore()
    for peer in peers:
        pl.semaphore_signal(barrier, inc=1, device_id=peer, device_id_type=MESH)
    pl.semaphore_wait(barrier, len(peers))


def dot_nt(left, right):
    return lax.dot_general(left, right, (((1,), (1,)), ((), ())), preferred_element_type=F32)


def dot_tn(left, right):
    return lax.dot_general(left, right, (((0,), (0,)), ((), ())), preferred_element_type=F32)


def dot_nn(left, right):
    return jnp.dot(left, right, preferred_element_type=F32)


class Line:
    def __init__(self, lay, links, source, slots, pos_1, pos_x):
        z, x, r, c = lay.here()
        self.inner = lay.inner(z)
        base = links.take(4)
        self.slots = slots
        peers = lay.line(z)
        self.side, self.near = lay.device(peers[1], x, r, c), lay.device(peers[2], x, r, c)

        def copy(src, dst, s, t, peer):
            return pltpu.make_async_remote_copy(
                src_ref=src,
                dst_ref=dst,
                send_sem=links.send_sems.at[base + s],
                recv_sem=links.recv_sems.at[base + t],
                device_id=peer,
                device_id_type=MESH,
            )

        self.first = copy(source, pos_1, 0, 0, self.side)
        self.cross = copy(source, pos_x, 1, 2 - self.inner, self.near)
        self.passed = {p: copy(slots(p), slots(p), p, p - 1, self.side) for p in (2, 3)}

    def start(self):
        self.first.start()
        self.cross.start()

    def relay(self, p):
        @pl.when(self.inner == 1)
        def _():
            self.passed[p].wait_recv()
            self.passed[p].start()

    def arrive(self, p):
        if p == 1:
            self.first.wait_recv()
            return

        @pl.when(self.inner == 0)
        def _():
            self.passed[p].wait_recv()

    def flush(self):
        self.first.wait_send()
        self.cross.wait_send()

        @pl.when(self.inner == 1)
        def _():
            self.passed[2].wait_send()
            self.passed[3].wait_send()


class LineSum:
    def __init__(self, lay, links, landing):
        z, x, r, c = lay.here()
        base = links.take(3)
        side, mirror = lay.device(lay.line(z)[1], x, r, c), lay.device(lay.planes - 1 - z, x, r, c)
        self.copy = lambda source, s: pltpu.make_async_remote_copy(
            src_ref=source,
            dst_ref=landing.at[s],
            send_sem=links.send_sems.at[base + s],
            recv_sem=links.recv_sems.at[base + s],
            device_id=mirror if s == 2 else side,
            device_id_type=MESH,
        )
        self.landing, self.used = landing, set()

    def send(self, s, source):
        self.used.add(s)
        self.copy(source, s).start()

    def arrive(self, s):
        self.copy(self.landing.at[s], s).wait_recv()

    def flush(self):
        for s in sorted(self.used):
            self.copy(self.landing.at[s], s).wait_send()


class Links:
    def __init__(self, send_sems, recv_sems):
        self.send_sems, self.recv_sems, self.used = send_sems, recv_sems, 0
        self.open = []

    def take(self, count):
        first = self.used
        self.used += count
        return first

    def send(self, src, dst, peer, source=None):
        at = self.take(1)
        copy = pltpu.make_async_remote_copy(
            src_ref=src,
            dst_ref=dst,
            send_sem=self.send_sems.at[at],
            recv_sem=self.recv_sems.at[at],
            device_id=peer,
            device_id_type=MESH,
        )
        copy.start()
        self.open.append((source, copy))
        return copy

    def flush(self, *sources):
        for source, copy in self.open:
            if not sources or source in sources:
                copy.wait_send()
        self.open = [o for o in self.open if sources and o[0] not in sources]


def turn(rows, cosine, sine):
    lanes = rows.shape[1]
    many = lanes // 128
    half = HEAD_SIZE // 2
    lane = lax.broadcasted_iota(jnp.int32, rows.shape, 1)
    swapped = jnp.where(
        lax.rem(lane, HEAD_SIZE) < half, pltpu.roll(rows, lanes - half, 1), pltpu.roll(rows, half, 1)
    )
    wide = lambda t: t if many == 1 else jnp.concatenate([t] * many, axis=1)
    return rows * wide(cosine) + swapped * wide(sine)


def stack_heads(rows, count):
    return jnp.concatenate([rows[:, i * HEAD_SIZE : (i + 1) * HEAD_SIZE] for i in range(count)], axis=0)


def spread_heads(rows, count):
    return jnp.concatenate([rows[i * TREE_TOKENS : (i + 1) * TREE_TOKENS] for i in range(count)], axis=1)


def add_into(dest, other, step):
    def some(i, _):
        rows = pl.ds(pl.multiple_of(i * step, step), step)
        dest[rows, :] = (dest[rows, :].astype(F32) + other[rows, :].astype(F32)).astype(dest.dtype)
        return 0

    lax.fori_loop(0, dest.shape[0] // step, some, 0)


def sum_into(dest, parts, step):
    def some(i, _):
        rows = pl.ds(pl.multiple_of(i * step, step), step)
        acc = parts[0][rows, :].astype(F32)
        for part in parts[1:]:
            acc = acc + part[rows, :].astype(F32)
        dest[rows, :] = acc.astype(dest.dtype)
        return 0

    lax.fori_loop(0, dest.shape[0] // step, some, 0)


def layer_kernel(
    lay,
    q_ref, kv_ref, o_ref, gate_ref, up_ref, down_ref, tok_ref, cot_ref, gain_ref, seg_ref, par_ref,
    out_hbm, in_grad_hbm, gain_out, q_hbm, kv_hbm, o_hbm, gate_hbm, up_hbm, down_hbm,
    ga, gf, wq, wkv, wo, gn, gdy, act, dgate, dup, d_act, gate_s, down_grad, gfull, normed, qs, ks, vs, probs, mix, resid,
    rot_cos, rot_sin, dq, dk5, dv5, d_part, d_in, y_part, y_in,
    fc_in, f1a, f1b, f2a, f2b, ac_in, a1a, a1b, a2, az_in, nsum, nin,
    out_ref, in_grad_ref, a_out, f_out,
    send_sems, recv_sems, own_sems, out_sems,
):
    z, x, r, c = lay.here()
    W, T, D = lay.width, TREE_TOKENS, HEAD_SIZE
    frows = gate_ref.shape[0]
    hid = lay.lines * lay.cores * frows
    groups = KEY_VALUE_HEADS
    per = QUERY_HEADS // KEY_VALUE_HEADS
    kvw = KEY_VALUE_HEADS * D
    scale = D**-0.5
    x_other, c_other, r_other = 1 - x, 1 - c, 1 - r
    x_peer = lay.device(z, x_other, r, c)
    y_peer = lay.device(z, x, r, c_other)
    sibling = lay.device(z, x, r_other, c)
    planes = lay.line(z)
    inner = lay.inner(z)
    line = range(lay.planes)
    lanes = lambda cc: pl.ds(pl.multiple_of(cc * W, 128), W)
    links = Links(send_sems, recv_sems)
    send = links.send
    outgoing = []

    def put(source, dest):
        copy = pltpu.make_async_copy(source, dest, out_sems.at[len(outgoing)])
        copy.start()
        outgoing.append(copy)

    def block(zz, xx, rr):
        return ga.at[zz * lay.lines + xx, rr]

    half = frows // 2
    halves = (pl.ds(0, half), pl.ds(half, half))
    weights = lambda w: gf[w].reshape(hid, MODEL_WIDTH)

    mine = block(z, x, r).at[:, lanes(c)]
    f_refs = (gate_ref, up_ref, down_ref)
    own = [
        pltpu.make_async_copy(q_ref, mine.at[pl.ds(0, lay.qrows), :], own_sems.at[0]),
        pltpu.make_async_copy(o_ref, mine.at[pl.ds(lay.out_at, lay.qrows), :], own_sems.at[1]),
        pltpu.make_async_copy(cot_ref, gdy.at[0], own_sems.at[2]),
    ]
    for w in range(3):
        own.append(pltpu.make_async_copy(f_refs[w], gf.at[w, x, r, :, lanes(c)], own_sems.at[3 + w]))
    for copy in own:
        copy.start()
    pad = jnp.zeros((lay.out_at - lay.kv_at - lay.kvrows, W), BF16)
    mine[lay.kv_at : lay.out_at, :] = jnp.concatenate([kv_ref[...], pad], axis=0)
    if lay.arows > lay.out_at + lay.qrows:
        mine[lay.out_at + lay.qrows :, :] = jnp.zeros((lay.arows - lay.out_at - lay.qrows, W), BF16)

    greet(lay, [lay.device(planes[p], x, r, c) for p in line[1:]] + [x_peer, y_peer, sibling])
    for copy in own[:2]:
        copy.wait()

    gfull[:, lanes(c)] = gain_ref[...]
    gain_y = send(gain_ref, gfull.at[:, lanes(c)], y_peer)
    ax, ay, arx, ary, acore = {}, {}, {}, {}, {}

    def a_rows(part, first=0, rows=None):
        at, many = lay.parts[part]
        return pl.ds(at + first, many if rows is None else rows)

    def a_here(part, zz):
        return block(zz, x, r).at[a_rows(part), lanes(c)]

    a_line = [
        Line(lay, links, a_here(i, z), lambda p, i=i: a_here(i, planes[p]), a_here(i, z), a_here(i, z)) for i in range(2)
    ]
    dy_line = Line(lay, links, gdy.at[0], lambda p: gdy.at[p], gdy.at[1], gdy.at[3 - inner])
    n_line = []
    for rows in (pl.ds(0, T // 2), pl.ds(T // 2, T // 2)):
        n_line.append(
            Line(lay, links, gn.at[0, rows], lambda p, rows=rows: gn.at[p, rows], gn.at[1, rows], gn.at[3 - inner, rows])
        )
    d_line, y_line, n_sum = (LineSum(lay, links, landing) for landing in (d_in, y_in, nin.at[pl.ds(3, 3)]))
    g_line = [LineSum(lay, links, az_in.at[:, a_rows(i), :]) for i in range(2)]

    def a_own(i, k):
        if k:
            a_line[i].arrive(k)
        here = a_here(i, planes[k])
        ax[i, k] = send(here, here, x_peer, "ga")
        ay[i, k] = send(here, here, y_peer, "ga")

    def a_core(i, k, xx, j):
        rows = block(planes[k], xx, r).at[a_rows(i), :]
        acore[i, k, j] = send(rows, rows, sibling, "ga")

    def a_relay(i, k):
        ax[i, k].wait_recv()
        top = block(planes[k], x_other, r).at[a_rows(i, 0, lay.cuts[i]), lanes(c)]
        ary[i, k] = send(top, top, y_peer, "ga")
        ay[i, k].wait_recv()
        low = block(planes[k], x, r).at[a_rows(i, lay.cuts[i], lay.parts[i][1] - lay.cuts[i]), lanes(c_other)]
        arx[i, k] = send(low, low, x_peer, "ga")
        a_core(i, k, x, 0)

    def a_finish(i, k):
        ary[i, k].wait_recv()
        arx[i, k].wait_recv()
        a_core(i, k, x_other, 1)

    def a_unpack(i, k):
        acore[i, k, 0].wait_recv()
        acore[i, k, 1].wait_recv()
        zz = planes[k]
        heads = QUERY_HEADS // lay.cores
        dest = (wq, wo)[i]
        for rr in range(lay.cores):

            def pair(m, _):
                rows = pl.ds(pl.multiple_of(lay.parts[i][0] + m * 16, 16), 16)
                left = ga[zz * lay.lines, rr, rows, :].astype(F32)
                right = ga[zz * lay.lines + 1, rr, rows, :].astype(F32)
                at = (rr * heads + 2 * m) * D + zz * 16
                dest[pl.ds(pl.multiple_of(at, 16), 16), :] = jnp.concatenate([left[:8], right[:8]], axis=0).astype(BF16)
                dest[pl.ds(pl.multiple_of(at + D, 16), 16), :] = jnp.concatenate([left[8:], right[8:]], axis=0).astype(BF16)
                return 0

            lax.fori_loop(0, heads // 2, pair, 0)
            if i == 0:
                n = lay.kvrows
                left = ga[zz * lay.lines, rr, lay.kv_at : lay.out_at, :].astype(F32)
                right = ga[zz * lay.lines + 1, rr, lay.kv_at : lay.out_at, :].astype(F32)
                at = rr * kvw + zz * (2 * n)
                wkv[pl.ds(pl.multiple_of(at, 16), 2 * n), :] = jnp.concatenate([left[:n], right[:n]], axis=0).astype(BF16)

    a_own(0, 0)
    a_line[0].start()
    a_own(1, 0)

    stream = tok_ref[...].astype(F32)
    rstd1 = lax.rsqrt(jnp.sum(stream * stream, axis=1, keepdims=True) / MODEL_WIDTH + EPS)
    tree = r * lay.cols + c
    seg_row = jnp.broadcast_to(seg_ref[pl.ds(tree, 1), :].astype(F32), (T, T))
    par_row = par_ref[pl.ds(tree, 1), :].astype(F32)
    seg_col = jnp.transpose(seg_row)
    above = jnp.zeros((T, T), F32)
    for s in range(par_ref.shape[1]):
        above = jnp.where(seg_col == s, par_row[:, s : s + 1], above)
    row_at = lax.broadcasted_iota(jnp.int32, (T, T), 0)
    lane_at = lax.broadcasted_iota(jnp.int32, (T, T), 1)
    seen = (seg_row == seg_col) | (seg_row == above) | (seg_row == 0.0)
    allowed = jnp.where(seen & (row_at >= lane_at), 1.0, 0.0)
    depth = jnp.sum(allowed, axis=1, keepdims=True) - 1.0
    freq = lax.rem(lane_at, D // 2).astype(F32) * (2.0 / D)
    angle = depth * jnp.exp(freq * -math.log(THETA))
    rot_cos[...] = jnp.cos(angle)
    sine = jnp.sin(angle)
    rot_sin[...] = jnp.where(lax.rem(lane_at, D) < D // 2, -sine, sine)
    for copy in own[2:]:
        copy.wait()
    gain_y.wait_recv()
    normed[...] = (stream * rstd1 * gfull[0:1, :]).astype(BF16)

    a_line[0].relay(2)
    a_own(0, 1)
    a_relay(0, 0)
    a_line[0].relay(3)
    a_own(0, 2)
    a_finish(0, 0)
    a_line[1].start()
    a_relay(0, 1)
    a_own(0, 3)
    a_finish(0, 1)
    a_relay(0, 2)
    a_line[1].relay(2)
    a_unpack(0, 0)
    a_line[1].relay(3)
    dy_line.start()
    a_relay(0, 3)
    a_own(1, 1)
    a_own(1, 2)
    a_finish(0, 2)
    a_unpack(0, 1)
    a_finish(0, 3)
    a_unpack(0, 2)
    a_unpack(0, 3)
    a_own(1, 3)

    fx, fy, frx, fry, fcore = {}, {}, {}, {}, {}

    def f_send(w):
        for h in range(2):
            here = gf.at[w, x, r, halves[h], lanes(c)]
            fx[w, h] = send(here, here, x_peer, "gf")
            fy[w, 1 - h] = send(gf.at[w, x, r, halves[1 - h], lanes(c)], gf.at[w, x, r, halves[1 - h], lanes(c)], y_peer, "gf")

    def f_relay(w):
        fx[w, 0].wait_recv()
        top = gf.at[w, x_other, r, halves[0], lanes(c)]
        fry[w] = send(top, top, y_peer, "gf")
        fy[w, 1].wait_recv()
        low = gf.at[w, x, r, halves[1], lanes(c_other)]
        frx[w] = send(low, low, x_peer, "gf")

    def f_core(w):
        fy[w, 0].wait_recv()
        fcore[w, 0] = send(gf.at[w, x, r], gf.at[w, x, r], sibling, "gf")

    def f_finish(w):
        fx[w, 1].wait_recv()
        fry[w].wait_recv()
        frx[w].wait_recv()
        fcore[w, 1] = send(gf.at[w, x_other, r], gf.at[w, x_other, r], sibling, "gf")

    def f_ready(w):
        fcore[w, 0].wait_recv()
        fcore[w, 1].wait_recv()

    kv = dot_nt(normed[...], wkv[...])
    turned = turn(kv, rot_cos[...], rot_sin[...])
    for g in range(groups):
        ks[g] = turned[:, g * D : (g + 1) * D].astype(BF16)
        vs[g] = kv[:, kvw + g * D : kvw + (g + 1) * D].astype(BF16)
    allowed4 = jnp.concatenate([allowed] * per, axis=0) > 0.5
    between = {
        0: [lambda: dy_line.relay(2)],
        1: [lambda: a_relay(1, 0)],
        2: [lambda: a_relay(1, 1)],
        3: [lambda: a_relay(1, 2), lambda: a_finish(1, 0)],
        4: [lambda: a_relay(1, 3), lambda: dy_line.relay(3), lambda: f_send(2), lambda: a_unpack(1, 0)],
    }
    for g in range(groups):
        cols = slice(g * per * D, (g + 1) * per * D)
        pre = turn(dot_nt(normed[...], wq[cols, :]), rot_cos[...], rot_sin[...])
        qs[g] = stack_heads(pre, per).astype(BF16)
        scores = jnp.where(allowed4, dot_nt(qs[g], ks[g]) * scale, -1e30)
        weight = jnp.exp(scores - jnp.max(scores, axis=1, keepdims=True))
        share = weight / jnp.sum(weight, axis=1, keepdims=True)
        probs[g] = share
        mixed = dot_nn(share.astype(BF16), vs[g])
        mix[:, cols] = spread_heads(mixed, per).astype(BF16)
        for step in between[g]:
            step()
    a_finish(1, 1)
    a_unpack(1, 1)
    a_finish(1, 2)
    f_send(0)
    a_unpack(1, 2)
    a_finish(1, 3)
    f_relay(2)
    a_unpack(1, 3)
    res = stream + dot_nn(mix[...], wo[...])
    resid[...] = res
    rstd2 = lax.rsqrt(jnp.sum(res * res, axis=1, keepdims=True) / MODEL_WIDTH + EPS)
    gn[0] = (res * rstd2 * gfull[1:2, :]).astype(BF16)
    for part in n_line:
        part.start()
    f_send(1)
    f_core(2)
    n_line[0].relay(2)
    n_line[1].relay(2)
    f_relay(0)
    n_line[0].relay(3)
    f_finish(2)
    f_core(0)
    n_line[1].relay(3)
    f_relay(1)
    for p in line[1:]:
        dy_line.arrive(p)
    f_ready(2)
    n_rows = lay.planes * T
    dy_all = lambda: gdy[...].reshape(n_rows, MODEL_WIDTH)
    d_act[...] = dot_nt(dy_all(), weights(2))
    f_finish(0)
    f_core(1)
    for part in n_line:
        part.arrive(1)
        part.arrive(2)
    f_finish(1)
    f_ready(0)
    gate_s[: 3 * T, :] = dot_nt(gn[:3].reshape(3 * T, MODEL_WIDTH), weights(0))
    for part in n_line:
        part.arrive(3)
    gate_s[3 * T :, :] = dot_nt(gn[3], weights(0))
    f_ready(1)

    def feed(first, last):
        count = (last - first) * T
        rows = slice(first * T, last * T)
        up = dot_nt(gn[first:last].reshape(count, MODEL_WIDTH), weights(1))
        gate = gate_s[rows, :]
        sig = 1.0 / (1.0 + jnp.exp(-gate))
        silu = gate * sig
        act[rows, :] = (silu * up).astype(BF16)
        da = d_act[rows, :]
        dup[rows, :] = (da * silu).astype(BF16)
        dgate[rows, :] = (da * up * sig * (1.0 + gate * (1.0 - sig))).astype(BF16)

    def back(p):
        rows = pl.ds(pl.multiple_of(p * T, T), T)
        part = dot_nn(dgate[rows, :], weights(0)) + dot_nn(dup[rows, :], weights(1))
        d_part[p] = part.astype(BF16)

    def mirror(line_sum, terms, landing):
        line_sum.arrive(0)
        p = 3 - inner
        terms[p] = (terms[p].astype(F32) + landing[0].astype(F32)).astype(BF16)
        line_sum.send(2, terms.at[p])

    links.flush("ga", "gf")
    for part in a_line:
        part.flush()
    fc, fs1a, fs1b, fs2a, fs2b = {}, {}, {}, {}, {}

    def fg(w):
        return gf.at[w] if w < 2 else down_grad

    def f_grad(w):
        n2 = gn[...].reshape(n_rows, MODEL_WIDTH)
        if w == 0:
            grad = dot_tn(dgate[...], n2)
        elif w == 1:
            grad = dot_tn(dup[...], n2)
        else:
            grad = dot_tn(act[...], dy_all())
        fg(w)[...] = grad.astype(BF16).reshape(lay.lines, lay.cores, frows, MODEL_WIDTH)
        fc[w] = send(fg(w).at[:, r_other], fc_in.at[w], sibling)

    def f_stage1(w):
        fc[w].wait_recv()
        for xx in range(lay.lines):
            add_into(fg(w).at[xx, r], fc_in.at[w, xx], 32)
        fs1a[w] = send(fg(w).at[x_other, r, halves[0], :], f1a.at[w], x_peer)
        fs1b[w] = send(fg(w).at[:, r, halves[1], lanes(c_other)], f1b.at[w], y_peer)

    def f_stage2(w):
        fs1a[w].wait_recv()
        add_into(fg(w).at[x, r, halves[0], :], f1a.at[w], 16)
        fs2a[w] = send(fg(w).at[x, r, halves[0], lanes(c_other)], f2a.at[w], y_peer)
        fs1b[w].wait_recv()
        for xx in range(lay.lines):
            add_into(fg(w).at[xx, r, halves[1], lanes(c)], f1b.at[w, xx], 16)
        fs2b[w] = send(fg(w).at[x_other, r, halves[1], lanes(c)], f2b.at[w], x_peer)

    def f_total(w, dest):
        fs2a[w].wait_recv()
        sum_into(f_out.at[w, halves[0], :], [fg(w).at[x, r, halves[0], lanes(c)], f2a.at[w]], 16)
        fs2b[w].wait_recv()
        sum_into(f_out.at[w, halves[1], :], [fg(w).at[x, r, halves[1], lanes(c)], f2b.at[w]], 16)
        put(f_out.at[w], dest)

    feed(0, 4)
    f_grad(2)
    back(2 + inner)
    d_line.send(0, d_part.at[2 + inner])
    back(1)
    d_line.send(1, d_part.at[1])
    f_stage1(2)
    back(3 - inner)
    back(0)
    f_grad(0)
    f_grad(1)
    mirror(d_line, d_part, d_in)
    f_stage1(0)
    f_stage1(1)
    f_stage2(2)
    y_part[...] = dot_nn(act[...], weights(2)).astype(BF16).reshape(lay.planes, T, MODEL_WIDTH)
    f_stage2(0)

    d_line.arrive(1)
    d_line.arrive(2)
    y_line.send(0, y_part.at[2 + inner])
    y_line.send(1, y_part.at[1])
    d_n2 = d_part[0].astype(F32) + d_in[1].astype(F32) + d_in[2].astype(F32)
    res = resid[...]
    rstd2 = lax.rsqrt(jnp.sum(res * res, axis=1, keepdims=True) / MODEL_WIDTH + EPS)
    gain2_grad = jnp.sum(d_n2 * res * rstd2, axis=0, keepdims=True)
    scaled2 = d_n2 * gfull[1:2, :]
    inner2 = jnp.sum(scaled2 * res, axis=1, keepdims=True)
    d_res = cot_ref[...].astype(F32) + rstd2 * scaled2 - res * (rstd2 * rstd2 * rstd2 * inner2 / MODEL_WIDTH)
    d_attn = d_res.astype(BF16)

    def place_heads(source, other, base):
        heads = QUERY_HEADS // lay.cores
        for rr in range(lay.cores):
            grad = dot_tn(source[:, rr * heads * D : (rr + 1) * heads * D], other)
            for m in range(heads // 2):
                at = 2 * m * D
                for dp in range(lay.dp):
                    tile = jnp.concatenate([grad[at + dp * 8 : at + dp * 8 + 8], grad[at + D + dp * 8 : at + D + dp * 8 + 8]], axis=0)
                    ga[dp, rr, base + m * 16 : base + m * 16 + 16, :] = tile.astype(BF16)

    to_plane = (planes[2] + inner * (planes[3] - planes[2]), planes[3] + inner * (planes[2] - planes[3]), planes[1], z)
    ac, as1a, as1b, as2a, as2b = {}, {}, {}, {}, {}

    def a_pair(zz, rr, rows):
        return ga.at[pl.ds(zz * lay.lines, lay.lines), rr, rows]

    def a_core_sums(i):
        for t in line:
            ac[i, t] = send(a_pair(to_plane[t], r_other, a_rows(i)), ac_in.at[t, :, a_rows(i), :], sibling)

    def ends(i):
        return a_rows(i, 0, lay.cuts[i]), a_rows(i, lay.cuts[i], lay.parts[i][1] - lay.cuts[i])

    def landed(i):
        tops, lows = lay.cuts[0] * i, (lay.parts[0][1] - lay.cuts[0]) * i
        return pl.ds(tops, lay.cuts[i]), pl.ds(lows, lay.parts[i][1] - lay.cuts[i])

    def a_stage1(i, t):
        top, low = ends(i)
        top_in, low_in = landed(i)
        zz = to_plane[t]
        ac[i, t].wait_recv()
        for xx in range(lay.lines):
            add_into(block(zz, xx, r).at[a_rows(i), :], ac_in.at[t, xx, a_rows(i), :], 16)
        as1a[i, t] = send(block(zz, x_other, r).at[top, :], a1a.at[t, top_in, :], x_peer)
        as1b[i, t] = send(a_pair(zz, r, low).at[:, :, lanes(c_other)], a1b.at[t, :, low_in, :], y_peer)

    def a_stage2(i, t):
        top, low = ends(i)
        top_in, low_in = landed(i)
        zz = to_plane[t]
        as1a[i, t].wait_recv()
        add_into(block(zz, x, r).at[top, :], a1a.at[t, top_in, :], 16)
        as2a[i, t] = send(block(zz, x, r).at[top, lanes(c_other)], a2.at[t, top, :], y_peer)
        as1b[i, t].wait_recv()
        for xx in range(lay.lines):
            add_into(block(zz, xx, r).at[low, lanes(c)], a1b.at[t, xx, low_in, :], 16)
        as2b[i, t] = send(block(zz, x_other, r).at[low, lanes(c)], a2.at[t, low, :], x_peer)

    def a_line_sum(i, t):
        here = a_here(i, to_plane[t])
        as2a[i, t].wait_recv()
        as2b[i, t].wait_recv()
        add_into(here, a2.at[t, a_rows(i), :], 16)
        if t in (0, 2):
            g_line[i].send((0, 2, 1)[t], here)

    def a_mirror(i):
        here = a_here(i, to_plane[1])
        g_line[i].arrive(0)
        add_into(here, az_in.at[0, a_rows(i), :], 16)
        g_line[i].send(2, here)

    def a_total(i):
        g_line[i].arrive(1)
        g_line[i].arrive(2)
        parts = [a_here(i, z), az_in.at[1, a_rows(i), :], az_in.at[2, a_rows(i), :]]
        sum_into(a_out.at[a_rows(i), :], parts, 16)
        if i == 0:
            put(a_out.at[pl.ds(0, lay.qrows), :], q_hbm)
            put(a_out.at[pl.ds(lay.kv_at, lay.kvrows), :], kv_hbm)
        else:
            put(a_out.at[pl.ds(lay.out_at, lay.qrows), :], o_hbm)

    place_heads(mix, d_attn, lay.out_at)
    a_core_sums(1)
    f_stage2(1)
    between = {
        0: [lambda: a_stage1(1, 0), lambda: a_stage1(1, 1)],
        1: [lambda: a_stage1(1, 2), lambda: a_stage1(1, 3)],
        2: [lambda: mirror(y_line, y_part, y_in)],
        3: [lambda: a_stage2(1, 0)],
        4: [lambda: a_stage2(1, 1)],
    }
    for g in range(groups):
        cols = slice(g * per * D, (g + 1) * per * D)
        dms = stack_heads(dot_nt(d_attn, wo[cols, :]), per).astype(BF16)
        share = probs[g]
        dp_ = dot_nt(dms, vs[g])
        delta = jnp.sum(share * dp_, axis=1, keepdims=True)
        ds_ = (share * (dp_ - delta)).astype(BF16)
        d_query = spread_heads(dot_nn(ds_, ks[g]) * scale, per)
        dq[:, cols] = turn(d_query, rot_cos[...], -rot_sin[...]).astype(BF16)
        dk5[g] = dot_tn(ds_, qs[g]) * scale
        dv5[g] = dot_tn(share.astype(BF16), dms)
        for step in between[g]:
            step()
    zeros = jnp.zeros((T, D), F32)
    dk_all = jnp.concatenate([dk5[g] for g in range(groups)] + [zeros], axis=1)
    dk = turn(dk_all, rot_cos[...], -rot_sin[...])[:, :kvw].astype(BF16)
    dv = jnp.concatenate([dv5[g] for g in range(groups)], axis=1).astype(BF16)
    place_heads(dq, normed[...], 0)
    for rr, rows in enumerate((dk, dv)):
        grad = dot_tn(rows, normed[...])
        pad = jnp.zeros((lay.out_at - lay.kv_at - lay.kvrows, MODEL_WIDTH), F32)
        for dp in range(lay.dp):
            tile = jnp.concatenate([grad[dp * lay.kvrows : (dp + 1) * lay.kvrows], pad], axis=0)
            ga[dp, rr, lay.kv_at : lay.out_at, :] = tile.astype(BF16)
    a_core_sums(0)
    d_normed = dot_nn(dq[...], wq[...]) + dot_nn(dk, wkv[:kvw, :]) + dot_nn(dv, wkv[kvw:, :])
    stream = tok_ref[...].astype(F32)
    rstd1 = lax.rsqrt(jnp.sum(stream * stream, axis=1, keepdims=True) / MODEL_WIDTH + EPS)
    gain1_grad = jnp.sum(d_normed * stream * rstd1, axis=0, keepdims=True)
    nsum[0] = jnp.concatenate([gain1_grad, gain2_grad, jnp.zeros((6, MODEL_WIDTH), F32)], axis=0)
    g_core = send(nsum.at[0], nin.at[0], sibling)
    a_stage2(1, 2)
    a_stage2(1, 3)
    a_stage1(0, 0)
    a_line_sum(1, 0)
    g_core.wait_recv()
    nsum[1] = nsum[0] + nin[0]
    g_x = send(nsum.at[1], nin.at[1], x_peer)
    a_stage1(0, 1)
    a_line_sum(1, 1)
    a_stage2(0, 0)
    g_x.wait_recv()
    nsum[2] = nsum[1] + nin[1]
    g_y = send(nsum.at[2], nin.at[2], y_peer)
    a_stage1(0, 2)
    a_line_sum(1, 2)
    scaled1 = d_normed * gfull[0:1, :]
    inner1 = jnp.sum(scaled1 * stream, axis=1, keepdims=True)
    in_grad = d_res + rstd1 * scaled1 - stream * (rstd1 * rstd1 * rstd1 * inner1 / MODEL_WIDTH)
    in_grad_ref[...] = in_grad.astype(BF16)
    put(in_grad_ref, in_grad_hbm)
    a_stage2(0, 1)
    g_y.wait_recv()
    nsum[3] = nsum[2] + nin[2]
    n_sum.send(0, nsum.at[3])
    a_stage1(0, 3)
    a_line_sum(0, 0)
    a_mirror(1)
    y_line.arrive(1)
    y_line.arrive(2)
    y = resid[...] + y_part[0].astype(F32) + y_in[1].astype(F32) + y_in[2].astype(F32)
    out_ref[...] = y.astype(BF16)
    put(out_ref, out_hbm)
    a_stage2(0, 2)
    a_line_sum(0, 1)
    n_sum.arrive(0)
    nsum[4] = nsum[3] + nin[3]
    n_sum.send(2, nsum.at[4])
    a_line_sum(1, 3)
    f_total(2, down_hbm)
    a_mirror(0)
    a_stage2(0, 3)
    a_line_sum(0, 2)
    f_total(0, gate_hbm)
    f_total(1, up_hbm)
    a_total(1)
    n_sum.arrive(2)
    nsum[5] = nsum[4] + nin[5]
    gain_out[...] = nsum[5, :, lanes(c)]
    a_line_sum(0, 3)
    a_total(0)
    links.flush()
    for part in [dy_line, d_line, y_line, n_sum] + n_line + g_line:
        part.flush()
    for copy in outgoing:
        copy.wait()


def whole_layer(lay, blocks, tokens, cotangent, gains, seg_ids, parents):
    vm = lambda *shape: pltpu.VMEM(shape, BF16)
    vf = lambda *shape: pltpu.VMEM(shape, F32)
    M, T, D, W = MODEL_WIDTH, TREE_TOKENS, HEAD_SIZE, lay.width
    frows = blocks[3].shape[0]
    hid = lay.lines * lay.cores * frows
    G, per = KEY_VALUE_HEADS, QUERY_HEADS // KEY_VALUE_HEADS
    n, nl, half = lay.planes, lay.lines, frows // 2
    vmem, hbm = pl.BlockSpec(memory_space=pltpu.VMEM), pl.BlockSpec(memory_space=pl.ANY)
    count = 200
    scratch = [
        vm(lay.dp, lay.cores, lay.arows, M),
        vm(3, nl, lay.cores, frows, M),
        vm(QUERY_HEADS * D, M),
        vm(2 * G * D, M),
        vm(QUERY_HEADS * D, M),
        vm(n, T, M),
        vm(n, T, M),
        vm(n * T, hid),
        vm(n * T, hid),
        vm(n * T, hid),
        vf(n * T, hid),
        vf(n * T, hid),
        vm(nl, lay.cores, frows, M),
        vf(8, M),
        vm(T, M),
        vm(G, per * T, D),
        vm(G, T, D),
        vm(G, T, D),
        vf(G, per * T, T),
        vm(T, M),
        vf(T, M),
        vf(T, T),
        vf(T, T),
        vm(T, M),
        vf(G, T, D),
        vf(G, T, D),
        vm(n, T, M),
        vm(n - 1, T, M),
        vm(n, T, M),
        vm(n - 1, T, M),
        vm(3, nl, frows, M),
        vm(3, half, M),
        vm(3, nl, half, W),
        vm(3, half, W),
        vm(3, half, W),
        vm(n, nl, lay.arows, M),
        vm(n, sum(lay.cuts), M),
        vm(n, nl, lay.arows - sum(lay.cuts), W),
        vm(n, lay.arows, W),
        vm(n - 1, lay.arows, W),
        vf(6, 8, M),
        vf(2 + n, 8, M),
        vm(T, M),
        vm(T, M),
        vf(lay.arows, W),
        vf(3, frows, W),
        pltpu.SemaphoreType.DMA((count,)),
        pltpu.SemaphoreType.DMA((count,)),
        pltpu.SemaphoreType.DMA((6,)),
        pltpu.SemaphoreType.DMA((8,)),
    ]
    return pl.pallas_call(
        functools.partial(layer_kernel, lay),
        out_shape=(
            jax.ShapeDtypeStruct((T, M), BF16),
            jax.ShapeDtypeStruct((T, M), BF16),
            jax.ShapeDtypeStruct((8, W), F32),
        )
        + tuple(jax.ShapeDtypeStruct(b.shape, F32) for b in blocks),
        in_specs=[hbm, vmem, hbm, hbm, hbm, hbm, vmem, vmem, vmem, vmem, vmem],
        out_specs=(hbm, hbm, vmem) + (hbm,) * 6,
        scratch_shapes=scratch,
        compiler_params=pltpu.CompilerParams(collective_id=0, has_side_effects=True, vmem_limit_bytes=62 * 2**20),
        name="whole_layer",
    )(*blocks, tokens, cotangent, gains, seg_ids, parents)


def finish_kernel(count, *refs):
    held, (into, back) = refs[2 * count : 3 * count], refs[3 * count :]
    first = [pltpu.make_async_copy(refs[i], held[i], into.at[i]) for i in range(count)]
    last = [pltpu.make_async_copy(held[i], refs[count + i], back.at[i]) for i in range(count)]
    for copy in first:
        copy.start()
    for i in range(count):
        first[i].wait()
        last[i].start()
    for copy in last:
        copy.wait()


def finish(results):
    hbm = pl.BlockSpec(memory_space=pl.ANY)
    count = len(results)
    dma = pltpu.SemaphoreType.DMA((count,))
    return pl.pallas_call(
        functools.partial(finish_kernel, count),
        out_shape=tuple(jax.ShapeDtypeStruct(v.shape, v.dtype) for v in results),
        in_specs=[hbm] * count,
        out_specs=(hbm,) * count,
        scratch_shapes=[pltpu.VMEM(v.shape, v.dtype) for v in results] + [dma, dma],
        name="finish",
    )(*results)


def body(lay, tokens, cotangent, seg_ids, parents, norm1_gain, w_query, key_value_weight, w_out, norm2_gain, w_gate, w_up, w_down):
    W = lay.width
    blocks = (
        jnp.transpose(w_query, (1, 2, 0)).reshape(lay.qrows, W),
        jnp.transpose(key_value_weight[:, 0, :]),
        w_out.reshape(lay.qrows, W),
        w_gate.T,
        w_up.T,
        w_down,
    )
    gains = jnp.concatenate([norm1_gain[None], norm2_gain[None], jnp.zeros((6, W), F32)], axis=0)
    layer_out, in_grad, gain_sum, query, keyval, out, gate, up, down = whole_layer(
        lay, blocks, tokens, cotangent, gains, seg_ids, parents
    )
    layer_out, in_grad, query, keyval, out, gate, up, down = finish(
        (layer_out, in_grad, query, keyval, out, gate, up, down)
    )
    heads = QUERY_HEADS // lay.cores
    shape = (heads, HEAD_SIZE // lay.dp, W)
    return (
        layer_out,
        in_grad,
        gain_sum[0],
        jnp.transpose(query.reshape(shape), (2, 0, 1)),
        keyval.T[:, None, :],
        out.reshape(shape),
        gain_sum[1],
        gate.T,
        up.T,
        down,
    )


def general_layout(segment, parent):
    labels = jnp.arange(SEGS, dtype=jnp.int32)
    member = (segment[:, None] == labels[None, :]).astype(jnp.float32)
    link = ((parent[:, None] == labels[None, :]) & (labels[:, None] > 0)).astype(jnp.float32)
    ident = jnp.eye(SEGS, dtype=jnp.float32)

    def climb(level, reach):
        return ident + jnp.dot(link, reach, precision=lax.Precision.HIGHEST)

    reach = lax.fori_loop(0, SEGS, climb, ident)
    visible = jnp.dot(jnp.dot(member, reach, precision=lax.Precision.HIGHEST), member.T, precision=lax.Precision.HIGHEST) > 0.5
    places = jnp.arange(segment.shape[0], dtype=jnp.int32)
    allowed = visible & (places[:, None] >= places[None, :])
    sizes = jnp.sum(member, axis=0)
    earlier = (labels[None, :] < labels[:, None]).astype(jnp.float32)
    starts = jnp.dot(earlier, sizes, precision=lax.Precision.HIGHEST)
    above = jnp.dot(reach, sizes, precision=lax.Precision.HIGHEST) - sizes
    tree_depth = places.astype(jnp.float32) + jnp.dot(member, above - starts, precision=lax.Precision.HIGHEST)
    return (allowed, tree_depth)


def general_rotate(value_rows, tree_depth, sign):
    half = value_rows.shape[-1] // 2
    freqs = jnp.arange(half, dtype=jnp.float32) * (2.0 / value_rows.shape[-1])
    inverse = jnp.exp(freqs * -math.log(THETA))
    angle = tree_depth[:, None] * inverse[None, :]
    cosine = jnp.cos(angle)[:, None, :]
    sine = sign * jnp.sin(angle)[:, None, :]
    first = value_rows[..., :half]
    second = value_rows[..., half:]
    return jnp.concatenate(
        [first * cosine - second * sine, second * cosine + first * sine], axis=-1
    )


def product(left, right):
    return jnp.dot(left, right, preferred_element_type=jnp.float32)


def general_body(
    tokens,
    cotangent,
    seg_ids,
    parents,
    norm1_gain,
    w_query,
    key_value_weight,
    w_out,
    norm2_gain,
    w_gate,
    w_up,
    w_down,
):
    columns = lax.axis_size("col")
    row_index = lax.axis_index("row")
    col_index = lax.axis_index("col")
    feature_width = MODEL_WIDTH // columns
    half_rows = columns * TREE_TOKENS // 2
    heads_here = QUERY_HEADS // 2
    query_total_width = heads_here * HEAD_SIZE
    heads_per_group = QUERY_HEADS // KEY_VALUE_HEADS
    scale = HEAD_SIZE ** (-0.5)
    stream_rows, cot_rows = (
        lax.all_to_all(tokens, "col", split_axis=1, concat_axis=0, tiled=True),
        lax.all_to_all(cotangent, "col", split_axis=1, concat_axis=0, tiled=True),
    )

    def col_total(value_rows):
        return lax.psum(value_rows, "col")

    def gather_rows(value_rows):
        return lax.all_gather(value_rows, "row", axis=0, tiled=True)

    def gather_cols(value_rows):
        return lax.all_gather(value_rows, "col", axis=0, tiled=True)

    def col_reduce(term, rows):
        return lax.psum_scatter(
            term(jnp.int32(0), rows * lax.axis_size("col")), "col", scatter_dimension=0, tiled=True
        )

    def row_reduce(term, rows):
        return lax.psum_scatter(
            term(jnp.int32(0), rows * lax.axis_size("row")), "row", scatter_dimension=0, tiled=True
        )

    def fetch():
        blocks = (
            lax.all_gather(w_query, "dp", axis=2, tiled=True),
            lax.all_gather(key_value_weight, "dp", axis=2, tiled=True),
            lax.all_gather(w_out, "dp", axis=1, tiled=True),
            lax.all_gather(w_gate, "dp", axis=1, tiled=True),
            lax.all_gather(w_up, "dp", axis=1, tiled=True),
            lax.all_gather(w_down, "dp", axis=0, tiled=True),
        )
        wide = None
        return (blocks, wide)

    def local_heads(pair_part):
        spread_heads = jnp.repeat(pair_part, heads_per_group, axis=1)
        return lax.dynamic_slice_in_dim(spread_heads, row_index * heads_here, heads_here, 1)

    def fold_heads(grad_here):
        spread_heads = jnp.zeros((TREE_TOKENS, QUERY_HEADS, HEAD_SIZE), jnp.float32)
        spread_heads = lax.dynamic_update_slice_in_dim(
            spread_heads, grad_here, row_index * heads_here, 1
        )
        return jnp.sum(
            spread_heads.reshape(TREE_TOKENS, KEY_VALUE_HEADS, heads_per_group, HEAD_SIZE), axis=2
        )

    gradients = (
        jnp.zeros((feature_width,), jnp.float32),
        jnp.zeros((feature_width, heads_here, HEAD_SIZE), jnp.float32),
        jnp.zeros((feature_width, 1, KEY_VALUE_HEADS * HEAD_SIZE), jnp.float32),
        jnp.zeros((heads_here, HEAD_SIZE, feature_width), jnp.float32),
        jnp.zeros((feature_width,), jnp.float32),
        jnp.zeros((feature_width, w_gate.shape[1] * lax.axis_size("dp")), jnp.float32),
        jnp.zeros((feature_width, w_up.shape[1] * lax.axis_size("dp")), jnp.float32),
        jnp.zeros((w_down.shape[0] * lax.axis_size("dp"), feature_width), jnp.float32),
    )
    results = []
    input_grads = []
    for batch_index in range(2):
        blocks, wide = fetch()
        (
            forward_query_block,
            forward_key_value_block,
            forward_out_block,
            forward_gate_block,
            forward_up_block,
            forward_down_block,
        ) = blocks
        forward_query_matrix = forward_query_block.reshape(feature_width, query_total_width)
        forward_key_value_matrix = forward_key_value_block.reshape(
            feature_width, KEY_VALUE_HEADS * HEAD_SIZE
        )
        forward_out_matrix = forward_out_block.reshape(query_total_width, feature_width)
        forward_stream = lax.dynamic_slice_in_dim(
            stream_rows, batch_index * half_rows, half_rows, 0
        ).astype(jnp.float32)
        forward_rstd1 = lax.rsqrt(
            col_total(jnp.sum(forward_stream * forward_stream, axis=1)) / MODEL_WIDTH + EPS
        )
        normed = (forward_stream * forward_rstd1[:, None] * norm1_gain).astype(jnp.bfloat16)
        forward_normed_all = gather_rows(normed)

        def qkv_term(start, count):
            return jnp.concatenate(
                [
                    product(forward_normed_all, forward_query_matrix),
                    product(forward_normed_all, forward_key_value_matrix),
                ],
                axis=1,
            )

        projected_rows = col_reduce(qkv_term, TREE_TOKENS)
        half_cols = columns // 2
        tree_slot = (
            col_index // half_cols * (2 * half_cols)
            + batch_index * half_cols
            + col_index % half_cols
        )
        segment = lax.dynamic_index_in_dim(seg_ids, tree_slot, 0, keepdims=False)
        parent = lax.dynamic_index_in_dim(parents, tree_slot, 0, keepdims=False)
        forward_allowed, forward_tree_depth = general_layout(segment, parent)
        query_pre = projected_rows[:, :query_total_width].reshape(
            TREE_TOKENS, heads_here, HEAD_SIZE
        )
        forward_query = general_rotate(query_pre, forward_tree_depth, 1.0).astype(jnp.bfloat16)
        own_unrotated = projected_rows[:, query_total_width:].reshape(
            TREE_TOKENS, KEY_VALUE_HEADS, HEAD_SIZE
        )
        own_part = jnp.where(
            row_index == 0, general_rotate(own_unrotated, forward_tree_depth, 1.0), own_unrotated
        ).astype(jnp.bfloat16)
        forward_pair = lax.all_gather(own_part[:, None], "row", axis=1, tiled=True)
        forward_keys_here = local_heads(forward_pair[:, 0])
        forward_values_here = local_heads(forward_pair[:, 1])
        forward_scores = (
            jnp.einsum(
                "qhd,khd->hqk", forward_query, forward_keys_here, preferred_element_type=jnp.float32
            )
            * scale
        )
        forward_masked = jnp.where(forward_allowed[None], forward_scores, -1e30)
        row_max = jnp.max(forward_masked, axis=-1, keepdims=True)
        forward_total = (
            jnp.log(jnp.sum(jnp.exp(forward_masked - row_max), axis=-1, keepdims=True)) + row_max
        )
        probs = jnp.exp(forward_masked - forward_total).astype(jnp.bfloat16)
        mixed = jnp.einsum(
            "hqk,khd->qhd", probs, forward_values_here, preferred_element_type=jnp.float32
        )
        mixed = mixed.astype(jnp.bfloat16).reshape(TREE_TOKENS, query_total_width)
        forward_mixed_all = gather_cols(mixed)

        def out_term(start, count):
            return product(forward_mixed_all, forward_out_matrix)

        forward_resid = forward_stream + row_reduce(out_term, half_rows)
        forward_rstd2 = lax.rsqrt(
            col_total(jnp.sum(forward_resid * forward_resid, axis=1)) / MODEL_WIDTH + EPS
        )
        normed2 = (forward_resid * forward_rstd2[:, None] * norm2_gain).astype(jnp.bfloat16)
        normed2_all = gather_rows(normed2)
        forward_hidden_here = forward_gate_block.shape[1]

        def gate_term(start, count):
            return jnp.concatenate(
                [product(normed2_all, forward_gate_block), product(normed2_all, forward_up_block)],
                axis=1,
            )

        gate_up = col_reduce(gate_term, TREE_TOKENS)
        forward_gate = gate_up[:, :forward_hidden_here]
        forward_up_part = gate_up[:, forward_hidden_here:]
        hidden = (jax.nn.silu(forward_gate) * forward_up_part).astype(jnp.bfloat16)
        forward_hidden_all = gather_cols(hidden)

        def down_term(start, count):
            return product(forward_hidden_all, forward_down_block)

        result = (forward_resid + row_reduce(down_term, half_rows)).astype(jnp.bfloat16)
        forward_saved = (
            forward_stream,
            forward_rstd1,
            forward_normed_all,
            forward_query,
            forward_pair,
            forward_total,
            forward_allowed,
            forward_tree_depth,
            forward_mixed_all,
            forward_resid,
            forward_rstd2,
            normed2_all,
            forward_gate,
            forward_up_part,
            forward_hidden_all,
        )
        result, saved = (result, forward_saved)
        blocks, wide = fetch()
        backward_gradients = gradients
        query_block, key_value_block, out_block, gate_block, up_block, down_block = blocks
        (
            stream,
            rstd1,
            normed_all,
            query,
            pair,
            total,
            allowed,
            tree_depth,
            mixed_all,
            resid,
            rstd2,
            kept_features,
            gate,
            up_part,
            hidden_all,
        ) = saved
        query_matrix = query_block.reshape(feature_width, query_total_width)
        key_value_matrix = key_value_block.reshape(feature_width, KEY_VALUE_HEADS * HEAD_SIZE)
        out_matrix = out_block.reshape(query_total_width, feature_width)
        hidden_here = gate_block.shape[1]
        cot_low = lax.dynamic_slice_in_dim(cot_rows, batch_index * half_rows, half_rows, 0)
        cot_full = cot_low.astype(jnp.float32)
        cot_all = gather_rows(cot_low)
        down_grad = jnp.einsum("tf,td->fd", hidden_all, cot_all, preferred_element_type=jnp.float32)

        def hidden_term(start, count):
            return jnp.einsum("td,fd->tf", cot_all, down_block, preferred_element_type=jnp.float32)

        d_hidden = col_reduce(hidden_term, TREE_TOKENS)
        sigmoid_gate = jax.nn.sigmoid(gate)
        d_up = (d_hidden * gate * sigmoid_gate).astype(jnp.bfloat16)
        d_gate = (d_hidden * up_part * sigmoid_gate * (1.0 + gate * (1.0 - sigmoid_gate))).astype(
            jnp.bfloat16
        )
        d_both = gather_cols(jnp.concatenate([d_gate, d_up], axis=1))
        gate_grad = jnp.einsum(
            "td,tf->df", kept_features, d_both[:, :hidden_here], preferred_element_type=jnp.float32
        )
        up_grad = jnp.einsum(
            "td,tf->df", kept_features, d_both[:, hidden_here:], preferred_element_type=jnp.float32
        )

        def back2_term(start, count):
            first = jnp.einsum(
                "tf,df->td", d_both[:, :hidden_here], gate_block, preferred_element_type=jnp.float32
            )
            return first + jnp.einsum(
                "tf,df->td", d_both[:, hidden_here:], up_block, preferred_element_type=jnp.float32
            )

        d_normed2 = row_reduce(back2_term, half_rows)
        scaled2 = d_normed2 * norm2_gain
        gain2_grad = jnp.sum(d_normed2 * resid * rstd2[:, None], axis=0)
        inner2 = col_total(jnp.sum(scaled2 * resid, axis=1))
        d_resid = (
            cot_full
            + rstd2[:, None] * scaled2
            - resid * (rstd2 * rstd2 * rstd2 * inner2 / MODEL_WIDTH)[:, None]
        )
        d_attn_all = gather_rows(d_resid.astype(jnp.bfloat16))
        out_grad = jnp.einsum(
            "tq,td->qd", mixed_all, d_attn_all, preferred_element_type=jnp.float32
        )

        def mixed_term(start, count):
            return jnp.einsum(
                "td,qd->tq", d_attn_all, out_matrix, preferred_element_type=jnp.float32
            )

        d_mixed = (
            col_reduce(mixed_term, TREE_TOKENS)
            .astype(jnp.bfloat16)
            .reshape(TREE_TOKENS, heads_here, HEAD_SIZE)
        )
        keys_here = local_heads(pair[:, 0])
        values_here = local_heads(pair[:, 1])
        scores = (
            jnp.einsum("qhd,khd->hqk", query, keys_here, preferred_element_type=jnp.float32) * scale
        )
        masked = jnp.where(allowed[None], scores, -1e30)
        probs_full = jnp.exp(masked - total)
        probs_low = probs_full.astype(jnp.bfloat16)
        d_probs = jnp.einsum(
            "qhd,khd->hqk", d_mixed, values_here, preferred_element_type=jnp.float32
        )
        delta = jnp.sum(probs_full * d_probs, axis=-1, keepdims=True)
        d_scores = (probs_full * (d_probs - delta)).astype(jnp.bfloat16)
        d_query = (
            jnp.einsum("hqk,khd->qhd", d_scores, keys_here, preferred_element_type=jnp.float32)
            * scale
        )
        d_keys = (
            jnp.einsum("hqk,qhd->khd", d_scores, query, preferred_element_type=jnp.float32) * scale
        )
        d_values = jnp.einsum(
            "hqk,qhd->khd", probs_low, d_mixed, preferred_element_type=jnp.float32
        )
        d_pair = jnp.stack([fold_heads(d_keys), fold_heads(d_values)], axis=1)
        own_gradient = lax.psum_scatter(
            d_pair.astype(jnp.bfloat16), "row", scatter_dimension=1, tiled=True
        ).astype(jnp.float32)[:, 0]
        own_gradient = jnp.where(
            row_index == 0, general_rotate(own_gradient, tree_depth, -1.0), own_gradient
        )
        query_pre_gradient = general_rotate(d_query, tree_depth, -1.0)
        d_proj = jnp.concatenate(
            [
                query_pre_gradient.reshape(TREE_TOKENS, query_total_width),
                own_gradient.reshape(TREE_TOKENS, KEY_VALUE_HEADS * HEAD_SIZE),
            ],
            axis=1,
        ).astype(jnp.bfloat16)
        d_proj_all = gather_cols(d_proj)
        query_grad = jnp.einsum(
            "td,tq->dq",
            normed_all,
            d_proj_all[:, :query_total_width],
            preferred_element_type=jnp.float32,
        )
        keyval_grad = jnp.einsum(
            "td,tq->dq",
            normed_all,
            d_proj_all[:, query_total_width:],
            preferred_element_type=jnp.float32,
        )
        in_matrix = jnp.concatenate([query_matrix, key_value_matrix], axis=1)

        def back1_term(start, count):
            return jnp.einsum(
                "tq,dq->td", d_proj_all, in_matrix, preferred_element_type=jnp.float32
            )

        d_normed = row_reduce(back1_term, half_rows)
        scaled1 = d_normed * norm1_gain
        gain1_grad = jnp.sum(d_normed * stream * rstd1[:, None], axis=0)
        inner1 = col_total(jnp.sum(scaled1 * stream, axis=1))
        d_stream = (
            d_resid
            + rstd1[:, None] * scaled1
            - stream * (rstd1 * rstd1 * rstd1 * inner1 / MODEL_WIDTH)[:, None]
        )
        updates = (
            gain1_grad,
            query_grad.reshape(query_block.shape),
            keyval_grad.reshape(key_value_block.shape),
            out_grad.reshape(out_block.shape),
            gain2_grad,
            gate_grad,
            up_grad,
            down_grad,
        )
        backward_gradients = tuple((a + b for a, b in zip(backward_gradients, updates)))
        d_stream, gradients = (d_stream.astype(jnp.bfloat16), backward_gradients)
        results.append(result)
        input_grads.append(d_stream)
    shards = (
        lax.psum_scatter(
            gradients[1].astype(jnp.bfloat16), "dp", scatter_dimension=2, tiled=True
        ).astype(jnp.float32),
        lax.psum_scatter(
            gradients[2].astype(jnp.bfloat16), "dp", scatter_dimension=2, tiled=True
        ).astype(jnp.float32),
        lax.psum_scatter(
            gradients[3].astype(jnp.bfloat16), "dp", scatter_dimension=1, tiled=True
        ).astype(jnp.float32),
        lax.psum_scatter(
            gradients[5].astype(jnp.bfloat16), "dp", scatter_dimension=1, tiled=True
        ).astype(jnp.float32),
        lax.psum_scatter(
            gradients[6].astype(jnp.bfloat16), "dp", scatter_dimension=1, tiled=True
        ).astype(jnp.float32),
        lax.psum_scatter(
            gradients[7].astype(jnp.bfloat16), "dp", scatter_dimension=0, tiled=True
        ).astype(jnp.float32),
    )
    gains = lax.psum((gradients[0], gradients[4]), ("dp", "row"))
    final_out, final_grad = (
        lax.all_to_all(
            jnp.concatenate(results, axis=0), "col", split_axis=0, concat_axis=1, tiled=True
        ),
        lax.all_to_all(
            jnp.concatenate(input_grads, axis=0), "col", split_axis=0, concat_axis=1, tiled=True
        ),
    )
    return (
        final_out,
        final_grad,
        gains[0],
        shards[0],
        shards[1],
        shards[2],
        gains[1],
        shards[3],
        shards[4],
        shards[5],
    )


def solution(mesh):
    placed = (
        P(("dp", "row", "col"), None),
        P(("dp", "row", "col"), None),
        P("dp", None),
        P("dp", None),
        P("col"),
        P("col", "row", "dp"),
        P("col", "row", "dp"),
        P("row", "dp", "col"),
        P("col"),
        P("col", ("dp", "row")),
        P("col", ("dp", "row")),
        P(("dp", "row"), "col"),
    )
    lay = Layout(mesh.shape)
    work = functools.partial(body, lay) if lay.fits() else general_body
    return jax.shard_map(
        work,
        mesh=mesh,
        in_specs=placed,
        out_specs=(
            P(("dp", "row", "col"), None),
            P(("dp", "row", "col"), None),
            P("col"),
            P("col", "row", "dp"),
            P("col", "row", "dp"),
            P("row", "dp", "col"),
            P("col"),
            P("col", ("dp", "row")),
            P("col", ("dp", "row")),
            P(("dp", "row"), "col"),
        ),
        check_vma=False,
    )
```

```python
import functools
import math

import jax
import jax.numpy as jnp
from jax import lax
from jax.experimental import pallas as pl
from jax.experimental.pallas import tpu as pltpu
from jax.sharding import PartitionSpec as P

MODEL_WIDTH = 1280
QUERY_HEADS = 20
KEY_VALUE_HEADS = 5
HEAD_SIZE = 64
TREE_TOKENS = 128
SEGS = 13
PLANES = 4

EPS = 1e-05
THETA = 10000.0
MESH = pl.DeviceIdType.MESH
F32 = jnp.float32
BF16 = jnp.bfloat16


class Layout:
    def __init__(self, shape):
        self.planes = PLANES
        self.lines = shape["dp"] // PLANES
        self.cores = shape["row"]
        self.cols = shape["col"]
        self.dp = shape["dp"]
        self.width = MODEL_WIDTH // self.cols
        self.qrows = QUERY_HEADS // self.cores * (HEAD_SIZE // self.dp)
        self.kvrows = KEY_VALUE_HEADS * HEAD_SIZE // self.dp
        self.kv_at = self.qrows
        self.out_at = -(-(self.kv_at + self.kvrows) // 16) * 16
        self.arows = -(-(self.out_at + self.qrows) // 16) * 16
        self.parts = ((0, self.out_at), (self.out_at, self.arows - self.out_at))
        self.cuts = tuple(-(-(rows // 2) // 16) * 16 for _, rows in self.parts)

    def fits(self):
        return self.lines == 2 and self.cores == 2 and self.cols == 2 and self.dp == 2 * PLANES

    def here(self):
        dp = lax.axis_index("dp")
        return dp // self.lines, lax.rem(dp, self.lines), lax.axis_index("row"), lax.axis_index("col")

    def inner(self, z):
        return lax.rem((z + 1) // 2, 2)

    def line(self, z):
        half = z // 2
        return z, z + 1 - 2 * lax.rem(z, 2), 2 - half, 3 - 3 * half

    def device(self, z, x, r, c):
        return (z * self.lines + x, r, c)


def greet(peers):
    barrier = pltpu.get_barrier_semaphore()
    for peer in peers:
        pl.semaphore_signal(barrier, inc=1, device_id=peer, device_id_type=MESH)


def greeted(peers):
    pl.semaphore_wait(pltpu.get_barrier_semaphore(), len(peers))


def dot_nt(left, right):
    return lax.dot_general(left, right, (((1,), (1,)), ((), ())), preferred_element_type=F32)


def dot_tn(left, right):
    return lax.dot_general(left, right, (((0,), (0,)), ((), ())), preferred_element_type=F32)


def dot_nn(left, right):
    return jnp.dot(left, right, preferred_element_type=F32)


class Line:
    def __init__(self, lay, links, source, slots, pos_1, pos_x):
        z, x, r, c = lay.here()
        self.inner = lay.inner(z)
        base = links.take(4)
        self.slots = slots
        peers = lay.line(z)
        self.side, self.near = lay.device(peers[1], x, r, c), lay.device(peers[2], x, r, c)

        def copy(src, dst, s, t, peer):
            return pltpu.make_async_remote_copy(
                src_ref=src,
                dst_ref=dst,
                send_sem=links.send_sems.at[base + s],
                recv_sem=links.recv_sems.at[base + t],
                device_id=peer,
                device_id_type=MESH,
            )

        self.first = copy(source, pos_1, 0, 0, self.side)
        self.cross = copy(source, pos_x, 1, 2 - self.inner, self.near)
        self.passed = {p: copy(slots(p), slots(p), p, p - 1, self.side) for p in (2, 3)}

    def start(self):
        self.first.start()
        self.cross.start()

    def relay(self, p):
        @pl.when(self.inner == 1)
        def _():
            self.passed[p].wait_recv()
            self.passed[p].start()

    def arrive(self, p):
        if p == 1:
            self.first.wait_recv()
            return

        @pl.when(self.inner == 0)
        def _():
            self.passed[p].wait_recv()

    def flush(self):
        self.first.wait_send()
        self.cross.wait_send()

        @pl.when(self.inner == 1)
        def _():
            self.passed[2].wait_send()
            self.passed[3].wait_send()


class LineSum:
    def __init__(self, lay, links, landing):
        z, x, r, c = lay.here()
        base = links.take(3)
        side, mirror = lay.device(lay.line(z)[1], x, r, c), lay.device(lay.planes - 1 - z, x, r, c)
        self.copy = lambda source, s: pltpu.make_async_remote_copy(
            src_ref=source,
            dst_ref=landing.at[s],
            send_sem=links.send_sems.at[base + s],
            recv_sem=links.recv_sems.at[base + s],
            device_id=mirror if s == 2 else side,
            device_id_type=MESH,
        )
        self.landing, self.used = landing, set()

    def send(self, s, source):
        self.used.add(s)
        self.copy(source, s).start()

    def arrive(self, s):
        self.copy(self.landing.at[s], s).wait_recv()

    def flush(self):
        for s in sorted(self.used):
            self.copy(self.landing.at[s], s).wait_send()


class Links:
    def __init__(self, send_sems, recv_sems):
        self.send_sems, self.recv_sems, self.used = send_sems, recv_sems, 0
        self.open = []

    def take(self, count):
        first = self.used
        self.used += count
        return first

    def send(self, src, dst, peer, source=None):
        at = self.take(1)
        copy = pltpu.make_async_remote_copy(
            src_ref=src,
            dst_ref=dst,
            send_sem=self.send_sems.at[at],
            recv_sem=self.recv_sems.at[at],
            device_id=peer,
            device_id_type=MESH,
        )
        copy.start()
        self.open.append((source, copy))
        return copy

    def flush(self, *sources):
        for source, copy in self.open:
            if not sources or source in sources:
                copy.wait_send()
        self.open = [o for o in self.open if sources and o[0] not in sources]


def turn(rows, cosine, sine):
    lanes = rows.shape[1]
    many = lanes // 128
    half = HEAD_SIZE // 2
    lane = lax.broadcasted_iota(jnp.int32, rows.shape, 1)
    swapped = jnp.where(
        lax.rem(lane, HEAD_SIZE) < half, pltpu.roll(rows, lanes - half, 1), pltpu.roll(rows, half, 1)
    )
    wide = lambda t: t if many == 1 else jnp.concatenate([t] * many, axis=1)
    return rows * wide(cosine) + swapped * wide(sine)


def stack_heads(rows, count):
    return jnp.concatenate([rows[:, i * HEAD_SIZE : (i + 1) * HEAD_SIZE] for i in range(count)], axis=0)


def spread_heads(rows, count):
    return jnp.concatenate([rows[i * TREE_TOKENS : (i + 1) * TREE_TOKENS] for i in range(count)], axis=1)


def add_into(dest, other, step):
    def some(i, _):
        rows = pl.ds(pl.multiple_of(i * step, step), step)
        dest[rows, :] = (dest[rows, :].astype(F32) + other[rows, :].astype(F32)).astype(dest.dtype)
        return 0

    lax.fori_loop(0, dest.shape[0] // step, some, 0)


def sum_into(dest, parts, step):
    def some(i, _):
        rows = pl.ds(pl.multiple_of(i * step, step), step)
        acc = parts[0][rows, :].astype(F32)
        for part in parts[1:]:
            acc = acc + part[rows, :].astype(F32)
        dest[rows, :] = acc.astype(dest.dtype)
        return 0

    lax.fori_loop(0, dest.shape[0] // step, some, 0)


def layer_kernel(
    lay,
    q_ref, kv_ref, o_ref, gate_ref, up_ref, down_ref, tok_ref, cot_ref, gain1_ref, gain2_ref, seg_ref, par_ref,
    out_hbm, in_grad_hbm, gain_hbm, q_hbm, kv_hbm, o_hbm, gate_hbm, up_hbm, down_hbm,
    ga, gf, wq, wkv, wo, gn, gdy, act, dgate, dup, d_act, gate_s, down_grad, gate_grad, gfull, normed, qs, ks, vs, probs, mix, resid,
    rot_cos, rot_sin, dq, dkv, dk5, dv5, d_in, y_in,
    fc_in, f1a, f1b, f2a, f2b, ac_in, a1a, a1b, a2, az_in, nsum, nin,
    out_ref, in_grad_ref, gain_out,
    send_sems, recv_sems, own_sems, out_sems,
):
    z, x, r, c = lay.here()
    W, T, D = lay.width, TREE_TOKENS, HEAD_SIZE
    frows = gate_ref.shape[0]
    hid = lay.lines * lay.cores * frows
    groups = KEY_VALUE_HEADS
    per = QUERY_HEADS // KEY_VALUE_HEADS
    kvw = KEY_VALUE_HEADS * D
    scale = D**-0.5
    x_other, c_other, r_other = 1 - x, 1 - c, 1 - r
    x_peer = lay.device(z, x_other, r, c)
    y_peer = lay.device(z, x, r, c_other)
    sibling = lay.device(z, x, r_other, c)
    planes = lay.line(z)
    inner = lay.inner(z)
    line = range(lay.planes)
    lanes = lambda cc: pl.ds(pl.multiple_of(cc * W, 128), W)
    links = Links(send_sems, recv_sems)
    send = links.send
    outgoing = []

    def put(source, dest):
        copy = pltpu.make_async_copy(source, dest, out_sems.at[len(outgoing)])
        copy.start()
        outgoing.append(copy)

    def block(zz, xx, rr):
        return ga.at[zz * lay.lines + xx, rr]

    half = frows // 2
    halves = (pl.ds(0, half), pl.ds(half, half))
    weights = lambda w: gf[w].reshape(hid, MODEL_WIDTH)

    peers = [lay.device(planes[p], x, r, c) for p in line[1:]] + [x_peer, y_peer, sibling]
    greet(peers)

    mine = block(z, x, r).at[:, lanes(c)]
    f_refs = (gate_ref, up_ref, down_ref)
    own = [
        pltpu.make_async_copy(q_ref, mine.at[pl.ds(0, lay.qrows), :], own_sems.at[0]),
        pltpu.make_async_copy(o_ref, mine.at[pl.ds(lay.out_at, lay.qrows), :], own_sems.at[1]),
        pltpu.make_async_copy(cot_ref, gdy.at[0], own_sems.at[2]),
    ]
    for w in range(3):
        own.append(pltpu.make_async_copy(f_refs[w], gf.at[w, x, r, :, lanes(c)], own_sems.at[3 + w]))
    for copy in own:
        copy.start()
    pad = jnp.zeros((lay.out_at - lay.kv_at - lay.kvrows, W), BF16)
    gfull[:, lanes(c)] = jnp.concatenate(
        [gain1_ref[...].reshape(1, W), gain2_ref[...].reshape(1, W), jnp.zeros((6, W), F32)], axis=0
    )
    mine[lay.kv_at : lay.out_at, :] = jnp.concatenate([kv_ref[...], pad], axis=0)
    if lay.arows > lay.out_at + lay.qrows:
        mine[lay.out_at + lay.qrows :, :] = jnp.zeros((lay.arows - lay.out_at - lay.qrows, W), BF16)

    greeted(peers)
    for copy in own[:2]:
        copy.wait()

    gain_y = send(gfull.at[:, lanes(c)], gfull.at[:, lanes(c)], y_peer)
    ax, ay, arx, ary, acore = {}, {}, {}, {}, {}

    def a_rows(part, first=0, rows=None):
        at, many = lay.parts[part]
        return pl.ds(at + first, many if rows is None else rows)

    def a_here(part, zz):
        return block(zz, x, r).at[a_rows(part), lanes(c)]

    a_line = [
        Line(lay, links, a_here(i, z), lambda p, i=i: a_here(i, planes[p]), a_here(i, z), a_here(i, z)) for i in range(2)
    ]
    dy_line = Line(lay, links, gdy.at[0], lambda p: gdy.at[p], gdy.at[1], gdy.at[3 - inner])
    n_line = []
    for rows in (pl.ds(0, T // 2), pl.ds(T // 2, T // 2)):
        n_line.append(
            Line(lay, links, gn.at[0, rows], lambda p, rows=rows: gn.at[p, rows], gn.at[1, rows], gn.at[3 - inner, rows])
        )
    d_line, y_line, n_sum = (LineSum(lay, links, landing) for landing in (d_in, y_in, nin.at[pl.ds(3, 3)]))
    g_line = [LineSum(lay, links, az_in.at[:, a_rows(i), :]) for i in range(2)]

    def a_own(i, k):
        if k:
            a_line[i].arrive(k)
        here = a_here(i, planes[k])
        ax[i, k] = send(here, here, x_peer, "ga")
        ay[i, k] = send(here, here, y_peer, "ga")

    def a_core(i, k, xx, j):
        rows = block(planes[k], xx, r).at[a_rows(i), :]
        acore[i, k, j] = send(rows, rows, sibling, "ga")

    def a_relay(i, k):
        ax[i, k].wait_recv()
        top = block(planes[k], x_other, r).at[a_rows(i, 0, lay.cuts[i]), lanes(c)]
        ary[i, k] = send(top, top, y_peer, "ga")
        ay[i, k].wait_recv()
        low = block(planes[k], x, r).at[a_rows(i, lay.cuts[i], lay.parts[i][1] - lay.cuts[i]), lanes(c_other)]
        arx[i, k] = send(low, low, x_peer, "ga")
        a_core(i, k, x, 0)

    def a_finish(i, k):
        ary[i, k].wait_recv()
        arx[i, k].wait_recv()
        a_core(i, k, x_other, 1)

    def a_unpack(i, k):
        acore[i, k, 0].wait_recv()
        acore[i, k, 1].wait_recv()
        zz = planes[k]
        heads = QUERY_HEADS // lay.cores
        dest = (wq, wo)[i]
        for rr in range(lay.cores):

            def pair(m, _):
                rows = pl.ds(pl.multiple_of(lay.parts[i][0] + m * 16, 16), 16)
                left = ga[zz * lay.lines, rr, rows, :].astype(F32)
                right = ga[zz * lay.lines + 1, rr, rows, :].astype(F32)
                at = (rr * heads + 2 * m) * D + zz * 16
                dest[pl.ds(pl.multiple_of(at, 16), 16), :] = jnp.concatenate([left[:8], right[:8]], axis=0).astype(BF16)
                dest[pl.ds(pl.multiple_of(at + D, 16), 16), :] = jnp.concatenate([left[8:], right[8:]], axis=0).astype(BF16)
                return 0

            lax.fori_loop(0, heads // 2, pair, 0)
            if i == 0:
                n = lay.kvrows
                left = ga[zz * lay.lines, rr, lay.kv_at : lay.out_at, :].astype(F32)
                right = ga[zz * lay.lines + 1, rr, lay.kv_at : lay.out_at, :].astype(F32)
                at = rr * kvw + zz * (2 * n)
                wkv[pl.ds(pl.multiple_of(at, 16), 2 * n), :] = jnp.concatenate([left[:n], right[:n]], axis=0).astype(BF16)

    a_own(0, 0)
    a_line[0].start()
    a_own(1, 0)

    stream = tok_ref[...].astype(F32)
    rstd1 = lax.rsqrt(jnp.sum(stream * stream, axis=1, keepdims=True) / MODEL_WIDTH + EPS)
    tree = r * lay.cols + c
    seg_row = jnp.broadcast_to(seg_ref[pl.ds(tree, 1), :].astype(F32), (T, T))
    par_row = par_ref[pl.ds(tree, 1), :].astype(F32)
    seg_col = jnp.transpose(seg_row)
    above = jnp.zeros((T, T), F32)
    for s in range(par_ref.shape[1]):
        above = jnp.where(seg_col == s, par_row[:, s : s + 1], above)
    row_at = lax.broadcasted_iota(jnp.int32, (T, T), 0)
    lane_at = lax.broadcasted_iota(jnp.int32, (T, T), 1)
    seen = (seg_row == seg_col) | (seg_row == above) | (seg_row == 0.0)
    allowed = jnp.where(seen & (row_at >= lane_at), 1.0, 0.0)
    depth = jnp.sum(allowed, axis=1, keepdims=True) - 1.0
    freq = lax.rem(lane_at, D // 2).astype(F32) * (2.0 / D)
    angle = depth * jnp.exp(freq * -math.log(THETA))
    rot_cos[...] = jnp.cos(angle)
    sine = jnp.sin(angle)
    rot_sin[...] = jnp.where(lax.rem(lane_at, D) < D // 2, -sine, sine)
    for copy in own[2:]:
        copy.wait()
    gain_y.wait_recv()
    normed[...] = (stream * rstd1 * gfull[0:1, :]).astype(BF16)

    def a_step(i, p):
        a_line[i].relay(p)

    fx, fy, frx, fry, fcore = {}, {}, {}, {}, {}

    def f_send(w):
        for h in range(2):
            here = gf.at[w, x, r, halves[h], lanes(c)]
            fx[w, h] = send(here, here, x_peer, "gf")
            fy[w, 1 - h] = send(gf.at[w, x, r, halves[1 - h], lanes(c)], gf.at[w, x, r, halves[1 - h], lanes(c)], y_peer, "gf")

    def f_relay(w):
        fx[w, 0].wait_recv()
        top = gf.at[w, x_other, r, halves[0], lanes(c)]
        fry[w] = send(top, top, y_peer, "gf")
        fy[w, 1].wait_recv()
        low = gf.at[w, x, r, halves[1], lanes(c_other)]
        frx[w] = send(low, low, x_peer, "gf")

    def f_core(w):
        fy[w, 0].wait_recv()
        fcore[w, 0] = send(gf.at[w, x, r], gf.at[w, x, r], sibling, "gf")

    def f_finish(w):
        fx[w, 1].wait_recv()
        fry[w].wait_recv()
        frx[w].wait_recv()
        fcore[w, 1] = send(gf.at[w, x_other, r], gf.at[w, x_other, r], sibling, "gf")

    def f_ready(w):
        fcore[w, 0].wait_recv()
        fcore[w, 1].wait_recv()

    allowed4 = jnp.concatenate([allowed] * per, axis=0) > 0.5

    def kv_project():
        kv = dot_nt(normed[...], wkv[...])
        turned = turn(kv, rot_cos[...], rot_sin[...])
        for g in range(groups):
            ks[g] = turned[:, g * D : (g + 1) * D].astype(BF16)
            vs[g] = kv[:, kvw + g * D : kvw + (g + 1) * D].astype(BF16)

    def forward(g):
        cols = slice(g * per * D, (g + 1) * per * D)
        pre = turn(dot_nt(normed[...], wq[cols, :]), rot_cos[...], rot_sin[...])
        qs[g] = stack_heads(pre, per).astype(BF16)
        scores = jnp.where(allowed4, dot_nt(qs[g], ks[g]) * scale, -1e30)
        weight = jnp.exp(scores - jnp.max(scores, axis=1, keepdims=True))
        share = weight / jnp.sum(weight, axis=1, keepdims=True)
        probs[g] = share
        mixed = dot_nn(share.astype(BF16), vs[g])
        mix[:, cols] = spread_heads(mixed, per).astype(BF16)

    def out_project():
        res = stream + dot_nn(mix[...], wo[...])
        resid[...] = res
        rstd2 = lax.rsqrt(jnp.sum(res * res, axis=1, keepdims=True) / MODEL_WIDTH + EPS)
        gn[0] = (res * rstd2 * gfull[1:2, :]).astype(BF16)

    def n_start():
        for part in n_line:
            part.start()

    def n_arrive(*positions):
        for part in n_line:
            for p in positions:
                part.arrive(p)

    def dy_arrive():
        for p in line[1:]:
            dy_line.arrive(p)

    n_rows = lay.planes * T
    dy_all = lambda: gdy[...].reshape(n_rows, MODEL_WIDTH)

    def hidden_back():
        d_act[...] = dot_nt(dy_all(), weights(2))

    def gates(first, last):
        gate_s[first * T : last * T, :] = dot_nt(gn[first:last].reshape((last - first) * T, MODEL_WIDTH), weights(0))

    def feed(first, last):
        count = (last - first) * T
        rows = slice(first * T, last * T)
        up = dot_nt(gn[first:last].reshape(count, MODEL_WIDTH), weights(1))
        gate = gate_s[rows, :]
        sig = 1.0 / (1.0 + jnp.exp(-gate))
        silu = gate * sig
        act[rows, :] = (silu * up).astype(BF16)
        da = d_act[rows, :]
        dup[rows, :] = (da * silu).astype(BF16)
        dgate[rows, :] = (da * up * sig * (1.0 + gate * (1.0 - sig))).astype(BF16)

    d_part = gdy

    def back(p):
        rows = pl.ds(pl.multiple_of(p * T, T), T)
        part = dot_nn(dgate[rows, :], weights(0)) + dot_nn(dup[rows, :], weights(1))
        d_part[p] = part.astype(BF16)

    def mirror(line_sum, terms, landing):
        line_sum.arrive(0)
        p = 3 - inner
        terms[p] = (terms[p].astype(F32) + landing[0].astype(F32)).astype(BF16)
        line_sum.send(2, terms.at[p])

    def release():
        links.flush("ga", "gf")
        for part in a_line:
            part.flush()

    fc, fs1a, fs1b, fs2a, fs2b = {}, {}, {}, {}, {}

    def fg(w):
        return (gate_grad, gf.at[1], down_grad)[w]

    def f_grad(w):
        n2 = gn[...].reshape(n_rows, MODEL_WIDTH)
        if w == 0:
            grad = dot_tn(dgate[...], n2)
        elif w == 1:
            grad = dot_tn(dup[...], n2)
        else:
            grad = dot_tn(act[...], dy_all())
        fg(w)[...] = grad.astype(BF16).reshape(lay.lines, lay.cores, frows, MODEL_WIDTH)
        for xx in (x_other, x):
            fc[w, xx is x] = send(fg(w).at[xx, r_other], fc_in.at[w, xx], sibling)

    def f_stage1(w):
        for xx in (x_other, x):
            fc[w, xx is x].wait_recv()
            add_into(fg(w).at[xx, r], fc_in.at[w, xx], 32)
            if xx is x_other:
                fs1a[w] = send(fg(w).at[xx, r, halves[0], :], f1a.at[w], x_peer)
            fs1b[w, xx is x] = send(fg(w).at[xx, r, halves[1], lanes(c_other)], f1b.at[w, xx], y_peer)

    def f_stage2(w):
        fs1a[w].wait_recv()
        add_into(fg(w).at[x, r, halves[0], :], f1a.at[w], 16)
        fs2a[w] = send(fg(w).at[x, r, halves[0], lanes(c_other)], f2a.at[w], y_peer)
        for xx in (x_other, x):
            fs1b[w, xx is x].wait_recv()
            add_into(fg(w).at[xx, r, halves[1], lanes(c)], f1b.at[w, xx], 16)
        fs2b[w] = send(fg(w).at[x_other, r, halves[1], lanes(c)], f2b.at[w], x_peer)

    f_out = [d_act.at[pl.ds(i * frows, frows), pl.ds(0, W)] for i in range(2)] + [gate_s.at[pl.ds(0, frows), pl.ds(0, W)]]

    def f_total(w, dest):
        fs2a[w].wait_recv()
        total = f_out[w]
        sum_into(total.at[halves[0], :], [fg(w).at[x, r, halves[0], lanes(c)], f2a.at[w]], 16)
        fs2b[w].wait_recv()
        sum_into(total.at[halves[1], :], [fg(w).at[x, r, halves[1], lanes(c)], f2b.at[w]], 16)
        put(total, dest)

    y_part = gn

    def y_terms():
        for part in n_line:
            part.flush()
        y_part[...] = dot_nn(act[...], weights(2)).astype(BF16).reshape(lay.planes, T, MODEL_WIDTH)

    def y_send():
        y_line.send(0, y_part.at[2 + inner])
        y_line.send(1, y_part.at[1])

    def y_total():
        y_line.arrive(1)
        y_line.arrive(2)
        y = resid[...] + y_part[0].astype(F32) + y_in[1].astype(F32) + y_in[2].astype(F32)
        out_ref[...] = y.astype(BF16)
        put(out_ref, out_hbm)

    kept = {}

    def residual_back():
        d_line.arrive(1)
        d_line.arrive(2)
        d_n2 = d_part[0].astype(F32) + d_in[1].astype(F32) + d_in[2].astype(F32)
        res = resid[...]
        rstd2 = lax.rsqrt(jnp.sum(res * res, axis=1, keepdims=True) / MODEL_WIDTH + EPS)
        gain2_grad = jnp.sum(d_n2 * res * rstd2, axis=0, keepdims=True)
        scaled2 = d_n2 * gfull[1:2, :]
        inner2 = jnp.sum(scaled2 * res, axis=1, keepdims=True)
        d_res = cot_ref[...].astype(F32) + rstd2 * scaled2 - res * (rstd2 * rstd2 * rstd2 * inner2 / MODEL_WIDTH)
        d_attn = d_res.astype(BF16)

        kept.update(d_res=d_res, d_attn=d_attn, gain2_grad=gain2_grad)

    def place_heads(source, other, base, rr):
        heads = QUERY_HEADS // lay.cores
        grad = dot_tn(source[:, pl.ds(pl.multiple_of(rr * heads * D, 128), heads * D)], other)
        for m in range(heads // 2):
            at = 2 * m * D
            for dp in range(lay.dp):
                tile = jnp.concatenate([grad[at + dp * 8 : at + dp * 8 + 8], grad[at + D + dp * 8 : at + D + dp * 8 + 8]], axis=0)
                ga[dp, rr, base + m * 16 : base + m * 16 + 16, :] = tile.astype(BF16)

    to_plane = (planes[2] + inner * (planes[3] - planes[2]), planes[3] + inner * (planes[2] - planes[3]), planes[1], z)
    ac, as1a, as1b, as2a, as2b = {}, {}, {}, {}, {}

    def a_pair(zz, rr, rows):
        return ga.at[pl.ds(zz * lay.lines, lay.lines), rr, rows]

    def a_core_sums(i):
        for t in line:
            ac[i, t] = send(a_pair(to_plane[t], r_other, a_rows(i)), ac_in.at[t, :, a_rows(i), :], sibling)

    def ends(i):
        return a_rows(i, 0, lay.cuts[i]), a_rows(i, lay.cuts[i], lay.parts[i][1] - lay.cuts[i])

    def landed(i):
        tops, lows = lay.cuts[0] * i, (lay.parts[0][1] - lay.cuts[0]) * i
        return pl.ds(tops, lay.cuts[i]), pl.ds(lows, lay.parts[i][1] - lay.cuts[i])

    def a_stage1(i, t):
        top, low = ends(i)
        top_in, low_in = landed(i)
        zz = to_plane[t]
        ac[i, t].wait_recv()
        for xx in range(lay.lines):
            add_into(block(zz, xx, r).at[a_rows(i), :], ac_in.at[t, xx, a_rows(i), :], 16)
        as1a[i, t] = send(block(zz, x_other, r).at[top, :], a1a.at[t, top_in, :], x_peer)
        as1b[i, t] = send(a_pair(zz, r, low).at[:, :, lanes(c_other)], a1b.at[t, :, low_in, :], y_peer)

    def a_stage2(i, t):
        top, low = ends(i)
        top_in, low_in = landed(i)
        zz = to_plane[t]
        as1a[i, t].wait_recv()
        add_into(block(zz, x, r).at[top, :], a1a.at[t, top_in, :], 16)
        as2a[i, t] = send(block(zz, x, r).at[top, lanes(c_other)], a2.at[t, top, :], y_peer)
        as1b[i, t].wait_recv()
        for xx in range(lay.lines):
            add_into(block(zz, xx, r).at[low, lanes(c)], a1b.at[t, xx, low_in, :], 16)
        as2b[i, t] = send(block(zz, x_other, r).at[low, lanes(c)], a2.at[t, low, :], x_peer)

    def a_line_sum(i, t):
        here = a_here(i, to_plane[t])
        as2a[i, t].wait_recv()
        as2b[i, t].wait_recv()
        add_into(here, a2.at[t, a_rows(i), :], 16)
        if t in (0, 2):
            g_line[i].send((0, 2, 1)[t], here)

    def a_mirror(i):
        here = a_here(i, to_plane[1])
        g_line[i].arrive(0)
        add_into(here, az_in.at[0, a_rows(i), :], 16)
        g_line[i].send(2, here)

    a_out = gate_s.at[pl.ds(frows, lay.arows), pl.ds(0, W)]

    def a_total(i):
        g_line[i].arrive(1)
        g_line[i].arrive(2)
        parts = [a_here(i, z), az_in.at[1, a_rows(i), :], az_in.at[2, a_rows(i), :]]
        sum_into(a_out.at[a_rows(i), :], parts, 16)
        if i == 0:
            put(a_out.at[pl.ds(0, lay.qrows), :], q_hbm)
            put(a_out.at[pl.ds(lay.kv_at, lay.kvrows), :], kv_hbm)
        else:
            put(a_out.at[pl.ds(lay.out_at, lay.qrows), :], o_hbm)

    def backward(g):
        cols = slice(g * per * D, (g + 1) * per * D)
        dms = stack_heads(dot_nt(kept["d_attn"], wo[cols, :]), per).astype(BF16)
        share = probs[g]
        dp_ = dot_nt(dms, vs[g])
        delta = jnp.sum(share * dp_, axis=1, keepdims=True)
        ds_ = (share * (dp_ - delta)).astype(BF16)
        d_query = spread_heads(dot_nn(ds_, ks[g]) * scale, per)
        dq[:, cols] = turn(d_query, rot_cos[...], -rot_sin[...]).astype(BF16)
        dk5[g] = dot_tn(ds_, qs[g]) * scale
        dv5[g] = dot_tn(share.astype(BF16), dms)

    def keys_back():
        zeros = jnp.zeros((T, D), F32)
        dk_all = jnp.concatenate([dk5[g] for g in range(groups)] + [zeros], axis=1)
        dkv[0] = turn(dk_all, rot_cos[...], -rot_sin[...])[:, :kvw].astype(BF16)
        dkv[1] = jnp.concatenate([dv5[g] for g in range(groups)], axis=1).astype(BF16)


    def place_kv(rr):
        grad = dot_tn(dkv[rr], normed[...])
        pad = jnp.zeros((lay.out_at - lay.kv_at - lay.kvrows, MODEL_WIDTH), F32)
        for dp in range(lay.dp):
            tile = jnp.concatenate([grad[dp * lay.kvrows : (dp + 1) * lay.kvrows], pad], axis=0)
            ga[dp, rr, lay.kv_at : lay.out_at, :] = tile.astype(BF16)

    def input_back():
        d_normed = dot_nn(dq[...], wq[...]) + dot_nn(dkv[0], wkv[:kvw, :]) + dot_nn(dkv[1], wkv[kvw:, :])
        rows = tok_ref[...].astype(F32)
        rstd = lax.rsqrt(jnp.sum(rows * rows, axis=1, keepdims=True) / MODEL_WIDTH + EPS)
        gain1_grad = jnp.sum(d_normed * rows * rstd, axis=0, keepdims=True)
        nsum[0] = jnp.concatenate([gain1_grad, kept["gain2_grad"], jnp.zeros((6, MODEL_WIDTH), F32)], axis=0)
        scaled1 = d_normed * gfull[0:1, :]
        inner1 = jnp.sum(scaled1 * rows, axis=1, keepdims=True)
        in_grad = kept["d_res"] + rstd * scaled1 - rows * (rstd * rstd * rstd * inner1 / MODEL_WIDTH)
        in_grad_ref[...] = in_grad.astype(BF16)
        put(in_grad_ref, in_grad_hbm)
        kept["gains"] = send(nsum.at[0], nin.at[0], sibling)

    def gains_core():
        kept["gains"].wait_recv()
        nsum[1] = nsum[0] + nin[0]
        n_sum.send(0, nsum.at[1])

    def gains_side():
        n_sum.arrive(0)
        nsum[2] = nsum[1] + nin[3]
        n_sum.send(2, nsum.at[2])

    def gains_mirror():
        n_sum.arrive(2)
        nsum[3] = nsum[2] + nin[5]
        kept["gains"] = send(nsum.at[3], nin.at[1], x_peer)

    def gains_x():
        kept["gains"].wait_recv()
        nsum[4] = nsum[3] + nin[1]
        kept["gains"] = send(nsum.at[4], nin.at[2], y_peer)

    def gains_y():
        kept["gains"].wait_recv()
        nsum[5] = nsum[4] + nin[2]
        gain_out[...] = nsum[5, :, lanes(c)]
        put(gain_out, gain_hbm)

    a_step(0, 2)
    a_line[1].start()
    a_own(0, 1)
    a_relay(0, 0)
    a_step(0, 3)
    a_relay(0, 1)
    dy_line.start()
    a_own(0, 2)
    a_step(1, 3)
    a_step(1, 2)
    a_own(0, 3)
    a_relay(0, 2)
    a_own(1, 1)
    dy_line.relay(2)
    a_relay(1, 0)
    a_relay(0, 3)
    a_own(1, 3)
    a_finish(0, 1)
    a_finish(0, 2)
    a_own(1, 2)
    a_unpack(0, 1)
    dy_line.relay(3)
    a_finish(0, 3)
    a_finish(0, 0)
    a_relay(1, 1)
    a_finish(1, 0)
    a_unpack(0, 2)
    a_relay(1, 2)
    a_relay(1, 3)
    a_unpack(0, 0)
    a_unpack(0, 3)
    a_finish(1, 1)
    kv_project()
    f_send(0)
    a_unpack(1, 1)
    a_finish(1, 2)
    a_unpack(1, 0)
    f_send(2)
    forward(3)
    a_finish(1, 3)
    a_unpack(1, 2)
    forward(1)
    forward(4)
    forward(0)
    a_unpack(1, 3)
    forward(2)
    out_project()
    n_start()
    f_relay(2)
    f_send(1)
    f_relay(0)
    n_line[0].relay(2)
    f_core(0)
    f_finish(2)
    n_line[1].relay(2)
    dy_arrive()
    f_relay(1)
    n_line[0].relay(3)
    f_core(2)
    n_arrive(1, 2)
    f_ready(2)
    f_core(1)
    n_line[1].relay(3)
    f_finish(0)
    hidden_back()
    f_ready(0)
    f_finish(1)
    n_arrive(3)
    gates(0, 3)
    gates(3, 4)
    f_ready(1)
    feed(0, 4)
    f_grad(2)
    dy_line.flush()
    back(2 + inner)
    d_line.send(0, d_part.at[2 + inner])
    back(3 - inner)
    f_stage1(2)
    f_grad(0)
    back(1)
    f_stage1(0)
    d_line.send(1, d_part.at[1])
    mirror(d_line, d_part, d_in)
    back(0)
    release()
    f_grad(1)
    f_stage1(1)
    f_stage2(2)
    f_stage2(0)
    f_stage2(1)
    y_terms()
    y_send()
    residual_back()
    place_heads(mix, kept["d_attn"], lay.out_at, r)
    place_heads(mix, kept["d_attn"], lay.out_at, r_other)
    a_core_sums(1)
    backward(1)
    backward(4)
    a_stage1(1, 0)
    backward(0)
    a_stage1(1, 2)
    backward(2)
    backward(3)
    keys_back()
    a_stage2(1, 0)
    place_kv(r_other)
    mirror(y_line, y_part, y_in)
    a_stage1(1, 1)
    place_heads(dq, normed[...], 0, r_other)
    f_total(0, gate_hbm)
    place_heads(dq, normed[...], 0, r)
    a_core_sums(0)
    a_stage2(1, 2)
    a_line_sum(1, 0)
    place_kv(r)
    a_stage1(0, 0)
    a_stage1(0, 1)
    input_back()
    gains_core()
    a_stage2(0, 0)
    a_stage2(1, 1)
    a_line_sum(1, 2)
    a_stage1(0, 2)
    a_stage1(1, 3)
    a_line_sum(1, 1)
    gains_side()
    a_stage2(0, 1)
    a_mirror(1)
    f_total(1, up_hbm)
    a_line_sum(0, 0)
    a_stage2(0, 2)
    a_stage1(0, 3)
    a_stage2(1, 3)
    f_total(2, down_hbm)
    y_total()
    a_line_sum(0, 1)
    gains_mirror()
    a_mirror(0)
    a_line_sum(0, 2)
    a_stage2(0, 3)
    gains_x()
    a_line_sum(1, 3)
    a_line_sum(0, 3)
    a_total(1)
    a_total(0)
    gains_y()
    links.flush()
    for part in [d_line, y_line, n_sum] + g_line:
        part.flush()
    for copy in outgoing:
        copy.wait()


def whole_layer(lay, blocks, tokens, cotangent, gains, seg_ids, parents):
    vm = lambda *shape: pltpu.VMEM(shape, BF16)
    vf = lambda *shape: pltpu.VMEM(shape, F32)
    M, T, D, W = MODEL_WIDTH, TREE_TOKENS, HEAD_SIZE, lay.width
    frows = blocks[3].shape[0]
    hid = lay.lines * lay.cores * frows
    G, per = KEY_VALUE_HEADS, QUERY_HEADS // KEY_VALUE_HEADS
    n, nl, half = lay.planes, lay.lines, frows // 2
    vmem, hbm = pl.BlockSpec(memory_space=pltpu.VMEM), pl.BlockSpec(memory_space=pl.ANY)
    count = 200
    scratch = [
        vm(lay.dp, lay.cores, lay.arows, M),
        vm(3, nl, lay.cores, frows, M),
        vm(QUERY_HEADS * D, M),
        vm(2 * G * D, M),
        vm(QUERY_HEADS * D, M),
        vm(n, T, M),
        vm(n, T, M),
        vm(n * T, hid),
        vm(n * T, hid),
        vm(n * T, hid),
        vf(n * T, hid),
        vf(n * T, hid),
        vm(nl, lay.cores, frows, M),
        vm(nl, lay.cores, frows, M),
        vf(8, M),
        vm(T, M),
        vm(G, per * T, D),
        vm(G, T, D),
        vm(G, T, D),
        vf(G, per * T, T),
        vm(T, M),
        vf(T, M),
        vf(T, T),
        vf(T, T),
        vm(T, M),
        vm(2, T, G * D),
        vf(G, T, D),
        vf(G, T, D),
        vm(n - 1, T, M),
        vm(n - 1, T, M),
        vm(3, nl, frows, M),
        vm(3, half, M),
        vm(3, nl, half, W),
        vm(3, half, W),
        vm(3, half, W),
        vm(n, nl, lay.arows, M),
        vm(n, sum(lay.cuts), M),
        vm(n, nl, lay.arows - sum(lay.cuts), W),
        vm(n, lay.arows, W),
        vm(n - 1, lay.arows, W),
        vf(6, 8, M),
        vf(2 + n, 8, M),
        vm(T, M),
        vm(T, M),
        vf(8, W),
        pltpu.SemaphoreType.DMA((count,)),
        pltpu.SemaphoreType.DMA((count,)),
        pltpu.SemaphoreType.DMA((6,)),
        pltpu.SemaphoreType.DMA((9,)),
    ]
    return pl.pallas_call(
        functools.partial(layer_kernel, lay),
        out_shape=(
            jax.ShapeDtypeStruct((T, M), BF16),
            jax.ShapeDtypeStruct((T, M), BF16),
            jax.ShapeDtypeStruct((8, W), F32),
        )
        + tuple(jax.ShapeDtypeStruct(b.shape, F32) for b in blocks),
        in_specs=[hbm, vmem, hbm, hbm, hbm, hbm] + [vmem] * 6,
        out_specs=(hbm,) * 9,
        scratch_shapes=scratch,
        compiler_params=pltpu.CompilerParams(collective_id=0, has_side_effects=True, vmem_limit_bytes=63 * 2**20),
        name="whole_layer",
    )(*blocks, tokens, cotangent, *gains, seg_ids, parents)


def finish_kernel(count, *refs):
    sources, results, held = refs[:count], refs[count : 2 * count + 1], refs[2 * count + 1 : 3 * count + 1]
    into, back = refs[3 * count + 1 :]
    first = [pltpu.make_async_copy(sources[i], held[i], into.at[i]) for i in range(count)]
    last = [pltpu.make_async_copy(held[i], results[i], back.at[i]) for i in range(count - 1)]
    for copy in first:
        copy.start()
    for i in range(count - 1):
        first[i].wait()
        last[i].start()
    first[-1].wait()
    for i in range(2):
        results[count - 1 + i][...] = held[-1][i]
    for copy in last:
        copy.wait()


def finish(results, gain_rows):
    hbm = pl.BlockSpec(memory_space=pl.ANY)
    vmem = pl.BlockSpec(memory_space=pltpu.VMEM)
    given = (*results, gain_rows)
    count = len(given)
    dma = pltpu.SemaphoreType.DMA((count,))
    vector = jax.ShapeDtypeStruct((gain_rows.shape[1],), gain_rows.dtype)
    return pl.pallas_call(
        functools.partial(finish_kernel, count),
        out_shape=tuple(jax.ShapeDtypeStruct(v.shape, v.dtype) for v in results) + (vector, vector),
        in_specs=[hbm] * count,
        out_specs=(hbm,) * len(results) + (vmem, vmem),
        scratch_shapes=[pltpu.VMEM(v.shape, v.dtype) for v in given] + [dma, dma],
        name="finish",
    )(*given)


def body(lay, tokens, cotangent, seg_ids, parents, norm1_gain, w_query, key_value_weight, w_out, norm2_gain, w_gate, w_up, w_down):
    W = lay.width
    blocks = (
        jnp.transpose(w_query, (1, 2, 0)).reshape(lay.qrows, W),
        jnp.transpose(key_value_weight[:, 0, :]),
        w_out.reshape(lay.qrows, W),
        w_gate.T,
        w_up.T,
        w_down,
    )
    layer_out, in_grad, gain_sum, query, keyval, out, gate, up, down = whole_layer(
        lay, blocks, tokens, cotangent, (norm1_gain, norm2_gain), seg_ids, parents
    )
    layer_out, in_grad, query, keyval, out, gate, up, down, gain1_grad, gain2_grad = finish(
        (layer_out, in_grad, query, keyval, out, gate, up, down), gain_sum
    )
    heads = QUERY_HEADS // lay.cores
    shape = (heads, HEAD_SIZE // lay.dp, W)
    return (
        layer_out,
        in_grad,
        gain1_grad,
        jnp.transpose(query.reshape(shape), (2, 0, 1)),
        keyval.T[:, None, :],
        out.reshape(shape),
        gain2_grad,
        gate.T,
        up.T,
        down,
    )


def general_layout(segment, parent):
    labels = jnp.arange(SEGS, dtype=jnp.int32)
    member = (segment[:, None] == labels[None, :]).astype(jnp.float32)
    link = ((parent[:, None] == labels[None, :]) & (labels[:, None] > 0)).astype(jnp.float32)
    ident = jnp.eye(SEGS, dtype=jnp.float32)

    def climb(level, reach):
        return ident + jnp.dot(link, reach, precision=lax.Precision.HIGHEST)

    reach = lax.fori_loop(0, SEGS, climb, ident)
    visible = jnp.dot(jnp.dot(member, reach, precision=lax.Precision.HIGHEST), member.T, precision=lax.Precision.HIGHEST) > 0.5
    places = jnp.arange(segment.shape[0], dtype=jnp.int32)
    allowed = visible & (places[:, None] >= places[None, :])
    sizes = jnp.sum(member, axis=0)
    earlier = (labels[None, :] < labels[:, None]).astype(jnp.float32)
    starts = jnp.dot(earlier, sizes, precision=lax.Precision.HIGHEST)
    above = jnp.dot(reach, sizes, precision=lax.Precision.HIGHEST) - sizes
    tree_depth = places.astype(jnp.float32) + jnp.dot(member, above - starts, precision=lax.Precision.HIGHEST)
    return (allowed, tree_depth)


def general_rotate(value_rows, tree_depth, sign):
    half = value_rows.shape[-1] // 2
    freqs = jnp.arange(half, dtype=jnp.float32) * (2.0 / value_rows.shape[-1])
    inverse = jnp.exp(freqs * -math.log(THETA))
    angle = tree_depth[:, None] * inverse[None, :]
    cosine = jnp.cos(angle)[:, None, :]
    sine = sign * jnp.sin(angle)[:, None, :]
    first = value_rows[..., :half]
    second = value_rows[..., half:]
    return jnp.concatenate(
        [first * cosine - second * sine, second * cosine + first * sine], axis=-1
    )


def product(left, right):
    return jnp.dot(left, right, preferred_element_type=jnp.float32)


def general_body(
    tokens,
    cotangent,
    seg_ids,
    parents,
    norm1_gain,
    w_query,
    key_value_weight,
    w_out,
    norm2_gain,
    w_gate,
    w_up,
    w_down,
):
    columns = lax.axis_size("col")
    row_index = lax.axis_index("row")
    col_index = lax.axis_index("col")
    feature_width = MODEL_WIDTH // columns
    half_rows = columns * TREE_TOKENS // 2
    heads_here = QUERY_HEADS // 2
    query_total_width = heads_here * HEAD_SIZE
    heads_per_group = QUERY_HEADS // KEY_VALUE_HEADS
    scale = HEAD_SIZE ** (-0.5)
    stream_rows, cot_rows = (
        lax.all_to_all(tokens, "col", split_axis=1, concat_axis=0, tiled=True),
        lax.all_to_all(cotangent, "col", split_axis=1, concat_axis=0, tiled=True),
    )

    def col_total(value_rows):
        return lax.psum(value_rows, "col")

    def gather_rows(value_rows):
        return lax.all_gather(value_rows, "row", axis=0, tiled=True)

    def gather_cols(value_rows):
        return lax.all_gather(value_rows, "col", axis=0, tiled=True)

    def col_reduce(term, rows):
        return lax.psum_scatter(
            term(jnp.int32(0), rows * lax.axis_size("col")), "col", scatter_dimension=0, tiled=True
        )

    def row_reduce(term, rows):
        return lax.psum_scatter(
            term(jnp.int32(0), rows * lax.axis_size("row")), "row", scatter_dimension=0, tiled=True
        )

    def fetch():
        blocks = (
            lax.all_gather(w_query, "dp", axis=2, tiled=True),
            lax.all_gather(key_value_weight, "dp", axis=2, tiled=True),
            lax.all_gather(w_out, "dp", axis=1, tiled=True),
            lax.all_gather(w_gate, "dp", axis=1, tiled=True),
            lax.all_gather(w_up, "dp", axis=1, tiled=True),
            lax.all_gather(w_down, "dp", axis=0, tiled=True),
        )
        wide = None
        return (blocks, wide)

    def local_heads(pair_part):
        spread_heads = jnp.repeat(pair_part, heads_per_group, axis=1)
        return lax.dynamic_slice_in_dim(spread_heads, row_index * heads_here, heads_here, 1)

    def fold_heads(grad_here):
        spread_heads = jnp.zeros((TREE_TOKENS, QUERY_HEADS, HEAD_SIZE), jnp.float32)
        spread_heads = lax.dynamic_update_slice_in_dim(
            spread_heads, grad_here, row_index * heads_here, 1
        )
        return jnp.sum(
            spread_heads.reshape(TREE_TOKENS, KEY_VALUE_HEADS, heads_per_group, HEAD_SIZE), axis=2
        )

    gradients = (
        jnp.zeros((feature_width,), jnp.float32),
        jnp.zeros((feature_width, heads_here, HEAD_SIZE), jnp.float32),
        jnp.zeros((feature_width, 1, KEY_VALUE_HEADS * HEAD_SIZE), jnp.float32),
        jnp.zeros((heads_here, HEAD_SIZE, feature_width), jnp.float32),
        jnp.zeros((feature_width,), jnp.float32),
        jnp.zeros((feature_width, w_gate.shape[1] * lax.axis_size("dp")), jnp.float32),
        jnp.zeros((feature_width, w_up.shape[1] * lax.axis_size("dp")), jnp.float32),
        jnp.zeros((w_down.shape[0] * lax.axis_size("dp"), feature_width), jnp.float32),
    )
    results = []
    input_grads = []
    for batch_index in range(2):
        blocks, wide = fetch()
        (
            forward_query_block,
            forward_key_value_block,
            forward_out_block,
            forward_gate_block,
            forward_up_block,
            forward_down_block,
        ) = blocks
        forward_query_matrix = forward_query_block.reshape(feature_width, query_total_width)
        forward_key_value_matrix = forward_key_value_block.reshape(
            feature_width, KEY_VALUE_HEADS * HEAD_SIZE
        )
        forward_out_matrix = forward_out_block.reshape(query_total_width, feature_width)
        forward_stream = lax.dynamic_slice_in_dim(
            stream_rows, batch_index * half_rows, half_rows, 0
        ).astype(jnp.float32)
        forward_rstd1 = lax.rsqrt(
            col_total(jnp.sum(forward_stream * forward_stream, axis=1)) / MODEL_WIDTH + EPS
        )
        normed = (forward_stream * forward_rstd1[:, None] * norm1_gain).astype(jnp.bfloat16)
        forward_normed_all = gather_rows(normed)

        def qkv_term(start, count):
            return jnp.concatenate(
                [
                    product(forward_normed_all, forward_query_matrix),
                    product(forward_normed_all, forward_key_value_matrix),
                ],
                axis=1,
            )

        projected_rows = col_reduce(qkv_term, TREE_TOKENS)
        half_cols = columns // 2
        tree_slot = (
            col_index // half_cols * (2 * half_cols)
            + batch_index * half_cols
            + col_index % half_cols
        )
        segment = lax.dynamic_index_in_dim(seg_ids, tree_slot, 0, keepdims=False)
        parent = lax.dynamic_index_in_dim(parents, tree_slot, 0, keepdims=False)
        forward_allowed, forward_tree_depth = general_layout(segment, parent)
        query_pre = projected_rows[:, :query_total_width].reshape(
            TREE_TOKENS, heads_here, HEAD_SIZE
        )
        forward_query = general_rotate(query_pre, forward_tree_depth, 1.0).astype(jnp.bfloat16)
        own_unrotated = projected_rows[:, query_total_width:].reshape(
            TREE_TOKENS, KEY_VALUE_HEADS, HEAD_SIZE
        )
        own_part = jnp.where(
            row_index == 0, general_rotate(own_unrotated, forward_tree_depth, 1.0), own_unrotated
        ).astype(jnp.bfloat16)
        forward_pair = lax.all_gather(own_part[:, None], "row", axis=1, tiled=True)
        forward_keys_here = local_heads(forward_pair[:, 0])
        forward_values_here = local_heads(forward_pair[:, 1])
        forward_scores = (
            jnp.einsum(
                "qhd,khd->hqk", forward_query, forward_keys_here, preferred_element_type=jnp.float32
            )
            * scale
        )
        forward_masked = jnp.where(forward_allowed[None], forward_scores, -1e30)
        row_max = jnp.max(forward_masked, axis=-1, keepdims=True)
        forward_total = (
            jnp.log(jnp.sum(jnp.exp(forward_masked - row_max), axis=-1, keepdims=True)) + row_max
        )
        probs = jnp.exp(forward_masked - forward_total).astype(jnp.bfloat16)
        mixed = jnp.einsum(
            "hqk,khd->qhd", probs, forward_values_here, preferred_element_type=jnp.float32
        )
        mixed = mixed.astype(jnp.bfloat16).reshape(TREE_TOKENS, query_total_width)
        forward_mixed_all = gather_cols(mixed)

        def out_term(start, count):
            return product(forward_mixed_all, forward_out_matrix)

        forward_resid = forward_stream + row_reduce(out_term, half_rows)
        forward_rstd2 = lax.rsqrt(
            col_total(jnp.sum(forward_resid * forward_resid, axis=1)) / MODEL_WIDTH + EPS
        )
        normed2 = (forward_resid * forward_rstd2[:, None] * norm2_gain).astype(jnp.bfloat16)
        normed2_all = gather_rows(normed2)
        forward_hidden_here = forward_gate_block.shape[1]

        def gate_term(start, count):
            return jnp.concatenate(
                [product(normed2_all, forward_gate_block), product(normed2_all, forward_up_block)],
                axis=1,
            )

        gate_up = col_reduce(gate_term, TREE_TOKENS)
        forward_gate = gate_up[:, :forward_hidden_here]
        forward_up_part = gate_up[:, forward_hidden_here:]
        hidden = (jax.nn.silu(forward_gate) * forward_up_part).astype(jnp.bfloat16)
        forward_hidden_all = gather_cols(hidden)

        def down_term(start, count):
            return product(forward_hidden_all, forward_down_block)

        result = (forward_resid + row_reduce(down_term, half_rows)).astype(jnp.bfloat16)
        forward_saved = (
            forward_stream,
            forward_rstd1,
            forward_normed_all,
            forward_query,
            forward_pair,
            forward_total,
            forward_allowed,
            forward_tree_depth,
            forward_mixed_all,
            forward_resid,
            forward_rstd2,
            normed2_all,
            forward_gate,
            forward_up_part,
            forward_hidden_all,
        )
        result, saved = (result, forward_saved)
        blocks, wide = fetch()
        backward_gradients = gradients
        query_block, key_value_block, out_block, gate_block, up_block, down_block = blocks
        (
            stream,
            rstd1,
            normed_all,
            query,
            pair,
            total,
            allowed,
            tree_depth,
            mixed_all,
            resid,
            rstd2,
            kept_features,
            gate,
            up_part,
            hidden_all,
        ) = saved
        query_matrix = query_block.reshape(feature_width, query_total_width)
        key_value_matrix = key_value_block.reshape(feature_width, KEY_VALUE_HEADS * HEAD_SIZE)
        out_matrix = out_block.reshape(query_total_width, feature_width)
        hidden_here = gate_block.shape[1]
        cot_low = lax.dynamic_slice_in_dim(cot_rows, batch_index * half_rows, half_rows, 0)
        cot_full = cot_low.astype(jnp.float32)
        cot_all = gather_rows(cot_low)
        down_grad = jnp.einsum("tf,td->fd", hidden_all, cot_all, preferred_element_type=jnp.float32)

        def hidden_term(start, count):
            return jnp.einsum("td,fd->tf", cot_all, down_block, preferred_element_type=jnp.float32)

        d_hidden = col_reduce(hidden_term, TREE_TOKENS)
        sigmoid_gate = jax.nn.sigmoid(gate)
        d_up = (d_hidden * gate * sigmoid_gate).astype(jnp.bfloat16)
        d_gate = (d_hidden * up_part * sigmoid_gate * (1.0 + gate * (1.0 - sigmoid_gate))).astype(
            jnp.bfloat16
        )
        d_both = gather_cols(jnp.concatenate([d_gate, d_up], axis=1))
        gate_grad = jnp.einsum(
            "td,tf->df", kept_features, d_both[:, :hidden_here], preferred_element_type=jnp.float32
        )
        up_grad = jnp.einsum(
            "td,tf->df", kept_features, d_both[:, hidden_here:], preferred_element_type=jnp.float32
        )

        def back2_term(start, count):
            first = jnp.einsum(
                "tf,df->td", d_both[:, :hidden_here], gate_block, preferred_element_type=jnp.float32
            )
            return first + jnp.einsum(
                "tf,df->td", d_both[:, hidden_here:], up_block, preferred_element_type=jnp.float32
            )

        d_normed2 = row_reduce(back2_term, half_rows)
        scaled2 = d_normed2 * norm2_gain
        gain2_grad = jnp.sum(d_normed2 * resid * rstd2[:, None], axis=0)
        inner2 = col_total(jnp.sum(scaled2 * resid, axis=1))
        d_resid = (
            cot_full
            + rstd2[:, None] * scaled2
            - resid * (rstd2 * rstd2 * rstd2 * inner2 / MODEL_WIDTH)[:, None]
        )
        d_attn_all = gather_rows(d_resid.astype(jnp.bfloat16))
        out_grad = jnp.einsum(
            "tq,td->qd", mixed_all, d_attn_all, preferred_element_type=jnp.float32
        )

        def mixed_term(start, count):
            return jnp.einsum(
                "td,qd->tq", d_attn_all, out_matrix, preferred_element_type=jnp.float32
            )

        d_mixed = (
            col_reduce(mixed_term, TREE_TOKENS)
            .astype(jnp.bfloat16)
            .reshape(TREE_TOKENS, heads_here, HEAD_SIZE)
        )
        keys_here = local_heads(pair[:, 0])
        values_here = local_heads(pair[:, 1])
        scores = (
            jnp.einsum("qhd,khd->hqk", query, keys_here, preferred_element_type=jnp.float32) * scale
        )
        masked = jnp.where(allowed[None], scores, -1e30)
        probs_full = jnp.exp(masked - total)
        probs_low = probs_full.astype(jnp.bfloat16)
        d_probs = jnp.einsum(
            "qhd,khd->hqk", d_mixed, values_here, preferred_element_type=jnp.float32
        )
        delta = jnp.sum(probs_full * d_probs, axis=-1, keepdims=True)
        d_scores = (probs_full * (d_probs - delta)).astype(jnp.bfloat16)
        d_query = (
            jnp.einsum("hqk,khd->qhd", d_scores, keys_here, preferred_element_type=jnp.float32)
            * scale
        )
        d_keys = (
            jnp.einsum("hqk,qhd->khd", d_scores, query, preferred_element_type=jnp.float32) * scale
        )
        d_values = jnp.einsum(
            "hqk,qhd->khd", probs_low, d_mixed, preferred_element_type=jnp.float32
        )
        d_pair = jnp.stack([fold_heads(d_keys), fold_heads(d_values)], axis=1)
        own_gradient = lax.psum_scatter(
            d_pair.astype(jnp.bfloat16), "row", scatter_dimension=1, tiled=True
        ).astype(jnp.float32)[:, 0]
        own_gradient = jnp.where(
            row_index == 0, general_rotate(own_gradient, tree_depth, -1.0), own_gradient
        )
        query_pre_gradient = general_rotate(d_query, tree_depth, -1.0)
        d_proj = jnp.concatenate(
            [
                query_pre_gradient.reshape(TREE_TOKENS, query_total_width),
                own_gradient.reshape(TREE_TOKENS, KEY_VALUE_HEADS * HEAD_SIZE),
            ],
            axis=1,
        ).astype(jnp.bfloat16)
        d_proj_all = gather_cols(d_proj)
        query_grad = jnp.einsum(
            "td,tq->dq",
            normed_all,
            d_proj_all[:, :query_total_width],
            preferred_element_type=jnp.float32,
        )
        keyval_grad = jnp.einsum(
            "td,tq->dq",
            normed_all,
            d_proj_all[:, query_total_width:],
            preferred_element_type=jnp.float32,
        )
        in_matrix = jnp.concatenate([query_matrix, key_value_matrix], axis=1)

        def back1_term(start, count):
            return jnp.einsum(
                "tq,dq->td", d_proj_all, in_matrix, preferred_element_type=jnp.float32
            )

        d_normed = row_reduce(back1_term, half_rows)
        scaled1 = d_normed * norm1_gain
        gain1_grad = jnp.sum(d_normed * stream * rstd1[:, None], axis=0)
        inner1 = col_total(jnp.sum(scaled1 * stream, axis=1))
        d_stream = (
            d_resid
            + rstd1[:, None] * scaled1
            - stream * (rstd1 * rstd1 * rstd1 * inner1 / MODEL_WIDTH)[:, None]
        )
        updates = (
            gain1_grad,
            query_grad.reshape(query_block.shape),
            keyval_grad.reshape(key_value_block.shape),
            out_grad.reshape(out_block.shape),
            gain2_grad,
            gate_grad,
            up_grad,
            down_grad,
        )
        backward_gradients = tuple((a + b for a, b in zip(backward_gradients, updates)))
        d_stream, gradients = (d_stream.astype(jnp.bfloat16), backward_gradients)
        results.append(result)
        input_grads.append(d_stream)
    shards = (
        lax.psum_scatter(
            gradients[1].astype(jnp.bfloat16), "dp", scatter_dimension=2, tiled=True
        ).astype(jnp.float32),
        lax.psum_scatter(
            gradients[2].astype(jnp.bfloat16), "dp", scatter_dimension=2, tiled=True
        ).astype(jnp.float32),
        lax.psum_scatter(
            gradients[3].astype(jnp.bfloat16), "dp", scatter_dimension=1, tiled=True
        ).astype(jnp.float32),
        lax.psum_scatter(
            gradients[5].astype(jnp.bfloat16), "dp", scatter_dimension=1, tiled=True
        ).astype(jnp.float32),
        lax.psum_scatter(
            gradients[6].astype(jnp.bfloat16), "dp", scatter_dimension=1, tiled=True
        ).astype(jnp.float32),
        lax.psum_scatter(
            gradients[7].astype(jnp.bfloat16), "dp", scatter_dimension=0, tiled=True
        ).astype(jnp.float32),
    )
    gains = lax.psum((gradients[0], gradients[4]), ("dp", "row"))
    final_out, final_grad = (
        lax.all_to_all(
            jnp.concatenate(results, axis=0), "col", split_axis=0, concat_axis=1, tiled=True
        ),
        lax.all_to_all(
            jnp.concatenate(input_grads, axis=0), "col", split_axis=0, concat_axis=1, tiled=True
        ),
    )
    return (
        final_out,
        final_grad,
        gains[0],
        shards[0],
        shards[1],
        shards[2],
        gains[1],
        shards[3],
        shards[4],
        shards[5],
    )


def solution(mesh):
    placed = (
        P(("dp", "row", "col"), None),
        P(("dp", "row", "col"), None),
        P("dp", None),
        P("dp", None),
        P("col"),
        P("col", "row", "dp"),
        P("col", "row", "dp"),
        P("row", "dp", "col"),
        P("col"),
        P("col", ("dp", "row")),
        P("col", ("dp", "row")),
        P(("dp", "row"), "col"),
    )
    lay = Layout(mesh.shape)
    work = functools.partial(body, lay) if lay.fits() else general_body
    return jax.shard_map(
        work,
        mesh=mesh,
        in_specs=placed,
        out_specs=(
            P(("dp", "row", "col"), None),
            P(("dp", "row", "col"), None),
            P("col"),
            P("col", "row", "dp"),
            P("col", "row", "dp"),
            P("row", "dp", "col"),
            P("col"),
            P("col", ("dp", "row")),
            P("col", ("dp", "row")),
            P(("dp", "row"), "col"),
        ),
        check_vma=False,
    )
```
